32 devices in a mesh: gx: 4 (over z), gy: 4 (over y, core), gz: 2 (over x).
Axes of the slice: x: 2, y: 2, z: 4, core: 2. Of those that a mesh axis runs over, the one named last changes fastest.
Arguments:
- operator: bfloat16 [4, 4, 3072, 3072], P('gx', 'gy', 'gz'), may hold values from -1 to 4
- rhs_parts: float32 [4, 4, 8, 3072], P('gx', 'gy'), may hold values from -6 to 6
- stiffness: float32 [4, 4, 3072], P('gx', 'gy'), may hold values from 1 to 10
- traces: float32 [4, 4, 6, 3072], P('gx', 'gy'), may hold values from -6 to 6
- coarse_inverse: float32 [4, 4, 6, 96], P('gx', 'gy'), may hold values from -1 to 1, as said below
- rigid_loads: float32 [4, 4, 6, 8], P('gx', 'gy'), may hold values from -8192 to 8192
- face_lengths: int32 [4, 4, 4], P('gx', 'gy'), may hold values from 0 to 768, as said below
- face_order: int32 [4, 4, 4, 768], P('gx', 'gy'), may hold values from 0 to 767, as said below
- mode_count: int32 [4, 4], P('gx', 'gy'), may hold values from 0 to 6, as said below
Outputs:
- multipliers: float32 [4, 4, 8, 3072], P('gx', 'gy')
The draws below stay inside these ranges and needn't reach their ends.
Inputs may be any that keep to these rules, and one draw needn't show every extreme that they name: `coarse_inverse`: symmetric over the coefficient ordering. `face_lengths`: a face on the grid's edge has length 0; the two sides of an interface have the same length. `face_order`: on each face the live slots map one to one onto the neighbour's live slots of the opposite face, and that face maps them back; other slots map to themselves. `mode_count`: subdomains off the grid's edge have 6.
All inputs are finite; a program needn't handle non-finite values.
Results may differ from the reference program's by a relative error of at most 0.0036.
Values may be sent and summed in bfloat16 or wider, within the bound.
No kernel may reach another device: no remote copies, remote signals or barrier semaphores. Data moves between devices by JAX's collectives and lax.ppermute only.
A program may use at most 64 MiB of HBM per device.

```python
import math
import jax
import jax.numpy as jnp
from jax import lax

ORDER = 3072
LOADS = 8
MODES = 6
ITERS = 2
CAP = 768
SX = 4
SY = 4
COARSE = 96


def side_order(key, lengths):
    position = lax.broadcasted_iota(jnp.int32, (SX, SY, CAP), 2)
    scores = jax.random.randint(key, (SX, SY, CAP), 0, 2 ** 19) * CAP + position
    scores = jnp.where(position < lengths[:, :, None], scores, 2 ** 30 + position)
    return jnp.argsort(scores, axis=-1).astype(jnp.int32)


def interfaces(key):
    first_index = lax.broadcasted_iota(jnp.int32, (SX, SY), 0)
    second_index = lax.broadcasted_iota(jnp.int32, (SX, SY), 1)
    east_len = CAP - jax.random.randint(jax.random.fold_in(key, 11), (SX, SY), 0, CAP // 2 + 1)
    east_len = jnp.where((first_index == 0) & (second_index == 0), CAP, east_len)
    east_len = jnp.where(first_index == SX - 1, 0, east_len)
    north_len = CAP - jax.random.randint(jax.random.fold_in(key, 12), (SX, SY), 0, CAP // 2 + 1)
    north_len = jnp.where(second_index == SY - 1, 0, north_len)
    east_order = side_order(jax.random.fold_in(key, 13), east_len)
    north_order = side_order(jax.random.fold_in(key, 14), north_len)
    east_back = jnp.argsort(east_order, axis=-1).astype(jnp.int32)
    north_back = jnp.argsort(north_order, axis=-1).astype(jnp.int32)
    identity = lax.broadcasted_iota(jnp.int32, (SX, SY, CAP), 2)
    west_order = jnp.concatenate([identity[:1], east_back[:-1]], axis=0)
    south_order = jnp.concatenate([identity[:, :1], north_back[:, :-1]], axis=1)
    west_len = jnp.concatenate([jnp.zeros((1, SY), jnp.int32), east_len[:-1]], axis=0)
    south_len = jnp.concatenate([jnp.zeros((SX, 1), jnp.int32), north_len[:, :-1]], axis=1)
    lengths = jnp.stack([west_len, east_len, south_len, north_len], axis=-1).astype(jnp.int32)
    orders = jnp.stack([west_order, east_order, south_order, north_order], axis=2).astype(jnp.int32)
    return (lengths, orders)


def draw_face_lengths(key, part):
    return interfaces(key)[0]


def draw_face_order(key, part):
    return interfaces(key)[1]


def draw_mode_count(key, part):
    key = jax.random.fold_in(key, 21)
    first_index = lax.broadcasted_iota(jnp.int32, (SX, SY), 0)
    second_index = lax.broadcasted_iota(jnp.int32, (SX, SY), 1)
    inner = (first_index > 0) & (first_index < SX - 1) & (second_index > 0) & (second_index < SY - 1)
    edge_count = jax.random.randint(key, (SX, SY), 0, MODES + 1)
    return jnp.where(inner, MODES, edge_count).astype(jnp.int32)


def draw_operator(key, part):
    key = jax.random.fold_in(key, 31)
    noise_key = jax.random.fold_in(key, 1)
    diag_key = jax.random.fold_in(key, 2)
    shape = (SX, SY, ORDER, ORDER)
    noise = jnp.clip(jax.random.normal(noise_key, shape, jnp.float32), -4.0, 4.0)
    diagonal = jax.random.uniform(diag_key, (SX, SY, ORDER, 1), jnp.float32, 1.0, 2.0)
    row_index = lax.broadcasted_iota(jnp.int32, shape, 2)
    column_index = lax.broadcasted_iota(jnp.int32, shape, 3)
    values = 0.25 / ORDER ** 0.5 * noise + 0.5 / ORDER + jnp.where(row_index == column_index, diagonal, 0.0)
    return values.astype(jnp.bfloat16)


def draw_traces(key, part):
    key = jax.random.fold_in(key, 41)
    noise_key = jax.random.fold_in(key, 1)
    offset_key = jax.random.fold_in(key, 2)
    shape = (SX, SY, MODES, ORDER)
    noise = jnp.clip(jax.random.normal(noise_key, shape, jnp.float32), -4.0, 4.0)
    offset = jax.random.uniform(offset_key, (SX, SY, MODES, 1), jnp.float32, -1.0, 1.0)
    return noise + offset


def draw_rhs_parts(key, part):
    key = jax.random.fold_in(key, 51)
    noise_key = jax.random.fold_in(key, 1)
    offset_key = jax.random.fold_in(key, 2)
    shape = (SX, SY, LOADS, ORDER)
    noise = jnp.clip(jax.random.normal(noise_key, shape, jnp.float32), -4.0, 4.0)
    offset = jax.random.uniform(offset_key, (SX, SY, LOADS, 1), jnp.float32, -1.5, 1.5)
    return noise + offset


def draw_coarse_inverse(key, part):
    key = jax.random.fold_in(key, 61)
    noise_key = jax.random.fold_in(key, 1)
    gain_key = jax.random.fold_in(key, 2)
    shape = (COARSE, COARSE)
    noise = jnp.clip(jax.random.normal(noise_key, shape, jnp.float32), -4.0, 4.0)
    gain = jax.random.uniform(gain_key, (COARSE, 1), jnp.float32, 0.5, 1.0)
    symmetric = (noise + noise.T) * (0.15 / (2.0 * COARSE) ** 0.5)
    row_index = lax.broadcasted_iota(jnp.int32, shape, 0)
    column_index = lax.broadcasted_iota(jnp.int32, shape, 1)
    values = (symmetric + jnp.where(row_index == column_index, gain, 0.0)) / ORDER
    return values.reshape(SX, SY, MODES, COARSE)


def block_scale(rng, extent, pieces, least, top_value):
    def one(axis_at, blocks):
        draws = jax.random.uniform(jax.random.fold_in(jax.random.fold_in(rng, 6), axis_at), (blocks,), jnp.float32, least / len(pieces), top_value / len(pieces))
        return jnp.repeat(jnp.exp(draws), extent[axis_at] // blocks).reshape((-1,) + (1,) * (len(extent) - axis_at - 1))

    level = one(*pieces[0])
    for cut in pieces[1:]:
        level = level * one(*cut)
    return level


def gaussian(key, dims, spread, most, pieces=(), kind=jnp.bfloat16):
    entries = jax.random.normal(key, dims, jnp.float32) * spread
    if len(pieces) > 0:
        entries = block_scale(key, dims, pieces, -0.22, 0.18) * entries
    return jnp.clip(entries, min=-most, max=most).astype(kind)


def setup_inputs(seed: int = 0) -> dict:
    key_of = jax.random.split(jax.random.key(seed), 10)
    return {
        "operator": draw_operator(jax.random.fold_in(key_of[9], 71), 0),
        "rhs_parts": draw_rhs_parts(jax.random.fold_in(key_of[9], 71), 0),
        "stiffness": jnp.clip(jnp.exp(math.log(10.0) - 2.3025851 * jax.random.uniform(key_of[2], (SX, SY, ORDER), jnp.float32) ** block_scale(key_of[2], (SX, SY, ORDER), ((0, 4), (1, 4)), -0.2, 0.2)), 1.0, 10.0),
        "traces": draw_traces(jax.random.fold_in(key_of[9], 71), 0),
        "coarse_inverse": draw_coarse_inverse(jax.random.fold_in(key_of[9], 71), 0),
        "rigid_loads": gaussian(key_of[5], (SX, SY, MODES, LOADS), (ORDER / 2), 8192.0, ((0, 4), (1, 4)), jnp.float32),
        "face_lengths": draw_face_lengths(jax.random.fold_in(key_of[9], 71), 0),
        "face_order": draw_face_order(jax.random.fold_in(key_of[9], 71), 0),
        "mode_count": draw_mode_count(jax.random.fold_in(key_of[9], 71), 0),
    }


highest = lax.Precision.HIGHEST


def reference(operator, rhs_parts, stiffness, traces, coarse_inverse, rigid_loads, face_lengths, face_order, mode_count):
    position = jnp.arange(ORDER) % CAP
    face_index = jnp.arange(ORDER) // CAP
    live_mask = (position[None, None, :] < face_lengths[:, :, face_index]).astype(jnp.float32)
    mode_mask = (jnp.arange(MODES)[None, None, :] < mode_count[:, :, None]).astype(jnp.float32)
    active_modes = traces * mode_mask[:, :, :, None]

    def partner(vectors):
        row_count = vectors.shape[2]
        blocks = vectors.reshape(SX, SY, row_count, 4, CAP)
        edge_x = jnp.zeros((1, SY, row_count, CAP), jnp.float32)
        edge_y = jnp.zeros((SX, 1, row_count, CAP), jnp.float32)
        from_west = jnp.concatenate([edge_x, blocks[:-1, :, :, 1]], axis=0)
        from_east = jnp.concatenate([blocks[1:, :, :, 0], edge_x], axis=0)
        from_south = jnp.concatenate([edge_y, blocks[:, :-1, :, 3]], axis=1)
        from_north = jnp.concatenate([blocks[:, 1:, :, 2], edge_y], axis=1)
        facing = jnp.stack([from_west, from_east, from_south, from_north], axis=3)
        partner_slots = jnp.broadcast_to(face_order[:, :, None], facing.shape)
        return jnp.take_along_axis(facing, partner_slots, axis=4).reshape(SX, SY, row_count, ORDER)

    def assemble(vectors):
        return live_mask[:, :, None] * (vectors + partner(vectors))

    def coarse_solve(coarse_rhs):
        stacked = coarse_rhs.reshape(COARSE, LOADS)
        solved = jnp.dot(coarse_inverse.reshape(COARSE, COARSE), stacked, precision=highest)
        return solved.reshape(SX, SY, MODES, LOADS)

    def correction(coeffs):
        return assemble(jnp.einsum("xyml,xymi->xyli", coeffs, active_modes, precision=highest))

    def project(vectors):
        coarse_rhs = jnp.einsum("xymi,xyli->xyml", active_modes, vectors, precision=highest)
        return vectors - correction(coarse_solve(coarse_rhs))

    def apply_operator(vectors):
        matrices = operator.reshape(SX * SY, ORDER, ORDER)
        inputs = vectors.astype(jnp.bfloat16).reshape(SX * SY, LOADS, ORDER)

        def single(operands):
            return jnp.dot(operands[1], operands[0].T, preferred_element_type=jnp.float32).astype(jnp.bfloat16)

        return lax.map(single, (matrices, inputs)).reshape(SX, SY, LOADS, ORDER)

    estimate = correction(coarse_solve(rigid_loads * mode_mask[:, :, :, None]))
    stiff_sum = assemble(stiffness[:, :, None, :])[:, :, 0]
    weight = live_mask / (stiff_sum + 1.0 - live_mask)
    residual = project(assemble(rhs_parts - apply_operator(estimate).astype(jnp.float32)))
    direction = residual
    previous = jnp.ones((LOADS,), jnp.float32)
    for iteration in range(ITERS):
        scaled = weight[:, :, None] * residual
        resid_dot = jnp.sum(residual * scaled, axis=(0, 1, 3))
        projected = project(scaled)
        if iteration == 0:
            direction = projected
        else:
            direction = projected + (resid_dot / previous)[None, None, :, None] * direction
        image = assemble(apply_operator(direction).astype(jnp.float32))
        curvature = jnp.sum(direction * image, axis=(0, 1, 3))
        step_size = resid_dot / curvature
        estimate = estimate + step_size[None, None, :, None] * direction
        if iteration + 1 < ITERS:
            residual = residual - step_size[None, None, :, None] * project(image)
        previous = resid_dot
    return estimate
```

```python
import functools

import jax
import jax.numpy as jnp
from jax import lax
from jax.experimental import pallas as pl
from jax.experimental.pallas import tpu as pltpu
from jax.sharding import PartitionSpec as P

ROW_CHUNK = 256
IN_FLIGHT = 2
TILE = 128
SLOT = 8
MODE_SPAN = 5 * SLOT
SCALARS = 3 * MODE_SPAN
MIB = 1024 * 1024


class Sizes:
    def __init__(self, mesh_shape, operator, traces, loads):
        self.sx, self.sy, self.gz = mesh_shape
        self.rows = operator.shape[2]
        self.order = operator.shape[3]
        self.modes = traces.shape[2]
        self.cap = self.order // 4
        self.loads = loads
        self.subs = self.sx * self.sy
        self.devices = self.subs * self.gz
        self.coarse = self.subs * SLOT
        self.coarse_pad = -(-self.coarse // TILE) * TILE
        self.own_faces = self.rows // self.cap
        assert self.rows % self.cap == 0 and self.cap % TILE == 0
        assert self.modes <= SLOT - 2 and self.loads == 8


def f32(*shape):
    return jax.ShapeDtypeStruct(shape, jnp.float32)


def lanes(shape=(8, TILE)):
    return lax.broadcasted_iota(jnp.int32, shape, 1)


def exact_dot(a, b):
    return jnp.dot(a, b, precision=lax.Precision.HIGHEST, preferred_element_type=jnp.float32)


def clamp(index, count):
    return jnp.minimum(jnp.maximum(index, 0), count - 1)


def neighbour(sz, face):
    gx, gy = lax.axis_index("gx"), lax.axis_index("gy")
    x = gx + jnp.where(face == 0, -1, jnp.where(face == 1, 1, 0))
    y = gy + jnp.where(face == 2, -1, jnp.where(face == 3, 1, 0))
    return clamp(x, sz.sx) * sz.sy + clamp(y, sz.sy)


def grid_neighbour(sz, sub, face):
    x, y = divmod(sub, sz.sy)
    x, y = [(x - 1, y), (x + 1, y), (x, y - 1), (x, y + 1)][face]
    return x * sz.sy + y if 0 <= x < sz.sx and 0 <= y < sz.sy else None


def face_pairs(sz, local):
    pairs = []
    for sub in range(sz.subs):
        for part in range(sz.gz):
            face = part * sz.own_faces + local
            other = grid_neighbour(sz, sub, face)
            if other is not None:
                pairs.append((sub * sz.gz + part, other * sz.gz + (face ^ 1) // sz.own_faces))
    return pairs


def own_face(sz, j):
    return slice(j * sz.cap, (j + 1) * sz.cap)


def facing(sz, j):
    return j ^ 1 if sz.own_faces > 1 else j


def permuted(sz, block, slots):
    count = sz.cap // TILE
    pieces = [block[:, k * TILE : (k + 1) * TILE] for k in range(count)]
    result = []
    for j in range(count):
        index = slots[:, j * TILE : (j + 1) * TILE].astype(jnp.int32)
        low = index & (TILE - 1)
        high = index >> (TILE.bit_length() - 1)
        total = jnp.zeros((8, TILE), jnp.float32)
        for k in range(count):
            picked = jnp.take_along_axis(pieces[k], low, axis=1, mode="promise_in_bounds")
            total = jnp.where(high == k, picked, total)
        result.append(total)
    return jnp.concatenate(result, axis=1)


def coefficients(sz, coarse_ref):
    gz = lax.axis_index("gz")
    subs = [lax.axis_index("gx") * sz.sy + lax.axis_index("gy")]
    subs += [neighbour(sz, gz * sz.own_faces + j) for j in range(sz.own_faces)]
    result = []
    for sub in subs:
        start = sub * SLOT
        base = pl.multiple_of((start // TILE) * TILE, TILE)
        tile = coarse_ref[:, pl.ds(base, TILE)]
        shift = lax.rem(TILE - lax.rem(start, TILE), TILE)
        result.append(pltpu.roll(tile, shift, 1))
    return result


def mode_sum(sz, coeffs, modes_ref, j):
    total = None
    for tile, base in ((coeffs[0], 0), (coeffs[1 + j], SLOT)):
        for m in range(sz.modes):
            term = tile[:, m : m + 1] * modes_ref[base + m : base + m + 1, own_face(sz, j)]
            total = term if total is None else total + term
    return total


def mode_products(sz, tile, blocks, modes_ref, first_lane):
    lane = lanes()
    gz = lax.axis_index("gz")
    for m in range(sz.modes):
        total = None
        for j, block in enumerate(blocks):
            term = jnp.sum(block * modes_ref[m : m + 1, own_face(sz, j)], axis=1, keepdims=True)
            total = term if total is None else total + term
        tile = jnp.where(lane == first_lane + m, total, tile)
    for j, block in enumerate(blocks):
        face_lane = first_lane + SLOT * (1 + gz * sz.own_faces + j)
        for m in range(sz.modes):
            row = modes_ref[SLOT + m : SLOT + m + 1, own_face(sz, j)]
            total = jnp.sum(block * row, axis=1, keepdims=True)
            tile = jnp.where(lane == face_lane + m, total, tile)
    return tile


def weights_of(sz, modes_ref):
    return [modes_ref[6:7, own_face(sz, j)] for j in range(sz.own_faces)]


def sub_tile(sz, tiles, sub):
    total = tiles[sub * sz.gz]
    for part in range(1, sz.gz):
        total = total + tiles[sub * sz.gz + part]
    return total


def gathered_coarse(sz, tiles, held_ref, group):
    lane = lanes()
    held_ref[...] = jnp.zeros((8, sz.coarse_pad), jnp.float32)
    for sub in range(sz.subs):
        total = tiles[sub]
        for face in range(4):
            other = grid_neighbour(sz, sub, face)
            if other is not None:
                total = total + pltpu.roll(tiles[other], TILE - SLOT * (1 + (face ^ 1)), 1)
        start = sub * SLOT
        base, offset = start // TILE * TILE, start % TILE
        moved = pltpu.roll(total, (offset - group * MODE_SPAN) % TILE, 1)
        moved = jnp.where((lane >= offset) & (lane < offset + sz.modes), moved, 0.0)
        held_ref[:, base : base + TILE] += moved


def fill_coupling(sz, tiles, coupling_ref):
    lane = lanes()
    coupling_ref[...] = jnp.zeros((sz.coarse_pad, sz.coarse_pad), jnp.float32)
    for sub in range(sz.subs):
        for k in range(5):
            other = sub if k == 0 else grid_neighbour(sz, sub, k - 1)
            if other is None:
                continue
            base, offset = other * SLOT // TILE * TILE, other * SLOT % TILE
            moved = pltpu.roll(tiles[sub], (offset - 2 * MODE_SPAN - SLOT * k) % TILE, 1)
            moved = jnp.where((lane >= offset) & (lane < offset + sz.modes), moved, 0.0)
            coupling_ref[sub * SLOT : (sub + 1) * SLOT, base : base + TILE] += moved


def fill_inverse(sz, shared, inverse_ref):
    if sz.coarse_pad > sz.coarse:
        inverse_ref[sz.coarse :, :] = jnp.zeros((sz.coarse_pad - sz.coarse, sz.coarse_pad), jnp.float32)
    for sub in range(sz.subs):
        inverse_ref[sub * SLOT : (sub + 1) * SLOT, :] = shared[sub, :, 0 : sz.coarse_pad]


def solve_pair(sz, tiles, inverse_ref, coupling_ref, coarse_a, coarse_b):
    gathered_coarse(sz, tiles, coarse_a, 0)
    gathered_coarse(sz, tiles, coarse_b, 1)
    first = exact_dot(coarse_a[...], inverse_ref[...])
    coarse_a[...] = first
    coarse_b[...] = exact_dot(coarse_b[...] - exact_dot(first, coupling_ref[...]), inverse_ref[...])
    return coefficients(sz, coarse_a), coefficients(sz, coarse_b)


def spread(out, tile):
    out[...] = jnp.broadcast_to(tile[None], out.shape)


def part_slots(sz, part):
    return pl.ds(pl.multiple_of(part * sz.rows, TILE), sz.rows)


def put_parts(sz, parts, vector):
    if len(parts) == 1:
        for z in range(sz.gz):
            vector[:, z * sz.rows : (z + 1) * sz.rows] = parts[0][z].astype(vector.dtype)
    else:
        gz = lax.axis_index("gz")
        vector[:, part_slots(sz, gz)] = parts[0][...].astype(vector.dtype)
        vector[:, part_slots(sz, 1 - gz)] = parts[1][...].astype(vector.dtype)


def start_kernel(sz, traces, loads, inverse, stiffness, orders, rhs, lengths, count, *refs):
    outs, scratch = refs[: sz.own_faces + 2], refs[sz.own_faces + 2 :]
    faces, (pay, base) = outs[: sz.own_faces], outs[sz.own_faces :]
    traces_in, loads_in, inverse_in, stiffness_in, slots, lengths_in, count_in, sems = scratch
    gz = lax.axis_index("gz")
    here = pl.ds(pl.multiple_of(gz * sz.rows, TILE), sz.rows)
    copies = [
        pltpu.make_async_copy(inverse, inverse_in, sems.at[0]),
        pltpu.make_async_copy(loads, loads_in, sems.at[1]),
        pltpu.make_async_copy(traces.at[:, :, here], traces_in, sems.at[2]),
        pltpu.make_async_copy(stiffness.at[0, :, here], stiffness_in, sems.at[3]),
        pltpu.make_async_copy(orders.at[0, 0], slots, sems.at[4]),
        pltpu.make_async_copy(rhs.at[0, 0, :, here], base.at[pl.ds(8, 8), :], sems.at[5]),
        pltpu.make_async_copy(lengths, lengths_in, sems.at[6]),
        pltpu.make_async_copy(count, count_in, sems.at[7]),
    ]
    for copy in copies:
        copy.start()
    pay[...] = jnp.zeros(pay.shape, jnp.float32)
    for face in faces:
        face[sz.modes :, :] = jnp.zeros((8 - sz.modes, sz.cap), jnp.float32)
    for copy in copies:
        copy.wait()
    for m in range(sz.modes):
        mask = (m < count_in[0, 0]).astype(jnp.float32)
        for t in range(sz.subs):
            pay[0, m : m + 1, t * SLOT : t * SLOT + sz.modes] = inverse_in[
                m, :, t * sz.modes : (t + 1) * sz.modes
            ]
        pay[0, m : m + 1, sz.coarse_pad : sz.coarse_pad + sz.loads] = loads_in[m] * mask
        for j, face in enumerate(faces):
            face[m : m + 1, :] = traces_in[m, :, own_face(sz, j)] * mask
    position = lax.broadcasted_iota(jnp.int32, (1, sz.cap), 1)
    for j, face in enumerate(faces):
        face[6:7, :] = stiffness_in[:, own_face(sz, j)]
        index = gz * sz.own_faces + j
        face[7:8, :] = (position < lengths_in[0, 0, index]).astype(jnp.float32)
        base[0:8, own_face(sz, j)] = face[...]
        chosen = jnp.broadcast_to(slots[pl.ds(index, 1), :], (8, sz.cap))
        base[16:24, own_face(sz, j)] = chosen.astype(jnp.float32)
    chunk = pay[0]
    for k in range(1, pay.shape[0]):
        pay[k] = chunk


def first_kernel(sz, shared, base, *refs):
    arrived, refs = refs[: sz.own_faces], refs[sz.own_faces :]
    estimate_ref, modes_ref, inverse_ref, loads_ref, coarse_ref = refs
    fill_inverse(sz, shared, inverse_ref)
    if sz.coarse_pad > sz.coarse:
        loads_ref[sz.coarse :, :] = jnp.zeros((sz.coarse_pad - sz.coarse, TILE), jnp.float32)
    for sub in range(sz.subs):
        loads_ref[sub * SLOT : (sub + 1) * SLOT, :] = shared[sub, :, sz.coarse_pad :]
    turned = jnp.concatenate(
        [
            jnp.transpose(loads_ref[k * TILE : (k + 1) * TILE, :])[0:8, :]
            for k in range(sz.coarse_pad // TILE)
        ],
        axis=1,
    )
    coarse_ref[...] = exact_dot(turned, inverse_ref[...])
    row = lax.broadcasted_iota(jnp.int32, (8, 1), 0)
    for j in range(sz.own_faces):
        here = own_face(sz, j)
        other = permuted(sz, arrived[facing(sz, j)][...], base[16:24, here])
        mine = base[0:8, here]
        live = mine[7:8, :]
        total = live * (mine[6:7, :] + other[6:7, :])
        weight = live / (total + 1.0 - live)
        modes_ref[0:8, here] = jnp.where(row == 6, weight, jnp.where(row == 7, live, mine * live))
        modes_ref[8:16, here] = jnp.where(row < sz.modes, other * live, 0.0)
    coeffs = coefficients(sz, coarse_ref)
    for j in range(sz.own_faces):
        estimate_ref[:, own_face(sz, j)] = mode_sum(sz, coeffs, modes_ref, j)


def apply_rows(sz, vector, held, outs, arrive=None):
    for k in range(sz.rows // ROW_CHUNK):
        if arrive is not None:
            arrive(k)
        part = lax.dot_general(
            vector[...], held[k], (((1,), (1,)), ((), ())), preferred_element_type=jnp.float32
        )
        j, start = divmod(k * ROW_CHUNK, sz.cap)
        outs[j][:, start : start + ROW_CHUNK] = part.astype(jnp.bfloat16).astype(jnp.float32)


def first_apply_kernel(sz, operator, modes_ref, base, *refs):
    parts, refs = refs[: -sz.own_faces - 4], refs[-sz.own_faces - 4 :]
    outs, (pay, held, vector, sems) = refs[: sz.own_faces], refs[sz.own_faces :]
    copies = [
        pltpu.make_async_copy(
            operator.at[0, 0, pl.ds(k * ROW_CHUNK, ROW_CHUNK), :], held.at[k], sems.at[k]
        )
        for k in range(sz.rows // ROW_CHUNK)
    ]
    for copy in copies[:IN_FLIGHT]:
        copy.start()

    def arrive(k):
        copies[k].wait()
        if k + IN_FLIGHT < len(copies):
            copies[k + IN_FLIGHT].start()

    put_parts(sz, parts, vector)
    weights = weights_of(sz, modes_ref)
    row = lax.broadcasted_iota(jnp.int32, (8, 1), 0)
    coarse_rows = [
        jnp.where(row < sz.modes, modes_ref[0:8, own_face(sz, j)] * weights[j], 0.0)
        for j in range(sz.own_faces)
    ]
    tile = jnp.zeros((8, TILE), jnp.float32)
    tile = mode_products(sz, tile, coarse_rows, modes_ref, 2 * MODE_SPAN)
    apply_rows(sz, vector, held, outs, arrive)
    vectors = []
    for j, out in enumerate(outs):
        vectors.append(base[8:16, own_face(sz, j)] - out[...])
        out[...] = vectors[-1]
    tile = mode_products(sz, tile, vectors, modes_ref, 0)
    scaled = [v * w for v, w in zip(vectors, weights)]
    spread(pay, mode_products(sz, tile, scaled, modes_ref, MODE_SPAN))


def assembled(sz, own, arrived, base, modes_ref, j):
    other = permuted(sz, arrived[facing(sz, j)][...], base[16:24, own_face(sz, j)])
    return modes_ref[7:8, own_face(sz, j)] * (own[j][...] + other)


def second_kernel(sz, pieces, shared, base, modes_ref, *refs):
    own, refs = refs[: sz.own_faces], refs[sz.own_faces :]
    arrived, refs = refs[: sz.own_faces], refs[sz.own_faces :]
    residual_ref, direction_ref, inverse_ref, coupling_ref, coarse_a, coarse_b = refs
    fill_inverse(sz, shared, inverse_ref)
    tiles = [sub_tile(sz, pieces, sub) for sub in range(sz.subs)]
    fill_coupling(sz, tiles, coupling_ref)
    first, second = solve_pair(sz, tiles, inverse_ref, coupling_ref, coarse_a, coarse_b)
    for j in range(sz.own_faces):
        here = own_face(sz, j)
        gap = assembled(sz, own, arrived, base, modes_ref, j)
        residual = gap - mode_sum(sz, first, modes_ref, j)
        residual_ref[:, here] = residual
        direction_ref[:, here] = modes_ref[6:7, here] * residual - mode_sum(sz, second, modes_ref, j)


def second_apply_kernel(sz, held, modes_ref, direction, residual, *refs):
    parts, refs = refs[: -sz.own_faces - 2], refs[-sz.own_faces - 2 :]
    outs, (pay, vector) = refs[: sz.own_faces], refs[sz.own_faces :]
    put_parts(sz, parts, vector)
    weights = weights_of(sz, modes_ref)
    lane = lanes()
    curvature = jnp.zeros((8, 1), jnp.float32)
    resid_dot = jnp.zeros((8, 1), jnp.float32)
    for j in range(sz.own_faces):
        own = residual[:, own_face(sz, j)]
        resid_dot += jnp.sum(own * (weights[j] * own), axis=1, keepdims=True)
    apply_rows(sz, vector, held, outs)
    pieces = [out[...] for out in outs]
    for j, piece in enumerate(pieces):
        curvature += jnp.sum(direction[:, own_face(sz, j)] * piece, axis=1, keepdims=True)
    tile = jnp.where(lane == SCALARS, curvature, jnp.zeros((8, TILE), jnp.float32))
    tile = jnp.where(lane == SCALARS + 1, resid_dot, tile)
    tile = mode_products(sz, tile, pieces, modes_ref, 0)
    scaled = [v * w for v, w in zip(pieces, weights)]
    spread(pay, mode_products(sz, tile, scaled, modes_ref, MODE_SPAN))


def third_kernel(sz, pieces, shared, before, base, modes_ref, residual_ref, direction_ref, *refs):
    own, refs = refs[: sz.own_faces], refs[sz.own_faces :]
    arrived, refs = refs[: sz.own_faces], refs[sz.own_faces :]
    later_ref, scalars_ref, inverse_ref, coupling_ref, coarse_a, coarse_b = refs
    lane = lanes()
    fill_inverse(sz, shared, inverse_ref)
    fill_coupling(sz, [sub_tile(sz, before, sub) for sub in range(sz.subs)], coupling_ref)
    tiles = [sub_tile(sz, pieces, sub) for sub in range(sz.subs)]
    totals = tiles[0]
    for tile in tiles[1:]:
        totals = totals + tile
    curvature = 2.0 * totals[:, SCALARS : SCALARS + 1]
    resid_dot = totals[:, SCALARS + 1 : SCALARS + 2]
    step = resid_dot / curvature
    first, second = solve_pair(sz, tiles, inverse_ref, coupling_ref, coarse_a, coarse_b)
    dot_part = jnp.zeros((8, 1), jnp.float32)
    for j in range(sz.own_faces):
        here = own_face(sz, j)
        image = assembled(sz, own, arrived, base, modes_ref, j)
        corrected = image - mode_sum(sz, first, modes_ref, j)
        weight = modes_ref[6:7, here]
        scaled = weight * corrected - mode_sum(sz, second, modes_ref, j)
        residual = residual_ref[:, here] - step * corrected
        dot_part += jnp.sum(residual * (weight * residual), axis=1, keepdims=True)
        later_ref[:, here] = direction_ref[:, here] - step * scaled
    scalars_ref[...] = jnp.where(lane == 0, curvature, jnp.where(lane == 1, resid_dot, dot_part))


def third_apply_kernel(sz, held, later, direction, scalars, *refs):
    before, refs = refs[: sz.own_faces], refs[sz.own_faces :]
    parts, refs = refs[: -sz.own_faces - 2], refs[-sz.own_faces - 2 :]
    pay, vector, outs = *refs[:2], refs[2:]
    put_parts(sz, parts, vector)
    apply_rows(sz, vector, held, outs)
    lane = lanes()
    later_part = jnp.zeros((8, 1), jnp.float32)
    cross_part = jnp.zeros((8, 1), jnp.float32)
    for j, out in enumerate(outs):
        piece = out[...]
        mine = later[:, own_face(sz, j)]
        earlier = direction[:, own_face(sz, j)]
        later_part += jnp.sum(mine * piece, axis=1, keepdims=True)
        cross_part += jnp.sum(mine * before[j][...] + earlier * piece, axis=1, keepdims=True)
    load = lax.broadcasted_iota(jnp.int32, (8, TILE), 0)
    line = jnp.where(lane == load, later_part, 0.0)
    line = jnp.where(lane == load + 8, cross_part, line)
    line = jnp.where(lane == load + 16, scalars[:, 2:3], line)
    spread(pay, jnp.sum(line, axis=0, keepdims=True))


def last_kernel(sz, pieces, scalars, *refs):
    out = refs[-1]
    count = (len(refs) - 1) // 3
    estimate, direction, later = refs[:count], refs[count : 2 * count], refs[2 * count : 3 * count]
    totals = pieces[0]
    for k in range(1, pieces.shape[0]):
        totals = totals + pieces[k]
    curvature, previous = scalars[:, 0:1], scalars[:, 1:2]
    load = lax.broadcasted_iota(jnp.int32, (8, TILE), 0)
    later_part, cross_part, dot = [
        jnp.sum(jnp.where(lanes() == load + 8 * k, totals, 0.0), axis=1, keepdims=True)
        for k in range(3)
    ]
    ratio = dot / previous
    final = 2.0 * (later_part + ratio * cross_part) + ratio * ratio * curvature
    first, second = previous / curvature, dot / final
    gz = lax.axis_index("gz")
    for z in range(sz.gz):
        if count == 1:
            here, parts = part_slots(sz, z), [x[0][z] for x in (estimate, direction, later)]
        else:
            here = part_slots(sz, 1 - gz if z else gz)
            parts = [x[z][...] for x in (estimate, direction, later)]
        moved = parts[0] + first * parts[1]
        out[0, 0, :, here] = moved + second * (parts[2] + ratio * parts[1])


def shards(mesh_shape, operator, rhs_parts, stiffness, traces, coarse_inverse, rigid_loads,
           face_lengths, face_order, mode_count):
    sz = Sizes(mesh_shape, operator, traces, rhs_parts.shape[2])
    vmem = pl.BlockSpec(memory_space=pltpu.VMEM)
    smem = pl.BlockSpec(memory_space=pltpu.SMEM)
    hbm = pl.BlockSpec(memory_space=pltpu.HBM)
    everywhere = ("gx", "gy", "gz")
    small = sz.coarse_pad <= 256

    def call(kernel, out_shape, in_specs, scratch, *operands, limit=None):
        return pl.pallas_call(
            functools.partial(kernel, sz),
            out_shape=out_shape,
            in_specs=in_specs,
            out_specs=jax.tree.map(lambda _: vmem, out_shape),
            scratch_shapes=scratch,
            compiler_params=pltpu.CompilerParams(
                vmem_limit_bytes=(limit or (16 if small else 56)) * MIB
            ),
        )(*operands)

    faces = sz.own_faces
    chunks = sz.rows // ROW_CHUNK
    coarse = pltpu.VMEM((8, sz.coarse_pad), jnp.float32)
    square = pltpu.VMEM((sz.coarse_pad, sz.coarse_pad), jnp.float32)
    half = f32(8, sz.rows)
    face = f32(8, sz.cap)
    one_step = sz.devices <= 64
    spread_tile = f32(sz.devices if one_step else 1, 8, TILE)
    vector = pltpu.VMEM((8, sz.order), jnp.bfloat16)

    def swap(own):
        return [lax.ppermute(own[j], everywhere, face_pairs(sz, j)) for j in range(faces)]

    def share(chunk, axes):
        if chunk.shape[0] == 1:
            return lax.all_gather(chunk, axes, axis=0, tiled=True)
        return lax.all_to_all(chunk, axes, split_axis=0, concat_axis=0, tiled=True)

    def whole(part):
        if sz.gz == 2:
            return [part, lax.ppermute(part, "gz", [(0, 1), (1, 0)])]
        return [lax.all_gather(part, "gz", axis=0, tiled=False)]

    *own, pay, base = call(
        start_kernel,
        [face] * faces + [
            f32(sz.subs if one_step else 1, 8, sz.coarse_pad + TILE),
            f32(24, sz.rows),
        ],
        [hbm] * 8,
        [
            pltpu.VMEM((sz.modes, 1, sz.rows), jnp.float32),
            pltpu.VMEM((sz.modes, 1, sz.loads), jnp.float32),
            pltpu.VMEM((sz.modes, 1, sz.subs * sz.modes), jnp.float32),
            pltpu.VMEM((1, sz.rows), jnp.float32),
            pltpu.VMEM((4, sz.cap), jnp.int32),
            pltpu.SMEM((1, 1, 4), jnp.int32),
            pltpu.SMEM((1, 1), jnp.int32),
            pltpu.SemaphoreType.DMA((8,)),
        ],
        traces.reshape(sz.modes, 1, sz.order), rigid_loads.reshape(sz.modes, 1, sz.loads),
        coarse_inverse.reshape(sz.modes, 1, -1), stiffness, face_order, rhs_parts,
        face_lengths, mode_count, limit=60,
    )
    arrived = swap(own)
    shared = share(pay, ("gx", "gy"))
    estimate, modes = call(
        first_kernel, [half, f32(16, sz.rows)], [vmem] * (2 + faces),
        [square, pltpu.VMEM((sz.coarse_pad, TILE), jnp.float32), coarse],
        shared, base, *arrived,
    )
    estimates = whole(estimate)
    *own, pay, held = call(
        first_apply_kernel,
        [face] * faces + [
            spread_tile,
            jax.ShapeDtypeStruct((chunks, ROW_CHUNK, sz.order), jnp.bfloat16),
        ],
        [hbm] + [vmem] * (2 + len(estimates)),
        [vector, pltpu.SemaphoreType.DMA((chunks,))],
        operator, modes, base, *estimates, limit=42,
    )
    arrived = swap(own)
    before = share(pay, everywhere)
    residual, direction = call(
        second_kernel, [half, half], [vmem] * (4 + 2 * faces), [square, square, coarse, coarse],
        before, shared, base, modes, *own, *arrived,
    )
    directions = whole(direction)
    *own, pay = call(
        second_apply_kernel, [face] * faces + [spread_tile], [vmem] * (4 + len(directions)),
        [vector], held, modes, direction, residual, *directions,
    )
    arrived = swap(own)
    pieces = share(pay, everywhere)
    later, scalars = call(
        third_kernel, [half, f32(8, TILE)], [vmem] * (7 + 2 * faces),
        [square, square, coarse, coarse],
        pieces, shared, before, base, modes, residual, direction, *own, *arrived,
    )
    laters = whole(later)
    pay = call(
        third_apply_kernel, f32(sz.devices if one_step else 1, 1, TILE),
        [vmem] * (4 + faces + len(laters)),
        [vector] + [pltpu.VMEM((8, sz.cap), jnp.float32)] * faces,
        held, later, direction, scalars, *own, *laters,
    )
    return call(
        last_kernel, f32(1, 1, 8, sz.order), [vmem] * (2 + 3 * len(laters)), [],
        share(pay, everywhere), scalars, *estimates, *directions, *laters,
    )


def solution(mesh):
    in_specs = (
        P("gx", "gy", "gz", None),
        P("gx", "gy", None, None),
        P("gx", "gy", None),
        P("gx", "gy", None, None),
        P("gx", "gy", None, None),
        P("gx", "gy", None, None),
        P("gx", "gy", None),
        P("gx", "gy", None, None),
        P("gx", "gy"),
    )
    out_specs = P("gx", "gy", None, None)
    mesh_shape = tuple(mesh.shape[axis] for axis in ("gx", "gy", "gz"))
    return jax.shard_map(
        functools.partial(shards, mesh_shape),
        mesh=mesh, in_specs=in_specs, out_specs=out_specs, check_vma=False,
    )
```

```python
import functools

import jax
import jax.numpy as jnp
from jax import lax
from jax.experimental import pallas as pl
from jax.experimental.pallas import tpu as pltpu
from jax.sharding import PartitionSpec as P

ROW_CHUNK = 256
TILE = 128
SLOT = 8
MODE_SPAN = 5 * SLOT
SCALARS = 3 * MODE_SPAN
MIB = 1024 * 1024


class Sizes:
    def __init__(self, mesh_shape, operator, traces, loads):
        self.sx, self.sy, self.gz = mesh_shape
        self.rows = operator.shape[2]
        self.order = operator.shape[3]
        self.modes = traces.shape[2]
        self.cap = self.order // 4
        self.loads = loads
        self.subs = self.sx * self.sy
        self.devices = self.subs * self.gz
        self.coarse = self.subs * SLOT
        self.coarse_pad = -(-self.coarse // TILE) * TILE
        self.own_faces = self.rows // self.cap
        assert self.rows % self.cap == 0 and self.cap % TILE == 0
        assert self.modes <= SLOT - 2 and self.loads == 8


def f32(*shape):
    return jax.ShapeDtypeStruct(shape, jnp.float32)


def lanes(shape=(8, TILE)):
    return lax.broadcasted_iota(jnp.int32, shape, 1)


def exact_dot(a, b):
    return jnp.dot(a, b, precision=lax.Precision.HIGHEST, preferred_element_type=jnp.float32)


def clamp(index, count):
    return jnp.minimum(jnp.maximum(index, 0), count - 1)


def neighbour(sz, face):
    gx, gy = lax.axis_index("gx"), lax.axis_index("gy")
    x = gx + jnp.where(face == 0, -1, jnp.where(face == 1, 1, 0))
    y = gy + jnp.where(face == 2, -1, jnp.where(face == 3, 1, 0))
    return clamp(x, sz.sx) * sz.sy + clamp(y, sz.sy)


def grid_neighbour(sz, sub, face):
    x, y = divmod(sub, sz.sy)
    x, y = [(x - 1, y), (x + 1, y), (x, y - 1), (x, y + 1)][face]
    return x * sz.sy + y if 0 <= x < sz.sx and 0 <= y < sz.sy else None


def face_pairs(sz, slot):
    pairs = []
    for sub in range(sz.subs):
        for part in range(sz.gz):
            local = slot
            if sz.own_faces > 1:
                first = part * sz.own_faces + slot // 2 * 2
                index = divmod(sub, sz.sy)[first // 2]
                local = slot ^ 1 ^ index & 1
            face = part * sz.own_faces + local
            other = grid_neighbour(sz, sub, face)
            if other is not None:
                pairs.append((sub * sz.gz + part, other * sz.gz + (face ^ 1) // sz.own_faces))
    return pairs


def by_slot(sz, values):
    if sz.own_faces == 1:
        return values
    result = []
    for j in range(0, sz.own_faces, 2):
        first = lax.axis_index("gz") * sz.own_faces + j
        index = jnp.where(first < 2, lax.axis_index("gx"), lax.axis_index("gy"))
        odd = lax.rem(index, 2) == 1
        low, high = values[j], values[j + 1]
        result += [jnp.where(odd, low, high), jnp.where(odd, high, low)]
    return result


def own_face(sz, j):
    return slice(j * sz.cap, (j + 1) * sz.cap)


def put_slots(sz, outs, values):
    for out, value in zip(outs, by_slot(sz, values)):
        out[...] = value


def get_slots(sz, refs):
    return by_slot(sz, [ref[...] for ref in refs])


def permuted(sz, block, slots):
    count = sz.cap // TILE
    pieces = [block[:, k * TILE : (k + 1) * TILE] for k in range(count)]
    result = []
    for j in range(count):
        index = jnp.broadcast_to(slots[:, j * TILE : (j + 1) * TILE], (8, TILE)).astype(jnp.int32)
        low = index & (TILE - 1)
        high = index >> (TILE.bit_length() - 1)
        total = jnp.zeros((8, TILE), jnp.float32)
        for k in range(count):
            picked = jnp.take_along_axis(pieces[k], low, axis=1, mode="promise_in_bounds")
            total = jnp.where(high == k, picked, total)
        result.append(total)
    return jnp.concatenate(result, axis=1)


def coefficients(sz, coarse_ref):
    gz = lax.axis_index("gz")
    subs = [lax.axis_index("gx") * sz.sy + lax.axis_index("gy")]
    subs += [neighbour(sz, gz * sz.own_faces + j) for j in range(sz.own_faces)]
    result = []
    for sub in subs:
        start = sub * SLOT
        base = pl.multiple_of((start // TILE) * TILE, TILE)
        tile = coarse_ref[:, pl.ds(base, TILE)]
        shift = lax.rem(TILE - lax.rem(start, TILE), TILE)
        result.append(pltpu.roll(tile, shift, 1))
    return result


def mode_sum(sz, coeffs, modes_ref, j):
    total = None
    for tile, base in ((coeffs[0], 0), (coeffs[1 + j], SLOT)):
        for m in range(sz.modes):
            term = tile[:, m : m + 1] * modes_ref[base + m : base + m + 1, own_face(sz, j)]
            total = term if total is None else total + term
    return total


def mode_products(sz, tile, blocks, modes_ref, first_lane):
    lane = lanes()
    gz = lax.axis_index("gz")
    for m in range(sz.modes):
        total = None
        for j, block in enumerate(blocks):
            term = jnp.sum(block * modes_ref[m : m + 1, own_face(sz, j)], axis=1, keepdims=True)
            total = term if total is None else total + term
        tile = jnp.where(lane == first_lane + m, total, tile)
    for j, block in enumerate(blocks):
        face_lane = first_lane + SLOT * (1 + gz * sz.own_faces + j)
        for m in range(sz.modes):
            row = modes_ref[SLOT + m : SLOT + m + 1, own_face(sz, j)]
            total = jnp.sum(block * row, axis=1, keepdims=True)
            tile = jnp.where(lane == face_lane + m, total, tile)
    return tile


def weights_of(sz, modes_ref):
    return [modes_ref[6:7, own_face(sz, j)] for j in range(sz.own_faces)]


def sub_tile(sz, tiles, sub):
    total = tiles[sub * sz.gz]
    for part in range(1, sz.gz):
        total = total + tiles[sub * sz.gz + part]
    return total


def gathered_coarse(sz, tiles, held_ref, group):
    lane = lanes()
    held_ref[...] = jnp.zeros((8, sz.coarse_pad), jnp.float32)
    for sub in range(sz.subs):
        total = tiles[sub]
        for face in range(4):
            other = grid_neighbour(sz, sub, face)
            if other is not None:
                total = total + pltpu.roll(tiles[other], TILE - SLOT * (1 + (face ^ 1)), 1)
        start = sub * SLOT
        base, offset = start // TILE * TILE, start % TILE
        moved = pltpu.roll(total, (offset - group * MODE_SPAN) % TILE, 1)
        moved = jnp.where((lane >= offset) & (lane < offset + sz.modes), moved, 0.0)
        held_ref[:, base : base + TILE] += moved


def fill_coupling(sz, tiles, coupling_ref):
    lane = lanes()
    coupling_ref[...] = jnp.zeros((sz.coarse_pad, sz.coarse_pad), jnp.float32)
    for sub in range(sz.subs):
        for k in range(5):
            other = sub if k == 0 else grid_neighbour(sz, sub, k - 1)
            if other is None:
                continue
            base, offset = other * SLOT // TILE * TILE, other * SLOT % TILE
            moved = pltpu.roll(tiles[sub], (offset - 2 * MODE_SPAN - SLOT * k) % TILE, 1)
            moved = jnp.where((lane >= offset) & (lane < offset + sz.modes), moved, 0.0)
            coupling_ref[sub * SLOT : (sub + 1) * SLOT, base : base + TILE] += moved


def fill_inverse(sz, shared, inverse_ref):
    if sz.coarse_pad > sz.coarse:
        inverse_ref[sz.coarse :, :] = jnp.zeros((sz.coarse_pad - sz.coarse, sz.coarse_pad), jnp.float32)
    for sub in range(sz.subs):
        inverse_ref[sub * SLOT : (sub + 1) * SLOT, :] = shared[sub, :, 0 : sz.coarse_pad]


def solve_pair(sz, tiles, inverse_ref, coupling_ref, coarse_a, coarse_b):
    gathered_coarse(sz, tiles, coarse_a, 0)
    gathered_coarse(sz, tiles, coarse_b, 1)
    first = exact_dot(coarse_a[...], inverse_ref[...])
    coarse_a[...] = first
    coarse_b[...] = exact_dot(coarse_b[...] - exact_dot(first, coupling_ref[...]), inverse_ref[...])
    return coefficients(sz, coarse_a), coefficients(sz, coarse_b)


def spread(out, tile):
    out[...] = jnp.broadcast_to(tile[None], out.shape)


def part_slots(sz, part):
    return pl.ds(pl.multiple_of(part * sz.rows, TILE), sz.rows)


def put_parts(sz, parts, vector):
    if len(parts) == 1:
        for z in range(sz.gz):
            vector[:, z * sz.rows : (z + 1) * sz.rows] = parts[0][z].astype(vector.dtype)
    else:
        gz = lax.axis_index("gz")
        vector[:, part_slots(sz, gz)] = parts[0][...].astype(vector.dtype)
        vector[:, part_slots(sz, 1 - gz)] = parts[1][...].astype(vector.dtype)


def start_kernel(sz, traces, loads, inverse, stiffness, orders, rhs, lengths, count, *refs):
    outs, scratch = refs[: sz.own_faces + 2], refs[sz.own_faces + 2 :]
    faces, (pay, base) = outs[: sz.own_faces], outs[sz.own_faces :]
    traces_in, loads_in, inverse_in, stiffness_in, slots, lengths_in, count_in, sems = scratch
    gz = lax.axis_index("gz")
    here = pl.ds(pl.multiple_of(gz * sz.rows, TILE), sz.rows)
    copies = [
        pltpu.make_async_copy(inverse, inverse_in, sems.at[0]),
        pltpu.make_async_copy(loads, loads_in, sems.at[1]),
        pltpu.make_async_copy(traces.at[:, :, here], traces_in, sems.at[2]),
        pltpu.make_async_copy(stiffness.at[0, :, here], stiffness_in, sems.at[3]),
        pltpu.make_async_copy(orders.at[0, 0], slots, sems.at[4]),
        pltpu.make_async_copy(rhs.at[0, 0, :, here], base.at[pl.ds(8, 8), :], sems.at[5]),
        pltpu.make_async_copy(lengths, lengths_in, sems.at[6]),
        pltpu.make_async_copy(count, count_in, sems.at[7]),
    ]
    for copy in copies:
        copy.start()
    pay[...] = jnp.zeros(pay.shape, jnp.float32)
    base[sz.modes : 8, :] = jnp.zeros((8 - sz.modes, sz.rows), jnp.float32)
    for copy in copies:
        copy.wait()
    for m in range(sz.modes):
        mask = (m < count_in[0, 0]).astype(jnp.float32)
        for t in range(sz.subs):
            pay[0, m : m + 1, t * SLOT : t * SLOT + sz.modes] = inverse_in[
                m, :, t * sz.modes : (t + 1) * sz.modes
            ]
        pay[0, m : m + 1, sz.coarse_pad : sz.coarse_pad + sz.loads] = loads_in[m] * mask
        base[m : m + 1, :] = traces_in[m] * mask
    position = lax.broadcasted_iota(jnp.int32, (1, sz.cap), 1)
    base[6:7, :] = stiffness_in[...]
    for j in range(sz.own_faces):
        index = gz * sz.own_faces + j
        base[7:8, own_face(sz, j)] = (position < lengths_in[0, 0, index]).astype(jnp.float32)
        chosen = jnp.broadcast_to(slots[pl.ds(index, 1), :], (8, sz.cap))
        base[16:24, own_face(sz, j)] = chosen.astype(jnp.float32)
    put_slots(sz, faces, [base[0:8, own_face(sz, j)] for j in range(sz.own_faces)])
    chunk = pay[0]
    for k in range(1, pay.shape[0]):
        pay[k] = chunk


def first_kernel(sz, shared, base, *refs):
    arrived, refs = refs[: sz.own_faces], refs[sz.own_faces :]
    estimate_ref, modes_ref, right, inverse_ref, loads_ref, coarse_ref = refs
    right[...] = base[8:16, :]
    fill_inverse(sz, shared, inverse_ref)
    if sz.coarse_pad > sz.coarse:
        loads_ref[sz.coarse :, :] = jnp.zeros((sz.coarse_pad - sz.coarse, TILE), jnp.float32)
    for sub in range(sz.subs):
        loads_ref[sub * SLOT : (sub + 1) * SLOT, :] = shared[sub, :, sz.coarse_pad :]
    turned = jnp.concatenate(
        [
            jnp.transpose(loads_ref[k * TILE : (k + 1) * TILE, :])[0:8, :]
            for k in range(sz.coarse_pad // TILE)
        ],
        axis=1,
    )
    coarse_ref[...] = exact_dot(turned, inverse_ref[...])
    row = lax.broadcasted_iota(jnp.int32, (8, 1), 0)
    arrived = get_slots(sz, arrived)
    for j in range(sz.own_faces):
        here = own_face(sz, j)
        other = permuted(sz, arrived[j], base[16:24, here])
        mine = base[0:8, here]
        live = mine[7:8, :]
        total = live * (mine[6:7, :] + other[6:7, :])
        weight = live / (total + 1.0 - live)
        modes_ref[0:8, here] = jnp.where(row == 6, weight, jnp.where(row == 7, live, mine * live))
        shared_rows = jnp.where(row == 6, base[16:24, here], 0.0)
        modes_ref[8:16, here] = jnp.where(row < sz.modes, other * live, shared_rows)
    coeffs = coefficients(sz, coarse_ref)
    for j in range(sz.own_faces):
        estimate_ref[:, own_face(sz, j)] = mode_sum(sz, coeffs, modes_ref, j)


def hold_kernel(sz, operator, after, held, sems):
    del after
    copies = [
        pltpu.make_async_copy(
            operator.at[0, 0, pl.ds(k * ROW_CHUNK, ROW_CHUNK), :], held.at[k], sems.at[k]
        )
        for k in range(sz.rows // ROW_CHUNK)
    ]
    for copy in copies:
        copy.start()
    for copy in copies:
        copy.wait()


def apply_rows(sz, vector, held):
    parts = []
    for k in range(sz.rows // ROW_CHUNK):
        part = lax.dot_general(
            vector[...], held[k], (((1,), (1,)), ((), ())), preferred_element_type=jnp.float32
        )
        parts.append(part.astype(jnp.bfloat16).astype(jnp.float32))
    per_face = sz.cap // ROW_CHUNK
    return [
        jnp.concatenate(parts[j * per_face : (j + 1) * per_face], axis=1)
        for j in range(sz.own_faces)
    ]


def first_apply_kernel(sz, held, modes_ref, right, *refs):
    parts, refs = refs[: -sz.own_faces - 2], refs[-sz.own_faces - 2 :]
    outs, (pay, vector) = refs[: sz.own_faces], refs[sz.own_faces :]
    put_parts(sz, parts, vector)
    weights = weights_of(sz, modes_ref)
    row = lax.broadcasted_iota(jnp.int32, (8, 1), 0)
    coarse_rows = [
        jnp.where(row < sz.modes, modes_ref[0:8, own_face(sz, j)] * weights[j], 0.0)
        for j in range(sz.own_faces)
    ]
    tile = jnp.zeros((8, TILE), jnp.float32)
    tile = mode_products(sz, tile, coarse_rows, modes_ref, 2 * MODE_SPAN)
    pieces = apply_rows(sz, vector, held)
    vectors = [right[:, own_face(sz, j)] - piece for j, piece in enumerate(pieces)]
    put_slots(sz, outs, vectors)
    tile = mode_products(sz, tile, vectors, modes_ref, 0)
    scaled = [v * w for v, w in zip(vectors, weights)]
    spread(pay, mode_products(sz, tile, scaled, modes_ref, MODE_SPAN))


def assembled(sz, own, arrived, modes_ref, j):
    other = permuted(sz, arrived[j], modes_ref[14:15, own_face(sz, j)])
    return modes_ref[7:8, own_face(sz, j)] * (own[j] + other)


def second_kernel(sz, pieces, shared, modes_ref, *refs):
    own, refs = refs[: sz.own_faces], refs[sz.own_faces :]
    arrived, refs = refs[: sz.own_faces], refs[sz.own_faces :]
    residual_ref, direction_ref, inverse_ref, coupling_ref, coarse_a, coarse_b = refs
    fill_inverse(sz, shared, inverse_ref)
    tiles = [sub_tile(sz, pieces, sub) for sub in range(sz.subs)]
    fill_coupling(sz, tiles, coupling_ref)
    first, second = solve_pair(sz, tiles, inverse_ref, coupling_ref, coarse_a, coarse_b)
    own, arrived = get_slots(sz, own), get_slots(sz, arrived)
    for j in range(sz.own_faces):
        here = own_face(sz, j)
        gap = assembled(sz, own, arrived, modes_ref, j)
        residual = gap - mode_sum(sz, first, modes_ref, j)
        residual_ref[:, here] = residual
        direction_ref[:, here] = modes_ref[6:7, here] * residual - mode_sum(sz, second, modes_ref, j)


def second_apply_kernel(sz, held, modes_ref, direction, residual, *refs):
    parts, refs = refs[: -sz.own_faces - 2], refs[-sz.own_faces - 2 :]
    outs, (pay, vector) = refs[: sz.own_faces], refs[sz.own_faces :]
    put_parts(sz, parts, vector)
    weights = weights_of(sz, modes_ref)
    lane = lanes()
    curvature = jnp.zeros((8, 1), jnp.float32)
    resid_dot = jnp.zeros((8, 1), jnp.float32)
    for j in range(sz.own_faces):
        own = residual[:, own_face(sz, j)]
        resid_dot += jnp.sum(own * (weights[j] * own), axis=1, keepdims=True)
    pieces = apply_rows(sz, vector, held)
    put_slots(sz, outs, pieces)
    for j, piece in enumerate(pieces):
        curvature += jnp.sum(direction[:, own_face(sz, j)] * piece, axis=1, keepdims=True)
    tile = jnp.where(lane == SCALARS, curvature, jnp.zeros((8, TILE), jnp.float32))
    tile = jnp.where(lane == SCALARS + 1, resid_dot, tile)
    tile = mode_products(sz, tile, pieces, modes_ref, 0)
    scaled = [v * w for v, w in zip(pieces, weights)]
    spread(pay, mode_products(sz, tile, scaled, modes_ref, MODE_SPAN))


def third_kernel(sz, pieces, shared, before, modes_ref, residual_ref, direction_ref, *refs):
    own, refs = refs[: sz.own_faces], refs[sz.own_faces :]
    arrived, refs = refs[: sz.own_faces], refs[sz.own_faces :]
    later_ref, scalars_ref, inverse_ref, coupling_ref, coarse_a, coarse_b = refs
    lane = lanes()
    fill_inverse(sz, shared, inverse_ref)
    fill_coupling(sz, [sub_tile(sz, before, sub) for sub in range(sz.subs)], coupling_ref)
    tiles = [sub_tile(sz, pieces, sub) for sub in range(sz.subs)]
    totals = tiles[0]
    for tile in tiles[1:]:
        totals = totals + tile
    curvature = 2.0 * totals[:, SCALARS : SCALARS + 1]
    resid_dot = totals[:, SCALARS + 1 : SCALARS + 2]
    step = resid_dot / curvature
    first, second = solve_pair(sz, tiles, inverse_ref, coupling_ref, coarse_a, coarse_b)
    dot_part = jnp.zeros((8, 1), jnp.float32)
    own, arrived = get_slots(sz, own), get_slots(sz, arrived)
    for j in range(sz.own_faces):
        here = own_face(sz, j)
        image = assembled(sz, own, arrived, modes_ref, j)
        corrected = image - mode_sum(sz, first, modes_ref, j)
        weight = modes_ref[6:7, here]
        scaled = weight * corrected - mode_sum(sz, second, modes_ref, j)
        residual = residual_ref[:, here] - step * corrected
        dot_part += jnp.sum(residual * (weight * residual), axis=1, keepdims=True)
        later_ref[:, here] = direction_ref[:, here] - step * scaled
    scalars_ref[...] = jnp.where(lane == 0, curvature, jnp.where(lane == 1, resid_dot, dot_part))


def third_apply_kernel(sz, held, later, direction, scalars, *refs):
    before, refs = get_slots(sz, refs[: sz.own_faces]), refs[sz.own_faces :]
    parts, (pay, vector) = refs[:-2], refs[-2:]
    put_parts(sz, parts, vector)
    pieces = apply_rows(sz, vector, held)
    lane = lanes()
    later_part = jnp.zeros((8, 1), jnp.float32)
    cross_part = jnp.zeros((8, 1), jnp.float32)
    for j, piece in enumerate(pieces):
        mine = later[:, own_face(sz, j)]
        earlier = direction[:, own_face(sz, j)]
        later_part += jnp.sum(mine * piece, axis=1, keepdims=True)
        cross_part += jnp.sum(mine * before[j] + earlier * piece, axis=1, keepdims=True)
    load = lax.broadcasted_iota(jnp.int32, (8, TILE), 0)
    line = jnp.where(lane == load, later_part, 0.0)
    line = jnp.where(lane == load + 8, cross_part, line)
    line = jnp.where(lane == load + 16, scalars[:, 2:3], line)
    spread(pay, jnp.sum(line, axis=0, keepdims=True))


def last_kernel(sz, pieces, scalars, *refs):
    out = refs[-1]
    count = (len(refs) - 1) // 3
    estimate, direction, later = refs[:count], refs[count : 2 * count], refs[2 * count : 3 * count]
    totals = pieces[0]
    for k in range(1, pieces.shape[0]):
        totals = totals + pieces[k]
    curvature, previous = scalars[:, 0:1], scalars[:, 1:2]
    load = lax.broadcasted_iota(jnp.int32, (8, TILE), 0)
    later_part, cross_part, dot = [
        jnp.sum(jnp.where(lanes() == load + 8 * k, totals, 0.0), axis=1, keepdims=True)
        for k in range(3)
    ]
    ratio = dot / previous
    final = 2.0 * (later_part + ratio * cross_part) + ratio * ratio * curvature
    first, second = previous / curvature, dot / final
    gz = lax.axis_index("gz")
    for z in range(sz.gz):
        if count == 1:
            here, parts = part_slots(sz, z), [x[0][z] for x in (estimate, direction, later)]
        else:
            here = part_slots(sz, 1 - gz if z else gz)
            parts = [x[z][...] for x in (estimate, direction, later)]
        moved = parts[0] + first * parts[1]
        out[0, 0, :, here] = moved + second * (parts[2] + ratio * parts[1])


def shards(mesh_shape, operator, rhs_parts, stiffness, traces, coarse_inverse, rigid_loads,
           face_lengths, face_order, mode_count):
    sz = Sizes(mesh_shape, operator, traces, rhs_parts.shape[2])
    vmem = pl.BlockSpec(memory_space=pltpu.VMEM)
    smem = pl.BlockSpec(memory_space=pltpu.SMEM)
    hbm = pl.BlockSpec(memory_space=pltpu.HBM)
    everywhere = ("gx", "gy", "gz")
    small = sz.coarse_pad <= 256

    def call(kernel, out_shape, in_specs, scratch, *operands, limit=None, cost=None):
        return pl.pallas_call(
            functools.partial(kernel, sz),
            out_shape=out_shape,
            in_specs=in_specs,
            out_specs=jax.tree.map(lambda _: vmem, out_shape),
            scratch_shapes=scratch,
            cost_estimate=cost,
            compiler_params=pltpu.CompilerParams(
                vmem_limit_bytes=(limit or (16 if small else 56)) * MIB
            ),
        )(*operands)

    faces = sz.own_faces
    coarse = pltpu.VMEM((8, sz.coarse_pad), jnp.float32)
    square = pltpu.VMEM((sz.coarse_pad, sz.coarse_pad), jnp.float32)
    half = f32(8, sz.rows)
    face = f32(8, sz.cap)
    one_step = sz.devices <= 64
    spread_tile = f32(sz.devices if one_step else 1, 8, TILE)
    chunks = sz.rows // ROW_CHUNK
    vector = [pltpu.VMEM((8, sz.order), jnp.bfloat16)]

    def hold(after):
        return call(
            hold_kernel, jax.ShapeDtypeStruct((chunks, ROW_CHUNK, sz.order), jnp.bfloat16),
            [hbm, vmem], [pltpu.SemaphoreType.DMA((chunks,))], operator, after, limit=42,
            cost=pl.CostEstimate(flops=0, bytes_accessed=4 * sz.rows * sz.order, transcendentals=0),
        )

    def swap(own):
        return [lax.ppermute(own[j], everywhere, face_pairs(sz, j)) for j in range(faces)]

    def share(chunk, axes):
        if chunk.shape[0] == 1:
            return lax.all_gather(chunk, axes, axis=0, tiled=True)
        return lax.all_to_all(chunk, axes, split_axis=0, concat_axis=0, tiled=True)

    def whole(part):
        if sz.gz == 2:
            return [part, lax.ppermute(part, "gz", [(0, 1), (1, 0)])]
        return [lax.all_gather(part, "gz", axis=0, tiled=False)]

    *own, pay, base = call(
        start_kernel,
        [face] * faces + [
            f32(sz.subs if one_step else 1, 8, sz.coarse_pad + TILE),
            f32(24, sz.rows),
        ],
        [hbm] * 8,
        [
            pltpu.VMEM((sz.modes, 1, sz.rows), jnp.float32),
            pltpu.VMEM((sz.modes, 1, sz.loads), jnp.float32),
            pltpu.VMEM((sz.modes, 1, sz.subs * sz.modes), jnp.float32),
            pltpu.VMEM((1, sz.rows), jnp.float32),
            pltpu.VMEM((4, sz.cap), jnp.int32),
            pltpu.SMEM((1, 1, 4), jnp.int32),
            pltpu.SMEM((1, 1), jnp.int32),
            pltpu.SemaphoreType.DMA((8,)),
        ],
        traces.reshape(sz.modes, 1, sz.order), rigid_loads.reshape(sz.modes, 1, sz.loads),
        coarse_inverse.reshape(sz.modes, 1, -1), stiffness, face_order, rhs_parts,
        face_lengths, mode_count, limit=60,
    )
    arrived = swap(own)
    shared = share(pay, ("gx", "gy"))
    estimate, modes, right = call(
        first_kernel, [half, f32(16, sz.rows), half], [vmem] * (2 + faces),
        [square, pltpu.VMEM((sz.coarse_pad, TILE), jnp.float32), coarse],
        shared, base, *arrived,
    )
    estimates = whole(estimate)
    *own, pay = call(
        first_apply_kernel, [face] * faces + [spread_tile], [vmem] * (3 + len(estimates)),
        vector, hold(estimate), modes, right, *estimates,
    )
    arrived = swap(own)
    before = share(pay, everywhere)
    residual, direction = call(
        second_kernel, [half, half], [vmem] * (3 + 2 * faces), [square, square, coarse, coarse],
        before, shared, modes, *own, *arrived,
    )
    directions = whole(direction)
    *own, pay = call(
        second_apply_kernel, [face] * faces + [spread_tile], [vmem] * (4 + len(directions)),
        vector, hold(direction), modes, direction, residual, *directions,
    )
    arrived = swap(own)
    pieces = share(pay, everywhere)
    later, scalars = call(
        third_kernel, [half, f32(8, TILE)], [vmem] * (6 + 2 * faces),
        [square, square, coarse, coarse],
        pieces, shared, before, modes, residual, direction, *own, *arrived,
    )
    laters = whole(later)
    pay = call(
        third_apply_kernel, f32(sz.devices if one_step else 1, 1, TILE),
        [vmem] * (4 + faces + len(laters)),
        vector, hold(later), later, direction, scalars, *own, *laters,
    )
    return call(
        last_kernel, f32(1, 1, 8, sz.order), [vmem] * (2 + 3 * len(laters)), [],
        share(pay, everywhere), scalars, *estimates, *directions, *laters,
    )


def solution(mesh):
    in_specs = (
        P("gx", "gy", "gz", None),
        P("gx", "gy", None, None),
        P("gx", "gy", None),
        P("gx", "gy", None, None),
        P("gx", "gy", None, None),
        P("gx", "gy", None, None),
        P("gx", "gy", None),
        P("gx", "gy", None, None),
        P("gx", "gy"),
    )
    out_specs = P("gx", "gy", None, None)
    mesh_shape = tuple(mesh.shape[axis] for axis in ("gx", "gy", "gz"))
    return jax.shard_map(
        functools.partial(shards, mesh_shape),
        mesh=mesh, in_specs=in_specs, out_specs=out_specs, check_vma=False,
    )
```

```python
import functools

import jax
import jax.numpy as jnp
from jax import lax
from jax.experimental import pallas as pl
from jax.experimental.pallas import tpu as pltpu
from jax.sharding import PartitionSpec as P

ROW_CHUNK = 256
PIECE = 128
IN_FLIGHT = 4
LOAD_LANE = 6
TILE = 128
SLOT = 8
MODE_SPAN = 5 * SLOT
SCALARS = 3 * MODE_SPAN
MIB = 1024 * 1024


class Sizes:
    def __init__(self, mesh_shape, operator, traces, loads):
        self.sx, self.sy, self.gz = mesh_shape
        self.rows = operator.shape[2]
        self.order = operator.shape[3]
        self.modes = traces.shape[2]
        self.cap = self.order // 4
        self.loads = loads
        self.subs = self.sx * self.sy
        self.devices = self.subs * self.gz
        self.coarse = self.subs * SLOT
        self.coarse_pad = -(-self.coarse // TILE) * TILE
        self.own_faces = self.rows // self.cap
        assert self.rows % self.cap == 0 and self.cap % TILE == 0
        assert self.modes <= SLOT - 2 and self.loads == 8


def f32(*shape):
    return jax.ShapeDtypeStruct(shape, jnp.float32)


def lanes(shape=(8, TILE)):
    return lax.broadcasted_iota(jnp.int32, shape, 1)


def exact_dot(a, b):
    return jnp.dot(a, b, precision=lax.Precision.HIGHEST, preferred_element_type=jnp.float32)


def clamp(index, count):
    return jnp.minimum(jnp.maximum(index, 0), count - 1)


def neighbour(sz, face):
    gx, gy = lax.axis_index("gx"), lax.axis_index("gy")
    x = gx + jnp.where(face == 0, -1, jnp.where(face == 1, 1, 0))
    y = gy + jnp.where(face == 2, -1, jnp.where(face == 3, 1, 0))
    return clamp(x, sz.sx) * sz.sy + clamp(y, sz.sy)


def grid_neighbour(sz, sub, face):
    x, y = divmod(sub, sz.sy)
    x, y = [(x - 1, y), (x + 1, y), (x, y - 1), (x, y + 1)][face]
    return x * sz.sy + y if 0 <= x < sz.sx and 0 <= y < sz.sy else None


def face_pairs(sz, slot):
    pairs = []
    for sub in range(sz.subs):
        for part in range(sz.gz):
            local = slot
            if sz.own_faces > 1:
                first = part * sz.own_faces + slot // 2 * 2
                index = divmod(sub, sz.sy)[first // 2]
                local = slot ^ 1 ^ index & 1
            face = part * sz.own_faces + local
            other = grid_neighbour(sz, sub, face)
            if other is not None:
                pairs.append((sub * sz.gz + part, other * sz.gz + (face ^ 1) // sz.own_faces))
    return pairs


def by_slot(sz, values):
    if sz.own_faces == 1:
        return values
    result = []
    for j in range(0, sz.own_faces, 2):
        first = lax.axis_index("gz") * sz.own_faces + j
        index = jnp.where(first < 2, lax.axis_index("gx"), lax.axis_index("gy"))
        odd = lax.rem(index, 2) == 1
        low, high = values[j], values[j + 1]
        result += [jnp.where(odd, low, high), jnp.where(odd, high, low)]
    return result


def own_face(sz, j):
    return slice(j * sz.cap, (j + 1) * sz.cap)


def put_slots(sz, outs, values):
    for out, value in zip(outs, by_slot(sz, values)):
        out[...] = value


def get_slots(sz, refs):
    return by_slot(sz, [ref[...] for ref in refs])


def permuted(sz, block, slots):
    count = sz.cap // TILE
    pieces = [block[:, k * TILE : (k + 1) * TILE] for k in range(count)]
    result = []
    for j in range(count):
        index = jnp.broadcast_to(slots[:, j * TILE : (j + 1) * TILE], (8, TILE)).astype(jnp.int32)
        low = index & (TILE - 1)
        high = index >> (TILE.bit_length() - 1)
        total = jnp.zeros((8, TILE), jnp.float32)
        for k in range(count):
            picked = jnp.take_along_axis(pieces[k], low, axis=1, mode="promise_in_bounds")
            total = jnp.where(high == k, picked, total)
        result.append(total)
    return jnp.concatenate(result, axis=1)


def coefficients(sz, coarse_ref, sub):
    start = sub * SLOT
    base = pl.multiple_of((start // TILE) * TILE, TILE)
    tile = coarse_ref[:, pl.ds(base, TILE)]
    return pltpu.roll(tile, lax.rem(TILE - lax.rem(start, TILE), TILE), 1)


def views(sz, own, rest):
    if sz.gz == 2:
        gz = lax.axis_index("gz")
        return [(gz, own), (1 - gz, rest)]
    return [(z, rest.at[z]) for z in range(sz.gz)]


def mode_sum(sz, coarse_ref, mine, modes_ref, part, j):
    other = coefficients(sz, coarse_ref, neighbour(sz, part * sz.own_faces + j))
    total = None
    for tile, base in ((mine, 0), (other, SLOT)):
        for m in range(sz.modes):
            term = tile[:, m : m + 1] * modes_ref[base + m : base + m + 1, own_face(sz, j)]
            total = term if total is None else total + term
    return total


def own_coefficients(sz, coarse_ref):
    return coefficients(sz, coarse_ref, lax.axis_index("gx") * sz.sy + lax.axis_index("gy"))


def face_slots(sz, part, j):
    return pl.ds(pl.multiple_of(part * sz.rows + j * sz.cap, TILE), sz.cap)


def mode_products(sz, tile, blocks, modes_ref, first_lane):
    lane = lanes()
    gz = lax.axis_index("gz")
    for m in range(sz.modes):
        total = None
        for j, block in enumerate(blocks):
            term = jnp.sum(block * modes_ref[m : m + 1, own_face(sz, j)], axis=1, keepdims=True)
            total = term if total is None else total + term
        tile = jnp.where(lane == first_lane + m, total, tile)
    for j, block in enumerate(blocks):
        face_lane = first_lane + SLOT * (1 + gz * sz.own_faces + j)
        for m in range(sz.modes):
            row = modes_ref[SLOT + m : SLOT + m + 1, own_face(sz, j)]
            total = jnp.sum(block * row, axis=1, keepdims=True)
            tile = jnp.where(lane == face_lane + m, total, tile)
    return tile


def weights_of(sz, modes_ref):
    return [modes_ref[6:7, own_face(sz, j)] for j in range(sz.own_faces)]


def sub_tile(sz, tiles, sub):
    total = tiles[sub * sz.gz]
    for part in range(1, sz.gz):
        total = total + tiles[sub * sz.gz + part]
    return total


def gathered_coarse(sz, tiles, held_ref, group):
    lane = lanes()
    held_ref[...] = jnp.zeros((8, sz.coarse_pad), jnp.float32)
    for sub in range(sz.subs):
        total = tiles[sub]
        for face in range(4):
            other = grid_neighbour(sz, sub, face)
            if other is not None:
                total = total + pltpu.roll(tiles[other], TILE - SLOT * (1 + (face ^ 1)), 1)
        start = sub * SLOT
        base, offset = start // TILE * TILE, start % TILE
        moved = pltpu.roll(total, (offset - group * MODE_SPAN) % TILE, 1)
        moved = jnp.where((lane >= offset) & (lane < offset + sz.modes), moved, 0.0)
        held_ref[:, base : base + TILE] += moved


def fill_coupling(sz, tiles, coupling_ref):
    lane = lanes()
    coupling_ref[...] = jnp.zeros((sz.coarse_pad, sz.coarse_pad), jnp.float32)
    for sub in range(sz.subs):
        for k in range(5):
            other = sub if k == 0 else grid_neighbour(sz, sub, k - 1)
            if other is None:
                continue
            base, offset = other * SLOT // TILE * TILE, other * SLOT % TILE
            moved = pltpu.roll(tiles[sub], (offset - 2 * MODE_SPAN - SLOT * k) % TILE, 1)
            moved = jnp.where((lane >= offset) & (lane < offset + sz.modes), moved, 0.0)
            coupling_ref[sub * SLOT : (sub + 1) * SLOT, base : base + TILE] += moved


def fill_inverse(sz, shared, inverse_ref):
    if sz.coarse_pad > sz.coarse:
        inverse_ref[sz.coarse :, :] = jnp.zeros((sz.coarse_pad - sz.coarse, sz.coarse_pad), jnp.float32)
    for sub in range(sz.subs):
        inverse_ref[sub * SLOT : (sub + 1) * SLOT, :] = shared[sub]


def solve_pair(sz, tiles, inverse_ref, coupling_ref, coarse_a, coarse_b):
    gathered_coarse(sz, tiles, coarse_a, 0)
    gathered_coarse(sz, tiles, coarse_b, 1)
    first = exact_dot(coarse_a[...], inverse_ref[...])
    coarse_a[...] = first
    coarse_b[...] = exact_dot(coarse_b[...] - exact_dot(first, coupling_ref[...]), inverse_ref[...])


def spread(out, tile):
    out[...] = jnp.broadcast_to(tile[None], out.shape)


class Stream:
    def __init__(self, sz, operator, held, sems):
        self.sz, self.held = sz, held
        blocks = PIECE // 8
        self.copies = [
            pltpu.make_async_copy(
                operator.at[pl.ds(k * blocks, blocks)], held.at[pl.ds(k * blocks, blocks)], sems.at[k]
            )
            for k in range(sz.rows // PIECE)
        ]
        for copy in self.copies[:IN_FLIGHT]:
            copy.start()

    def apply(self, vector):
        sz, step, blocks = self.sz, ROW_CHUNK // PIECE, ROW_CHUNK // 8
        parts = []
        for k in range(sz.rows // ROW_CHUNK):
            for p in range(k * step, (k + 1) * step):
                self.copies[p].wait()
                if p + IN_FLIGHT < len(self.copies):
                    self.copies[p + IN_FLIGHT].start()
            rows = self.held[k * blocks : (k + 1) * blocks].reshape(ROW_CHUNK, sz.order)
            part = lax.dot_general(
                vector[...], rows, (((1,), (1,)), ((), ())), preferred_element_type=jnp.float32
            )
            parts.append(part.astype(jnp.bfloat16).astype(jnp.float32))
        per_face = sz.cap // ROW_CHUNK
        return [
            jnp.concatenate(parts[j * per_face : (j + 1) * per_face], axis=1)
            for j in range(sz.own_faces)
        ]


def start_kernel(sz, traces, loads, inverse, stiffness, orders, rhs, lengths, count, *refs):
    outs, scratch = refs[: sz.own_faces + 2], refs[sz.own_faces + 2 :]
    faces, (pay, base) = outs[: sz.own_faces], outs[sz.own_faces :]
    traces_in, loads_in, inverse_in, stiffness_in, slots, lengths_in, count_in, sems = scratch
    gz = lax.axis_index("gz")
    here = pl.ds(pl.multiple_of(gz * sz.rows, TILE), sz.rows)
    copies = [
        pltpu.make_async_copy(inverse, inverse_in, sems.at[0]),
        pltpu.make_async_copy(loads, loads_in, sems.at[1]),
        pltpu.make_async_copy(traces.at[:, :, here], traces_in, sems.at[2]),
        pltpu.make_async_copy(stiffness.at[0, :, here], stiffness_in, sems.at[3]),
        pltpu.make_async_copy(orders.at[0, 0], slots, sems.at[4]),
        pltpu.make_async_copy(rhs.at[0, 0, :, here], base.at[pl.ds(8, 8), :], sems.at[5]),
        pltpu.make_async_copy(lengths, lengths_in, sems.at[6]),
        pltpu.make_async_copy(count, count_in, sems.at[7]),
    ]
    for copy in copies:
        copy.start()
    pay[...] = jnp.zeros(pay.shape, jnp.float32)
    base[sz.modes : 8, :] = jnp.zeros((8 - sz.modes, sz.rows), jnp.float32)
    for copy in copies:
        copy.wait()
    for m in range(sz.modes):
        mask = (m < count_in[0, 0]).astype(jnp.float32)
        for t in range(sz.subs):
            pay[0, m : m + 1, t * SLOT : t * SLOT + sz.modes] = inverse_in[
                m, :, t * sz.modes : (t + 1) * sz.modes
            ]
        loads_row = loads_in[m] * mask
        row = pay[0, m : m + 1, 0:TILE]
        for load in range(sz.loads):
            row = jnp.where(lanes((1, TILE)) == SLOT * load + LOAD_LANE, loads_row[:, load : load + 1], row)
        pay[0, m : m + 1, 0:TILE] = row
        base[m : m + 1, :] = traces_in[m] * mask
    position = lax.broadcasted_iota(jnp.int32, (1, sz.cap), 1)
    base[6:7, :] = stiffness_in[...]
    for j in range(sz.own_faces):
        index = gz * sz.own_faces + j
        base[7:8, own_face(sz, j)] = (position < lengths_in[0, 0, index]).astype(jnp.float32)
        chosen = jnp.broadcast_to(slots[pl.ds(index, 1), :], (8, sz.cap))
        base[16:24, own_face(sz, j)] = chosen.astype(jnp.float32)
    put_slots(sz, faces, [base[0:8, own_face(sz, j)] for j in range(sz.own_faces)])
    chunk = pay[0]
    for k in range(1, pay.shape[0]):
        pay[k] = chunk


def modes_kernel(sz, base, *refs):
    arrived, (modes_ref, right) = refs[: sz.own_faces], refs[sz.own_faces :]
    right[...] = base[8:16, :]
    row = lax.broadcasted_iota(jnp.int32, (8, 1), 0)
    arrived = get_slots(sz, arrived)
    for j in range(sz.own_faces):
        here = own_face(sz, j)
        other = permuted(sz, arrived[j], base[16:24, here])
        mine = base[0:8, here]
        live = mine[7:8, :]
        total = live * (mine[6:7, :] + other[6:7, :])
        weight = live / (total + 1.0 - live)
        modes_ref[0:8, here] = jnp.where(row == 6, weight, jnp.where(row == 7, live, mine * live))
        slots_row = jnp.where(row == 6, base[16:24, here], 0.0)
        modes_ref[8:16, here] = jnp.where(row < sz.modes, other * live, slots_row)


def assemble_kernel(sz, modes_ref, *refs):
    own, arrived = get_slots(sz, refs[: sz.own_faces]), get_slots(sz, refs[sz.own_faces : -1])
    out = refs[-1]
    for j in range(sz.own_faces):
        here = own_face(sz, j)
        other = permuted(sz, arrived[j], modes_ref[14:15, here])
        out[:, here] = modes_ref[7:8, here] * (own[j] + other)


def first_kernel(sz, operator, shared, right, modes_ref, modes_rest, *refs):
    outs, refs = refs[: sz.own_faces], refs[sz.own_faces :]
    pay, estimate_ref, inverse_ref, coarse_ref, held, vector, sems = refs
    stream = Stream(sz, operator, held, sems)
    fill_inverse(sz, shared, inverse_ref)
    turned = []
    for k in range(sz.coarse_pad // TILE):
        block = jnp.transpose(inverse_ref[k * TILE : (k + 1) * TILE, 0:TILE])
        rows = [SLOT * load + LOAD_LANE for load in range(sz.loads)]
        turned.append(jnp.concatenate([block[r : r + 1] for r in rows], axis=0))
    coarse_ref[...] = exact_dot(jnp.concatenate(turned, axis=1), inverse_ref[...])
    mine = own_coefficients(sz, coarse_ref)
    for part, modes in views(sz, modes_ref, modes_rest):
        for j in range(sz.own_faces):
            here = face_slots(sz, part, j)
            estimate = mode_sum(sz, coarse_ref, mine, modes, part, j)
            estimate_ref[:, here] = estimate
            vector[:, here] = estimate.astype(jnp.bfloat16)
    weights = weights_of(sz, modes_ref)
    row = lax.broadcasted_iota(jnp.int32, (8, 1), 0)
    coarse_rows = [
        jnp.where(row < sz.modes, modes_ref[0:8, own_face(sz, j)] * weights[j], 0.0)
        for j in range(sz.own_faces)
    ]
    tile = jnp.zeros((8, TILE), jnp.float32)
    tile = mode_products(sz, tile, coarse_rows, modes_ref, 2 * MODE_SPAN)
    pieces = stream.apply(vector)
    vectors = [right[:, own_face(sz, j)] - piece for j, piece in enumerate(pieces)]
    put_slots(sz, outs, vectors)
    tile = mode_products(sz, tile, vectors, modes_ref, 0)
    scaled = [v * w for v, w in zip(vectors, weights)]
    spread(pay, mode_products(sz, tile, scaled, modes_ref, MODE_SPAN))


def second_kernel(sz, operator, pieces, shared, modes_ref, modes_rest, gap, gap_rest, *refs):
    outs, refs = refs[: sz.own_faces], refs[sz.own_faces :]
    pay, residual_ref, direction_ref = refs[:3]
    inverse_ref, coupling_ref, coarse_a, coarse_b, held, vector, sems = refs[3:]
    stream = Stream(sz, operator, held, sems)
    fill_inverse(sz, shared, inverse_ref)
    tiles = [sub_tile(sz, pieces, sub) for sub in range(sz.subs)]
    fill_coupling(sz, tiles, coupling_ref)
    solve_pair(sz, tiles, inverse_ref, coupling_ref, coarse_a, coarse_b)
    first, second = own_coefficients(sz, coarse_a), own_coefficients(sz, coarse_b)
    both = zip(views(sz, gap, gap_rest), views(sz, modes_ref, modes_rest))
    for (part, vector_part), (_, modes) in both:
        for j in range(sz.own_faces):
            here = face_slots(sz, part, j)
            residual = vector_part[:, own_face(sz, j)] - mode_sum(sz, coarse_a, first, modes, part, j)
            weight = modes[6:7, own_face(sz, j)]
            direction = weight * residual - mode_sum(sz, coarse_b, second, modes, part, j)
            residual_ref[:, here] = residual
            direction_ref[:, here] = direction
            vector[:, here] = direction.astype(jnp.bfloat16)
    weights = weights_of(sz, modes_ref)
    gz = lax.axis_index("gz")
    lane = lanes()
    curvature = jnp.zeros((8, 1), jnp.float32)
    resid_dot = jnp.zeros((8, 1), jnp.float32)
    for j in range(sz.own_faces):
        own = residual_ref[:, face_slots(sz, gz, j)]
        resid_dot += jnp.sum(own * (weights[j] * own), axis=1, keepdims=True)
    pieces = stream.apply(vector)
    put_slots(sz, outs, pieces)
    for j, piece in enumerate(pieces):
        direction = direction_ref[:, face_slots(sz, gz, j)]
        curvature += jnp.sum(direction * piece, axis=1, keepdims=True)
    tile = jnp.where(lane == SCALARS, curvature, jnp.zeros((8, TILE), jnp.float32))
    tile = jnp.where(lane == SCALARS + 1, resid_dot, tile)
    tile = mode_products(sz, tile, pieces, modes_ref, 0)
    scaled = [v * w for v, w in zip(pieces, weights)]
    spread(pay, mode_products(sz, tile, scaled, modes_ref, MODE_SPAN))


def third_kernel(
    sz, operator, pieces, shared, before, residual_ref, direction_ref,
    modes_ref, modes_rest, image, image_rest, *refs,
):
    earlier, refs = get_slots(sz, refs[: sz.own_faces]), refs[sz.own_faces :]
    pay, later_ref, scalars_ref = refs[:3]
    inverse_ref, coupling_ref, coarse_a, coarse_b, dots, held, vector, sems = refs[3:]
    stream = Stream(sz, operator, held, sems)
    lane = lanes()
    fill_inverse(sz, shared, inverse_ref)
    fill_coupling(sz, [sub_tile(sz, before, sub) for sub in range(sz.subs)], coupling_ref)
    tiles = [sub_tile(sz, pieces, sub) for sub in range(sz.subs)]
    totals = tiles[0]
    for tile in tiles[1:]:
        totals = totals + tile
    curvature = 2.0 * totals[:, SCALARS : SCALARS + 1]
    resid_dot = totals[:, SCALARS + 1 : SCALARS + 2]
    step = resid_dot / curvature
    scalars_ref[...] = jnp.where(lane == 0, curvature, resid_dot)
    solve_pair(sz, tiles, inverse_ref, coupling_ref, coarse_a, coarse_b)
    first, second = own_coefficients(sz, coarse_a), own_coefficients(sz, coarse_b)
    both = zip(views(sz, image, image_rest), views(sz, modes_ref, modes_rest))
    for (part, vector_part), (_, modes) in both:
        for j in range(sz.own_faces):
            here = face_slots(sz, part, j)
            corrected = vector_part[:, own_face(sz, j)] - mode_sum(sz, coarse_a, first, modes, part, j)
            weight = modes[6:7, own_face(sz, j)]
            scaled = weight * corrected - mode_sum(sz, coarse_b, second, modes, part, j)
            residual = residual_ref[:, here] - step * corrected
            dots[:, here] = residual * (weight * residual)
            later = direction_ref[:, here] - step * scaled
            later_ref[:, here] = later
            vector[:, here] = later.astype(jnp.bfloat16)
    gz = lax.axis_index("gz")
    dot_part = jnp.zeros((8, 1), jnp.float32)
    for j in range(sz.own_faces):
        dot_part += jnp.sum(dots[:, face_slots(sz, gz, j)], axis=1, keepdims=True)
    pieces = stream.apply(vector)
    later_part = jnp.zeros((8, 1), jnp.float32)
    cross_part = jnp.zeros((8, 1), jnp.float32)
    for j, piece in enumerate(pieces):
        mine = later_ref[:, face_slots(sz, gz, j)]
        direction = direction_ref[:, face_slots(sz, gz, j)]
        later_part += jnp.sum(mine * piece, axis=1, keepdims=True)
        cross_part += jnp.sum(mine * earlier[j] + direction * piece, axis=1, keepdims=True)
    load = lax.broadcasted_iota(jnp.int32, (8, TILE), 0)
    line = jnp.where(lane == load, later_part, 0.0)
    line = jnp.where(lane == load + 8, cross_part, line)
    line = jnp.where(lane == load + 16, dot_part, line)
    spread(pay, jnp.sum(line, axis=0, keepdims=True))


def last_kernel(sz, pieces, scalars, estimate, direction, later, out):
    totals = pieces[0]
    for k in range(1, pieces.shape[0]):
        totals = totals + pieces[k]
    curvature, previous = scalars[:, 0:1], scalars[:, 1:2]
    load = lax.broadcasted_iota(jnp.int32, (8, TILE), 0)
    later_part, cross_part, dot = [
        jnp.sum(jnp.where(lanes() == load + 8 * k, totals, 0.0), axis=1, keepdims=True)
        for k in range(3)
    ]
    ratio = dot / previous
    final = 2.0 * (later_part + ratio * cross_part) + ratio * ratio * curvature
    first, second = previous / curvature, dot / final
    moved = estimate[...] + first * direction[...]
    out[0, 0] = moved + second * (later[...] + ratio * direction[...])


def shards(mesh_shape, operator, rhs_parts, stiffness, traces, coarse_inverse, rigid_loads,
           face_lengths, face_order, mode_count):
    sz = Sizes(mesh_shape, operator, traces, rhs_parts.shape[2])
    vmem = pl.BlockSpec(memory_space=pltpu.VMEM)
    smem = pl.BlockSpec(memory_space=pltpu.SMEM)
    hbm = pl.BlockSpec(memory_space=pltpu.HBM)
    everywhere = ("gx", "gy", "gz")
    small = sz.coarse_pad <= 256

    def call(kernel, out_shape, in_specs, scratch, *operands, limit=None, cost=None):
        return pl.pallas_call(
            functools.partial(kernel, sz),
            out_shape=out_shape,
            in_specs=in_specs,
            out_specs=jax.tree.map(lambda _: vmem, out_shape),
            scratch_shapes=scratch,
            cost_estimate=cost,
            compiler_params=pltpu.CompilerParams(
                vmem_limit_bytes=(limit or (16 if small else 56)) * MIB
            ),
        )(*operands)

    faces = sz.own_faces
    pieces = sz.rows // PIECE
    coarse = pltpu.VMEM((8, sz.coarse_pad), jnp.float32)
    square = pltpu.VMEM((sz.coarse_pad, sz.coarse_pad), jnp.float32)
    half, full, face = f32(8, sz.rows), f32(8, sz.order), f32(8, sz.cap)
    blocks = operator.reshape(sz.rows // 8, 8, sz.order)
    one_step = sz.devices <= 64
    spread_tile = f32(sz.devices if one_step else 1, 8, TILE)
    apply_scratch = [
        pltpu.VMEM((sz.rows // 8, 8, sz.order), jnp.bfloat16),
        pltpu.VMEM((8, sz.order), jnp.bfloat16),
        pltpu.SemaphoreType.DMA((pieces,)),
    ]
    large = 50 if small else 56

    def swap(own):
        return [lax.ppermute(own[j], everywhere, face_pairs(sz, j)) for j in range(faces)]

    def share(chunk, axes):
        if chunk.shape[0] == 1:
            return lax.all_gather(chunk, axes, axis=0, tiled=True)
        return lax.all_to_all(chunk, axes, split_axis=0, concat_axis=0, tiled=True)

    def rest(part):
        if sz.gz == 2:
            return lax.ppermute(part, "gz", [(0, 1), (1, 0)])
        return lax.all_gather(part, "gz", axis=0, tiled=False)

    def assemble(own):
        part = call(
            assemble_kernel, half, [vmem] * (1 + 2 * faces), [], modes, *own, *swap(own)
        )
        return part, rest(part)

    *own, pay, base = call(
        start_kernel,
        [face] * faces + [f32(sz.subs if one_step else 1, 8, sz.coarse_pad), f32(24, sz.rows)],
        [hbm] * 8,
        [
            pltpu.VMEM((sz.modes, 1, sz.rows), jnp.float32),
            pltpu.VMEM((sz.modes, 1, sz.loads), jnp.float32),
            pltpu.VMEM((sz.modes, 1, sz.subs * sz.modes), jnp.float32),
            pltpu.VMEM((1, sz.rows), jnp.float32),
            pltpu.VMEM((4, sz.cap), jnp.int32),
            pltpu.SMEM((1, 1, 4), jnp.int32),
            pltpu.SMEM((1, 1), jnp.int32),
            pltpu.SemaphoreType.DMA((8,)),
        ],
        traces.reshape(sz.modes, 1, sz.order), rigid_loads.reshape(sz.modes, 1, sz.loads),
        coarse_inverse.reshape(sz.modes, 1, -1), stiffness, face_order, rhs_parts,
        face_lengths, mode_count, limit=60,
    )
    shared = share(pay, ("gx", "gy"))
    modes, right = call(
        modes_kernel, [f32(16, sz.rows), half], [vmem] * (1 + faces), [], base, *swap(own)
    )
    modes_rest = rest(modes)
    *own, pay, estimate = call(
        first_kernel, [face] * faces + [spread_tile, full], [hbm] + [vmem] * 4,
        [square, coarse] + apply_scratch,
        blocks, shared, right, modes, modes_rest, limit=large,
    )
    before = share(pay, everywhere)
    gap, gap_rest = assemble(own)
    *own, pay, residual, direction = call(
        second_kernel, [face] * faces + [spread_tile, full, full], [hbm] + [vmem] * 6,
        [square, square, coarse, coarse] + apply_scratch,
        blocks, before, shared, modes, modes_rest, gap, gap_rest, limit=large,
    )
    after = share(pay, everywhere)
    image, image_rest = assemble(own)
    pay, later, scalars = call(
        third_kernel,
        [f32(sz.devices if one_step else 1, 1, TILE), full, f32(8, TILE)],
        [hbm] + [vmem] * (9 + faces),
        [square, square, coarse, coarse, pltpu.VMEM((8, sz.order), jnp.float32)] + apply_scratch,
        blocks, after, shared, before, residual, direction, modes, modes_rest,
        image, image_rest, *own, limit=large,
    )
    return call(
        last_kernel, f32(1, 1, 8, sz.order), [vmem] * 5, [],
        share(pay, everywhere), scalars, estimate, direction, later,
    )


def solution(mesh):
    in_specs = (
        P("gx", "gy", "gz", None),
        P("gx", "gy", None, None),
        P("gx", "gy", None),
        P("gx", "gy", None, None),
        P("gx", "gy", None, None),
        P("gx", "gy", None, None),
        P("gx", "gy", None),
        P("gx", "gy", None, None),
        P("gx", "gy"),
    )
    out_specs = P("gx", "gy", None, None)
    mesh_shape = tuple(mesh.shape[axis] for axis in ("gx", "gy", "gz"))
    return jax.shard_map(
        functools.partial(shards, mesh_shape),
        mesh=mesh, in_specs=in_specs, out_specs=out_specs, check_vma=False,
    )
```

```python
import functools

import jax
import jax.numpy as jnp
from jax import lax
from jax.experimental import pallas as pl
from jax.experimental.pallas import tpu as pltpu
from jax.sharding import PartitionSpec as P

ROW_CHUNK = 256
PIECE = 128
LOAD_LANE = 6
TILE = 128
SLOT = 8
MODE_SPAN = 5 * SLOT
SCALARS = 3 * MODE_SPAN
MIB = 1024 * 1024


class Sizes:
    def __init__(self, mesh_shape, operator, traces, loads):
        self.sx, self.sy, self.gz = mesh_shape
        self.rows = operator.shape[2]
        self.order = operator.shape[3]
        self.modes = traces.shape[2]
        self.cap = self.order // 4
        self.loads = loads
        self.subs = self.sx * self.sy
        self.devices = self.subs * self.gz
        self.coarse = self.subs * SLOT
        self.coarse_pad = -(-self.coarse // TILE) * TILE
        self.own_faces = self.rows // self.cap
        assert self.rows % self.cap == 0 and self.cap % TILE == 0
        assert self.modes <= SLOT - 2 and self.loads == 8


def f32(*shape):
    return jax.ShapeDtypeStruct(shape, jnp.float32)


def lanes(shape=(8, TILE)):
    return lax.broadcasted_iota(jnp.int32, shape, 1)


def exact_dot(a, b):
    return jnp.dot(a, b, precision=lax.Precision.HIGHEST, preferred_element_type=jnp.float32)


def clamp(index, count):
    return jnp.minimum(jnp.maximum(index, 0), count - 1)


def neighbour(sz, face):
    gx, gy = lax.axis_index("gx"), lax.axis_index("gy")
    x = gx + jnp.where(face == 0, -1, jnp.where(face == 1, 1, 0))
    y = gy + jnp.where(face == 2, -1, jnp.where(face == 3, 1, 0))
    return clamp(x, sz.sx) * sz.sy + clamp(y, sz.sy)


def grid_neighbour(sz, sub, face):
    x, y = divmod(sub, sz.sy)
    x, y = [(x - 1, y), (x + 1, y), (x, y - 1), (x, y + 1)][face]
    return x * sz.sy + y if 0 <= x < sz.sx and 0 <= y < sz.sy else None


def face_pairs(sz, slot):
    pairs = []
    for sub in range(sz.subs):
        for part in range(sz.gz):
            local = slot
            if sz.own_faces > 1:
                first = part * sz.own_faces + slot // 2 * 2
                index = divmod(sub, sz.sy)[first // 2]
                local = slot ^ 1 ^ index & 1
            face = part * sz.own_faces + local
            other = grid_neighbour(sz, sub, face)
            if other is not None:
                pairs.append((sub * sz.gz + part, other * sz.gz + (face ^ 1) // sz.own_faces))
    return pairs


def by_slot(sz, values):
    if sz.own_faces == 1:
        return values
    result = []
    for j in range(0, sz.own_faces, 2):
        first = lax.axis_index("gz") * sz.own_faces + j
        index = jnp.where(first < 2, lax.axis_index("gx"), lax.axis_index("gy"))
        odd = lax.rem(index, 2) == 1
        low, high = values[j], values[j + 1]
        result += [jnp.where(odd, low, high), jnp.where(odd, high, low)]
    return result


def own_face(sz, j):
    return slice(j * sz.cap, (j + 1) * sz.cap)


def put_slots(sz, outs, values):
    for out, value in zip(outs, by_slot(sz, values)):
        out[...] = value


def get_slots(sz, refs):
    return by_slot(sz, [ref[...] for ref in refs])


def permuted(sz, block, slots):
    count = sz.cap // TILE
    pieces = [block[:, k * TILE : (k + 1) * TILE] for k in range(count)]
    result = []
    for j in range(count):
        index = jnp.broadcast_to(slots[:, j * TILE : (j + 1) * TILE], (8, TILE)).astype(jnp.int32)
        low = index & (TILE - 1)
        high = index >> (TILE.bit_length() - 1)
        total = jnp.zeros((8, TILE), jnp.float32)
        for k in range(count):
            picked = jnp.take_along_axis(pieces[k], low, axis=1, mode="promise_in_bounds")
            total = jnp.where(high == k, picked, total)
        result.append(total)
    return jnp.concatenate(result, axis=1)


def coefficients(sz, coarse_ref, sub):
    start = sub * SLOT
    base = pl.multiple_of((start // TILE) * TILE, TILE)
    tile = coarse_ref[:, pl.ds(base, TILE)]
    return pltpu.roll(tile, lax.rem(TILE - lax.rem(start, TILE), TILE), 1)


def views(sz, own, rest):
    if sz.gz == 2:
        gz = lax.axis_index("gz")
        return [(gz, own), (1 - gz, rest)]
    return [(z, rest.at[z]) for z in range(sz.gz)]


def mode_sum(sz, coarse_ref, mine, modes_ref, part, j):
    other = coefficients(sz, coarse_ref, neighbour(sz, part * sz.own_faces + j))
    total = None
    for tile, base in ((mine, 0), (other, SLOT)):
        for m in range(sz.modes):
            term = tile[:, m : m + 1] * modes_ref[base + m : base + m + 1, own_face(sz, j)]
            total = term if total is None else total + term
    return total


def own_coefficients(sz, coarse_ref):
    return coefficients(sz, coarse_ref, lax.axis_index("gx") * sz.sy + lax.axis_index("gy"))


def face_slots(sz, part, j):
    return pl.ds(pl.multiple_of(part * sz.rows + j * sz.cap, TILE), sz.cap)


def mode_products(sz, tile, blocks, modes_ref, first_lane):
    lane = lanes()
    gz = lax.axis_index("gz")
    for m in range(sz.modes):
        total = None
        for j, block in enumerate(blocks):
            term = jnp.sum(block * modes_ref[m : m + 1, own_face(sz, j)], axis=1, keepdims=True)
            total = term if total is None else total + term
        tile = jnp.where(lane == first_lane + m, total, tile)
    for j, block in enumerate(blocks):
        face_lane = first_lane + SLOT * (1 + gz * sz.own_faces + j)
        for m in range(sz.modes):
            row = modes_ref[SLOT + m : SLOT + m + 1, own_face(sz, j)]
            total = jnp.sum(block * row, axis=1, keepdims=True)
            tile = jnp.where(lane == face_lane + m, total, tile)
    return tile


def weights_of(sz, modes_ref):
    return [modes_ref[6:7, own_face(sz, j)] for j in range(sz.own_faces)]


def sub_tile(sz, tiles, sub):
    total = tiles[sub * sz.gz]
    for part in range(1, sz.gz):
        total = total + tiles[sub * sz.gz + part]
    return total


def gathered_coarse(sz, tiles, held_ref, group):
    lane = lanes()
    held_ref[...] = jnp.zeros((8, sz.coarse_pad), jnp.float32)
    for sub in range(sz.subs):
        total = tiles[sub]
        for face in range(4):
            other = grid_neighbour(sz, sub, face)
            if other is not None:
                total = total + pltpu.roll(tiles[other], TILE - SLOT * (1 + (face ^ 1)), 1)
        start = sub * SLOT
        base, offset = start // TILE * TILE, start % TILE
        moved = pltpu.roll(total, (offset - group * MODE_SPAN) % TILE, 1)
        moved = jnp.where((lane >= offset) & (lane < offset + sz.modes), moved, 0.0)
        held_ref[:, base : base + TILE] += moved


def fill_coupling(sz, tiles, coupling_ref):
    lane = lanes()
    coupling_ref[...] = jnp.zeros((sz.coarse_pad, sz.coarse_pad), jnp.float32)
    for sub in range(sz.subs):
        for k in range(5):
            other = sub if k == 0 else grid_neighbour(sz, sub, k - 1)
            if other is None:
                continue
            base, offset = other * SLOT // TILE * TILE, other * SLOT % TILE
            moved = pltpu.roll(tiles[sub], (offset - 2 * MODE_SPAN - SLOT * k) % TILE, 1)
            moved = jnp.where((lane >= offset) & (lane < offset + sz.modes), moved, 0.0)
            coupling_ref[sub * SLOT : (sub + 1) * SLOT, base : base + TILE] += moved


def fill_inverse(sz, shared, inverse_ref):
    if sz.coarse_pad > sz.coarse:
        inverse_ref[sz.coarse :, :] = jnp.zeros((sz.coarse_pad - sz.coarse, sz.coarse_pad), jnp.float32)
    for sub in range(sz.subs):
        inverse_ref[sub * SLOT : (sub + 1) * SLOT, :] = shared[sub]


def solve_pair(sz, tiles, inverse_ref, coupling_ref, coarse_a, coarse_b):
    gathered_coarse(sz, tiles, coarse_a, 0)
    gathered_coarse(sz, tiles, coarse_b, 1)
    first = exact_dot(coarse_a[...], inverse_ref[...])
    coarse_a[...] = first
    coarse_b[...] = exact_dot(coarse_b[...] - exact_dot(first, coupling_ref[...]), inverse_ref[...])


def spread(out, tile):
    out[...] = jnp.broadcast_to(tile[None], out.shape)


class Stream:
    def __init__(self, sz, operator, held, product, sems):
        self.sz, self.operator, self.held, self.product, self.sems = sz, operator, held, product, sems
        for p in range(sz.rows // PIECE):
            self.copy(p).start()

    def copy(self, p):
        here = pl.ds(p * (PIECE // 8), PIECE // 8)
        return pltpu.make_async_copy(self.operator.at[here], self.held.at[here], self.sems.at[p])

    def apply(self, vector):
        sz, step, blocks = self.sz, ROW_CHUNK // PIECE, ROW_CHUNK // 8

        def chunk(k, carry):
            for p in range(step):
                self.copy(k * step + p).wait()
            rows = self.held[pl.ds(k * blocks, blocks)].reshape(ROW_CHUNK, sz.order)
            part = lax.dot_general(
                vector[...], rows, (((1,), (1,)), ((), ())), preferred_element_type=jnp.float32
            )
            here = pl.ds(pl.multiple_of(k * ROW_CHUNK, TILE), ROW_CHUNK)
            self.product[:, here] = part.astype(jnp.bfloat16).astype(jnp.float32)
            return carry

        lax.fori_loop(0, sz.rows // ROW_CHUNK, chunk, 0)
        return [self.product[:, own_face(sz, j)] for j in range(sz.own_faces)]


def start_kernel(sz, traces, loads, inverse, stiffness, orders, rhs, lengths, count, *refs):
    outs, scratch = refs[: sz.own_faces + 2], refs[sz.own_faces + 2 :]
    faces, (pay, base) = outs[: sz.own_faces], outs[sz.own_faces :]
    traces_in, loads_in, inverse_in, stiffness_in, slots, lengths_in, count_in, sems = scratch
    gz = lax.axis_index("gz")
    here = pl.ds(pl.multiple_of(gz * sz.rows, TILE), sz.rows)
    copies = [
        pltpu.make_async_copy(inverse, inverse_in, sems.at[0]),
        pltpu.make_async_copy(loads, loads_in, sems.at[1]),
        pltpu.make_async_copy(traces.at[:, :, here], traces_in, sems.at[2]),
        pltpu.make_async_copy(stiffness.at[0, :, here], stiffness_in, sems.at[3]),
        pltpu.make_async_copy(orders.at[0, 0], slots, sems.at[4]),
        pltpu.make_async_copy(rhs.at[0, 0, :, here], base.at[pl.ds(8, 8), :], sems.at[5]),
        pltpu.make_async_copy(lengths, lengths_in, sems.at[6]),
        pltpu.make_async_copy(count, count_in, sems.at[7]),
    ]
    for copy in copies:
        copy.start()
    pay[...] = jnp.zeros(pay.shape, jnp.float32)
    base[sz.modes : 8, :] = jnp.zeros((8 - sz.modes, sz.rows), jnp.float32)
    for copy in copies:
        copy.wait()
    for m in range(sz.modes):
        mask = (m < count_in[0, 0]).astype(jnp.float32)
        for t in range(sz.subs):
            pay[0, m : m + 1, t * SLOT : t * SLOT + sz.modes] = inverse_in[
                m, :, t * sz.modes : (t + 1) * sz.modes
            ]
        loads_row = loads_in[m] * mask
        row = pay[0, m : m + 1, 0:TILE]
        for load in range(sz.loads):
            row = jnp.where(lanes((1, TILE)) == SLOT * load + LOAD_LANE, loads_row[:, load : load + 1], row)
        pay[0, m : m + 1, 0:TILE] = row
        base[m : m + 1, :] = traces_in[m] * mask
    position = lax.broadcasted_iota(jnp.int32, (1, sz.cap), 1)
    base[6:7, :] = stiffness_in[...]
    for j in range(sz.own_faces):
        index = gz * sz.own_faces + j
        base[7:8, own_face(sz, j)] = (position < lengths_in[0, 0, index]).astype(jnp.float32)
        chosen = jnp.broadcast_to(slots[pl.ds(index, 1), :], (8, sz.cap))
        base[16:24, own_face(sz, j)] = chosen.astype(jnp.float32)
    put_slots(sz, faces, [base[0:8, own_face(sz, j)] for j in range(sz.own_faces)])
    chunk = pay[0]
    for k in range(1, pay.shape[0]):
        pay[k] = chunk


def modes_kernel(sz, base, *refs):
    arrived, (modes_ref, right) = refs[: sz.own_faces], refs[sz.own_faces :]
    right[...] = base[8:16, :]
    row = lax.broadcasted_iota(jnp.int32, (8, 1), 0)
    arrived = get_slots(sz, arrived)
    for j in range(sz.own_faces):
        here = own_face(sz, j)
        other = permuted(sz, arrived[j], base[16:24, here])
        mine = base[0:8, here]
        live = mine[7:8, :]
        total = live * (mine[6:7, :] + other[6:7, :])
        weight = live / (total + 1.0 - live)
        modes_ref[0:8, here] = jnp.where(row == 6, weight, jnp.where(row == 7, live, mine * live))
        slots_row = jnp.where(row == 6, base[16:24, here], 0.0)
        modes_ref[8:16, here] = jnp.where(row < sz.modes, other * live, slots_row)


def assemble_kernel(sz, modes_ref, *refs):
    own, arrived = get_slots(sz, refs[: sz.own_faces]), get_slots(sz, refs[sz.own_faces : -1])
    out = refs[-1]
    for j in range(sz.own_faces):
        here = own_face(sz, j)
        other = permuted(sz, arrived[j], modes_ref[14:15, here])
        out[:, here] = modes_ref[7:8, here] * (own[j] + other)


def first_kernel(sz, operator, shared, right, modes_ref, modes_rest, *refs):
    outs, refs = refs[: sz.own_faces], refs[sz.own_faces :]
    pay, estimate_ref, inverse_ref, coarse_ref, held, product, vector, sems = refs
    stream = Stream(sz, operator, held, product, sems)
    fill_inverse(sz, shared, inverse_ref)
    turned = []
    for k in range(sz.coarse_pad // TILE):
        block = jnp.transpose(inverse_ref[k * TILE : (k + 1) * TILE, 0:TILE])
        rows = [SLOT * load + LOAD_LANE for load in range(sz.loads)]
        turned.append(jnp.concatenate([block[r : r + 1] for r in rows], axis=0))
    coarse_ref[...] = exact_dot(jnp.concatenate(turned, axis=1), inverse_ref[...])
    mine = own_coefficients(sz, coarse_ref)
    for part, modes in views(sz, modes_ref, modes_rest):
        for j in range(sz.own_faces):
            here = face_slots(sz, part, j)
            estimate = mode_sum(sz, coarse_ref, mine, modes, part, j)
            estimate_ref[:, here] = estimate
            vector[:, here] = estimate.astype(jnp.bfloat16)
    weights = weights_of(sz, modes_ref)
    row = lax.broadcasted_iota(jnp.int32, (8, 1), 0)
    coarse_rows = [
        jnp.where(row < sz.modes, modes_ref[0:8, own_face(sz, j)] * weights[j], 0.0)
        for j in range(sz.own_faces)
    ]
    tile = jnp.zeros((8, TILE), jnp.float32)
    tile = mode_products(sz, tile, coarse_rows, modes_ref, 2 * MODE_SPAN)
    pieces = stream.apply(vector)
    vectors = [right[:, own_face(sz, j)] - piece for j, piece in enumerate(pieces)]
    put_slots(sz, outs, vectors)
    tile = mode_products(sz, tile, vectors, modes_ref, 0)
    scaled = [v * w for v, w in zip(vectors, weights)]
    spread(pay, mode_products(sz, tile, scaled, modes_ref, MODE_SPAN))


def second_kernel(sz, operator, pieces, shared, modes_ref, modes_rest, gap, gap_rest, *refs):
    outs, refs = refs[: sz.own_faces], refs[sz.own_faces :]
    pay, residual_ref, direction_ref = refs[:3]
    inverse_ref, coupling_ref, coarse_a, coarse_b, held, product, vector, sems = refs[3:]
    stream = Stream(sz, operator, held, product, sems)
    fill_inverse(sz, shared, inverse_ref)
    tiles = [sub_tile(sz, pieces, sub) for sub in range(sz.subs)]
    fill_coupling(sz, tiles, coupling_ref)
    solve_pair(sz, tiles, inverse_ref, coupling_ref, coarse_a, coarse_b)
    first, second = own_coefficients(sz, coarse_a), own_coefficients(sz, coarse_b)
    both = zip(views(sz, gap, gap_rest), views(sz, modes_ref, modes_rest))
    for (part, vector_part), (_, modes) in both:
        for j in range(sz.own_faces):
            here = face_slots(sz, part, j)
            residual = vector_part[:, own_face(sz, j)] - mode_sum(sz, coarse_a, first, modes, part, j)
            weight = modes[6:7, own_face(sz, j)]
            direction = weight * residual - mode_sum(sz, coarse_b, second, modes, part, j)
            residual_ref[:, here] = residual
            direction_ref[:, here] = direction
            vector[:, here] = direction.astype(jnp.bfloat16)
    weights = weights_of(sz, modes_ref)
    gz = lax.axis_index("gz")
    lane = lanes()
    curvature = jnp.zeros((8, 1), jnp.float32)
    resid_dot = jnp.zeros((8, 1), jnp.float32)
    for j in range(sz.own_faces):
        own = residual_ref[:, face_slots(sz, gz, j)]
        resid_dot += jnp.sum(own * (weights[j] * own), axis=1, keepdims=True)
    pieces = stream.apply(vector)
    put_slots(sz, outs, pieces)
    for j, piece in enumerate(pieces):
        direction = direction_ref[:, face_slots(sz, gz, j)]
        curvature += jnp.sum(direction * piece, axis=1, keepdims=True)
    tile = jnp.where(lane == SCALARS, curvature, jnp.zeros((8, TILE), jnp.float32))
    tile = jnp.where(lane == SCALARS + 1, resid_dot, tile)
    tile = mode_products(sz, tile, pieces, modes_ref, 0)
    scaled = [v * w for v, w in zip(pieces, weights)]
    spread(pay, mode_products(sz, tile, scaled, modes_ref, MODE_SPAN))


def third_kernel(
    sz, operator, pieces, shared, before, residual_ref, direction_ref,
    modes_ref, modes_rest, image, image_rest, *refs,
):
    earlier, refs = get_slots(sz, refs[: sz.own_faces]), refs[sz.own_faces :]
    pay, later_ref, scalars_ref = refs[:3]
    inverse_ref, coupling_ref, coarse_a, coarse_b, dots, held, product, vector, sems = refs[3:]
    stream = Stream(sz, operator, held, product, sems)
    lane = lanes()
    fill_inverse(sz, shared, inverse_ref)
    fill_coupling(sz, [sub_tile(sz, before, sub) for sub in range(sz.subs)], coupling_ref)
    tiles = [sub_tile(sz, pieces, sub) for sub in range(sz.subs)]
    totals = tiles[0]
    for tile in tiles[1:]:
        totals = totals + tile
    curvature = 2.0 * totals[:, SCALARS : SCALARS + 1]
    resid_dot = totals[:, SCALARS + 1 : SCALARS + 2]
    step = resid_dot / curvature
    scalars_ref[...] = jnp.where(lane == 0, curvature, resid_dot)
    solve_pair(sz, tiles, inverse_ref, coupling_ref, coarse_a, coarse_b)
    first, second = own_coefficients(sz, coarse_a), own_coefficients(sz, coarse_b)
    both = zip(views(sz, image, image_rest), views(sz, modes_ref, modes_rest))
    for (part, vector_part), (_, modes) in both:
        for j in range(sz.own_faces):
            here = face_slots(sz, part, j)
            corrected = vector_part[:, own_face(sz, j)] - mode_sum(sz, coarse_a, first, modes, part, j)
            weight = modes[6:7, own_face(sz, j)]
            scaled = weight * corrected - mode_sum(sz, coarse_b, second, modes, part, j)
            residual = residual_ref[:, here] - step * corrected
            dots[:, here] = residual * (weight * residual)
            later = direction_ref[:, here] - step * scaled
            later_ref[:, here] = later
            vector[:, here] = later.astype(jnp.bfloat16)
    gz = lax.axis_index("gz")
    dot_part = jnp.zeros((8, 1), jnp.float32)
    for j in range(sz.own_faces):
        dot_part += jnp.sum(dots[:, face_slots(sz, gz, j)], axis=1, keepdims=True)
    pieces = stream.apply(vector)
    later_part = jnp.zeros((8, 1), jnp.float32)
    cross_part = jnp.zeros((8, 1), jnp.float32)
    for j, piece in enumerate(pieces):
        mine = later_ref[:, face_slots(sz, gz, j)]
        direction = direction_ref[:, face_slots(sz, gz, j)]
        later_part += jnp.sum(mine * piece, axis=1, keepdims=True)
        cross_part += jnp.sum(mine * earlier[j] + direction * piece, axis=1, keepdims=True)
    load = lax.broadcasted_iota(jnp.int32, (8, TILE), 0)
    line = jnp.where(lane == load, later_part, 0.0)
    line = jnp.where(lane == load + 8, cross_part, line)
    line = jnp.where(lane == load + 16, dot_part, line)
    spread(pay, jnp.sum(line, axis=0, keepdims=True))


def last_kernel(sz, pieces, scalars, estimate, direction, later, out):
    totals = pieces[0]
    for k in range(1, pieces.shape[0]):
        totals = totals + pieces[k]
    curvature, previous = scalars[:, 0:1], scalars[:, 1:2]
    load = lax.broadcasted_iota(jnp.int32, (8, TILE), 0)
    later_part, cross_part, dot = [
        jnp.sum(jnp.where(lanes() == load + 8 * k, totals, 0.0), axis=1, keepdims=True)
        for k in range(3)
    ]
    ratio = dot / previous
    final = 2.0 * (later_part + ratio * cross_part) + ratio * ratio * curvature
    first, second = previous / curvature, dot / final
    moved = estimate[...] + first * direction[...]
    out[0, 0] = moved + second * (later[...] + ratio * direction[...])


def shards(mesh_shape, operator, rhs_parts, stiffness, traces, coarse_inverse, rigid_loads,
           face_lengths, face_order, mode_count):
    sz = Sizes(mesh_shape, operator, traces, rhs_parts.shape[2])
    vmem = pl.BlockSpec(memory_space=pltpu.VMEM)
    smem = pl.BlockSpec(memory_space=pltpu.SMEM)
    hbm = pl.BlockSpec(memory_space=pltpu.HBM)
    everywhere = ("gx", "gy", "gz")
    small = sz.coarse_pad <= 256

    def call(kernel, out_shape, in_specs, scratch, *operands, limit=None, cost=None):
        return pl.pallas_call(
            functools.partial(kernel, sz),
            out_shape=out_shape,
            in_specs=in_specs,
            out_specs=jax.tree.map(lambda _: vmem, out_shape),
            scratch_shapes=scratch,
            cost_estimate=cost,
            compiler_params=pltpu.CompilerParams(
                vmem_limit_bytes=(limit or (16 if small else 56)) * MIB
            ),
        )(*operands)

    faces = sz.own_faces
    pieces = sz.rows // PIECE
    coarse = pltpu.VMEM((8, sz.coarse_pad), jnp.float32)
    square = pltpu.VMEM((sz.coarse_pad, sz.coarse_pad), jnp.float32)
    half, full, face = f32(8, sz.rows), f32(8, sz.order), f32(8, sz.cap)
    blocks = operator.reshape(sz.rows // 8, 8, sz.order)
    one_step = sz.devices <= 64
    spread_tile = f32(sz.devices if one_step else 1, 8, TILE)
    apply_scratch = [
        pltpu.VMEM((sz.rows // 8, 8, sz.order), jnp.bfloat16),
        pltpu.VMEM((8, sz.rows), jnp.float32),
        pltpu.VMEM((8, sz.order), jnp.bfloat16),
        pltpu.SemaphoreType.DMA((pieces,)),
    ]
    large = 50 if small else 56

    def swap(own):
        return [lax.ppermute(own[j], everywhere, face_pairs(sz, j)) for j in range(faces)]

    def share(chunk, axes):
        if chunk.shape[0] == 1:
            return lax.all_gather(chunk, axes, axis=0, tiled=True)
        return lax.all_to_all(chunk, axes, split_axis=0, concat_axis=0, tiled=True)

    def rest(part):
        if sz.gz == 2:
            return lax.ppermute(part, "gz", [(0, 1), (1, 0)])
        return lax.all_gather(part, "gz", axis=0, tiled=False)

    def assemble(own):
        part = call(
            assemble_kernel, half, [vmem] * (1 + 2 * faces), [], modes, *own, *swap(own)
        )
        return part, rest(part)

    *own, pay, base = call(
        start_kernel,
        [face] * faces + [f32(sz.subs if one_step else 1, 8, sz.coarse_pad), f32(24, sz.rows)],
        [hbm] * 8,
        [
            pltpu.VMEM((sz.modes, 1, sz.rows), jnp.float32),
            pltpu.VMEM((sz.modes, 1, sz.loads), jnp.float32),
            pltpu.VMEM((sz.modes, 1, sz.subs * sz.modes), jnp.float32),
            pltpu.VMEM((1, sz.rows), jnp.float32),
            pltpu.VMEM((4, sz.cap), jnp.int32),
            pltpu.SMEM((1, 1, 4), jnp.int32),
            pltpu.SMEM((1, 1), jnp.int32),
            pltpu.SemaphoreType.DMA((8,)),
        ],
        traces.reshape(sz.modes, 1, sz.order), rigid_loads.reshape(sz.modes, 1, sz.loads),
        coarse_inverse.reshape(sz.modes, 1, -1), stiffness, face_order, rhs_parts,
        face_lengths, mode_count, limit=60,
    )
    shared = share(pay, ("gx", "gy"))
    modes, right = call(
        modes_kernel, [f32(16, sz.rows), half], [vmem] * (1 + faces), [], base, *swap(own)
    )
    modes_rest = rest(modes)
    *own, pay, estimate = call(
        first_kernel, [face] * faces + [spread_tile, full], [hbm] + [vmem] * 4,
        [square, coarse] + apply_scratch,
        blocks, shared, right, modes, modes_rest, limit=large,
    )
    before = share(pay, everywhere)
    gap, gap_rest = assemble(own)
    *own, pay, residual, direction = call(
        second_kernel, [face] * faces + [spread_tile, full, full], [hbm] + [vmem] * 6,
        [square, square, coarse, coarse] + apply_scratch,
        blocks, before, shared, modes, modes_rest, gap, gap_rest, limit=large,
    )
    after = share(pay, everywhere)
    image, image_rest = assemble(own)
    pay, later, scalars = call(
        third_kernel,
        [f32(sz.devices if one_step else 1, 1, TILE), full, f32(8, TILE)],
        [hbm] + [vmem] * (9 + faces),
        [square, square, coarse, coarse, pltpu.VMEM((8, sz.order), jnp.float32)] + apply_scratch,
        blocks, after, shared, before, residual, direction, modes, modes_rest,
        image, image_rest, *own, limit=large,
    )
    return call(
        last_kernel, f32(1, 1, 8, sz.order), [vmem] * 5, [],
        share(pay, everywhere), scalars, estimate, direction, later,
    )


def solution(mesh):
    in_specs = (
        P("gx", "gy", "gz", None),
        P("gx", "gy", None, None),
        P("gx", "gy", None),
        P("gx", "gy", None, None),
        P("gx", "gy", None, None),
        P("gx", "gy", None, None),
        P("gx", "gy", None),
        P("gx", "gy", None, None),
        P("gx", "gy"),
    )
    out_specs = P("gx", "gy", None, None)
    mesh_shape = tuple(mesh.shape[axis] for axis in ("gx", "gy", "gz"))
    return jax.shard_map(
        functools.partial(shards, mesh_shape),
        mesh=mesh, in_specs=in_specs, out_specs=out_specs, check_vma=False,
    )
```

```python
import functools

import jax
import jax.numpy as jnp
from jax import lax
from jax.experimental import pallas as pl
from jax.experimental.pallas import tpu as pltpu
from jax.sharding import PartitionSpec as P

ROW_CHUNK = 256
PIECE = 128
LOAD_LANE = 6
TILE = 128
SLOT = 8
MODE_SPAN = 5 * SLOT
SCALARS = 3 * MODE_SPAN
MIB = 1024 * 1024


class Sizes:
    def __init__(self, mesh_shape, operator, traces, loads):
        self.sx, self.sy, self.gz = mesh_shape
        self.rows = operator.shape[2]
        self.order = operator.shape[3]
        self.modes = traces.shape[2]
        self.cap = self.order // 4
        self.loads = loads
        self.subs = self.sx * self.sy
        self.devices = self.subs * self.gz
        self.coarse = self.subs * SLOT
        self.coarse_pad = -(-self.coarse // TILE) * TILE
        self.own_faces = self.rows // self.cap
        assert self.rows % self.cap == 0 and self.cap % TILE == 0
        assert self.modes <= SLOT - 2 and self.loads == 8


def f32(*shape):
    return jax.ShapeDtypeStruct(shape, jnp.float32)


def lanes(shape=(8, TILE)):
    return lax.broadcasted_iota(jnp.int32, shape, 1)


def exact_dot(a, b):
    return jnp.dot(a, b, precision=lax.Precision.HIGHEST, preferred_element_type=jnp.float32)


def clamp(index, count):
    return jnp.minimum(jnp.maximum(index, 0), count - 1)


def neighbour(sz, face):
    gx, gy = lax.axis_index("gx"), lax.axis_index("gy")
    x = gx + jnp.where(face == 0, -1, jnp.where(face == 1, 1, 0))
    y = gy + jnp.where(face == 2, -1, jnp.where(face == 3, 1, 0))
    return clamp(x, sz.sx) * sz.sy + clamp(y, sz.sy)


def grid_neighbour(sz, sub, face):
    x, y = divmod(sub, sz.sy)
    x, y = [(x - 1, y), (x + 1, y), (x, y - 1), (x, y + 1)][face]
    return x * sz.sy + y if 0 <= x < sz.sx and 0 <= y < sz.sy else None


def face_pairs(sz, slot):
    pairs = []
    for sub in range(sz.subs):
        for part in range(sz.gz):
            local = slot
            if sz.own_faces > 1:
                first = part * sz.own_faces + slot // 2 * 2
                index = divmod(sub, sz.sy)[first // 2]
                local = slot ^ 1 ^ index & 1
            face = part * sz.own_faces + local
            other = grid_neighbour(sz, sub, face)
            if other is not None:
                pairs.append((sub * sz.gz + part, other * sz.gz + (face ^ 1) // sz.own_faces))
    return pairs


def by_slot(sz, values):
    if sz.own_faces == 1:
        return values
    result = []
    for j in range(0, sz.own_faces, 2):
        first = lax.axis_index("gz") * sz.own_faces + j
        index = jnp.where(first < 2, lax.axis_index("gx"), lax.axis_index("gy"))
        odd = lax.rem(index, 2) == 1
        low, high = values[j], values[j + 1]
        result += [jnp.where(odd, low, high), jnp.where(odd, high, low)]
    return result


def own_face(sz, j):
    return slice(j * sz.cap, (j + 1) * sz.cap)


def put_slots(sz, outs, values):
    for out, value in zip(outs, by_slot(sz, values)):
        out[...] = value


def get_slots(sz, refs):
    return by_slot(sz, [ref[...] for ref in refs])


def permuted(sz, block, slots):
    count = sz.cap // TILE
    pieces = [block[:, k * TILE : (k + 1) * TILE] for k in range(count)]
    result = []
    for j in range(count):
        index = jnp.broadcast_to(slots[:, j * TILE : (j + 1) * TILE], (8, TILE)).astype(jnp.int32)
        low = index & (TILE - 1)
        high = index >> (TILE.bit_length() - 1)
        total = jnp.zeros((8, TILE), jnp.float32)
        for k in range(count):
            picked = jnp.take_along_axis(pieces[k], low, axis=1, mode="promise_in_bounds")
            total = jnp.where(high == k, picked, total)
        result.append(total)
    return jnp.concatenate(result, axis=1)


def coefficients(sz, coarse_ref, sub):
    start = sub * SLOT
    base = pl.multiple_of((start // TILE) * TILE, TILE)
    tile = coarse_ref[:, pl.ds(base, TILE)]
    return pltpu.roll(tile, lax.rem(TILE - lax.rem(start, TILE), TILE), 1)


def views(sz, own, rest):
    if sz.gz == 2:
        gz = lax.axis_index("gz")
        return [(gz, own), (1 - gz, rest)]
    return [(z, rest.at[z]) for z in range(sz.gz)]


def mode_sum(sz, coarse_ref, mine, modes_ref, part, j):
    other = coefficients(sz, coarse_ref, neighbour(sz, part * sz.own_faces + j))
    total = None
    for tile, base in ((mine, 0), (other, SLOT)):
        for m in range(sz.modes):
            term = tile[:, m : m + 1] * modes_ref[base + m : base + m + 1, own_face(sz, j)]
            total = term if total is None else total + term
    return total


def own_coefficients(sz, coarse_ref):
    return coefficients(sz, coarse_ref, lax.axis_index("gx") * sz.sy + lax.axis_index("gy"))


def face_slots(sz, part, j):
    return pl.ds(pl.multiple_of(part * sz.rows + j * sz.cap, TILE), sz.cap)


def mode_products(sz, tile, blocks, modes_ref, first_lane):
    lane = lanes()
    gz = lax.axis_index("gz")
    for m in range(sz.modes):
        total = None
        for j, block in enumerate(blocks):
            term = jnp.sum(block * modes_ref[m : m + 1, own_face(sz, j)], axis=1, keepdims=True)
            total = term if total is None else total + term
        tile = jnp.where(lane == first_lane + m, total, tile)
    for j, block in enumerate(blocks):
        face_lane = first_lane + SLOT * (1 + gz * sz.own_faces + j)
        for m in range(sz.modes):
            row = modes_ref[SLOT + m : SLOT + m + 1, own_face(sz, j)]
            total = jnp.sum(block * row, axis=1, keepdims=True)
            tile = jnp.where(lane == face_lane + m, total, tile)
    return tile


def weights_of(sz, modes_ref):
    return [modes_ref[6:7, own_face(sz, j)] for j in range(sz.own_faces)]


def sub_tile(sz, tiles, sub):
    total = tiles[sub * sz.gz]
    for part in range(1, sz.gz):
        total = total + tiles[sub * sz.gz + part]
    return total


def gathered_coarse(sz, tiles, held_ref, group):
    lane = lanes()
    held_ref[...] = jnp.zeros((8, sz.coarse_pad), jnp.float32)
    for sub in range(sz.subs):
        total = tiles[sub]
        for face in range(4):
            other = grid_neighbour(sz, sub, face)
            if other is not None:
                total = total + pltpu.roll(tiles[other], TILE - SLOT * (1 + (face ^ 1)), 1)
        start = sub * SLOT
        base, offset = start // TILE * TILE, start % TILE
        moved = pltpu.roll(total, (offset - group * MODE_SPAN) % TILE, 1)
        moved = jnp.where((lane >= offset) & (lane < offset + sz.modes), moved, 0.0)
        held_ref[:, base : base + TILE] += moved


def fill_coupling(sz, tiles, coupling_ref):
    lane = lanes()
    coupling_ref[...] = jnp.zeros((sz.coarse_pad, sz.coarse_pad), jnp.float32)
    for sub in range(sz.subs):
        for k in range(5):
            other = sub if k == 0 else grid_neighbour(sz, sub, k - 1)
            if other is None:
                continue
            base, offset = other * SLOT // TILE * TILE, other * SLOT % TILE
            moved = pltpu.roll(tiles[sub], (offset - 2 * MODE_SPAN - SLOT * k) % TILE, 1)
            moved = jnp.where((lane >= offset) & (lane < offset + sz.modes), moved, 0.0)
            coupling_ref[sub * SLOT : (sub + 1) * SLOT, base : base + TILE] += moved


def fill_inverse(sz, shared, inverse_ref):
    if sz.coarse_pad > sz.coarse:
        inverse_ref[sz.coarse :, :] = jnp.zeros((sz.coarse_pad - sz.coarse, sz.coarse_pad), jnp.float32)
    for sub in range(sz.subs):
        inverse_ref[sub * SLOT : (sub + 1) * SLOT, :] = shared[sub]


def solve_pair(sz, tiles, inverse_ref, coupling_ref, coarse_a, coarse_b):
    gathered_coarse(sz, tiles, coarse_a, 0)
    gathered_coarse(sz, tiles, coarse_b, 1)
    first = exact_dot(coarse_a[...], inverse_ref[...])
    coarse_a[...] = first
    coarse_b[...] = exact_dot(coarse_b[...] - exact_dot(first, coupling_ref[...]), inverse_ref[...])


def spread(out, tile):
    out[...] = jnp.broadcast_to(tile[None], out.shape)


class Stream:
    def __init__(self, sz, operator, held, product, sems):
        self.sz, self.operator, self.held, self.product, self.sems = sz, operator, held, product, sems
        for p in range(sz.rows // PIECE):
            self.copy(p).start()

    def copy(self, p):
        here = pl.ds(p * (PIECE // 8), PIECE // 8)
        return pltpu.make_async_copy(self.operator.at[here], self.held.at[here], self.sems.at[p])

    def apply(self, vector):
        sz, step, blocks = self.sz, ROW_CHUNK // PIECE, ROW_CHUNK // 8

        def chunk(k, carry):
            for p in range(step):
                self.copy(k * step + p).wait()
            rows = self.held[pl.ds(k * blocks, blocks)].reshape(ROW_CHUNK, sz.order)
            part = lax.dot_general(
                vector[...], rows, (((1,), (1,)), ((), ())), preferred_element_type=jnp.float32
            )
            here = pl.ds(pl.multiple_of(k * ROW_CHUNK, TILE), ROW_CHUNK)
            self.product[:, here] = part.astype(jnp.bfloat16).astype(jnp.float32)
            return carry

        lax.fori_loop(0, sz.rows // ROW_CHUNK, chunk, 0)
        return [self.product[:, own_face(sz, j)] for j in range(sz.own_faces)]


def start_kernel(sz, traces, loads, inverse, stiffness, orders, rhs, lengths, count, *refs):
    outs, scratch = refs[: sz.own_faces + 2], refs[sz.own_faces + 2 :]
    faces, (pay, base) = outs[: sz.own_faces], outs[sz.own_faces :]
    traces_in, loads_in, inverse_in, stiffness_in, slots, lengths_in, count_in, sems = scratch
    gz = lax.axis_index("gz")
    here = pl.ds(pl.multiple_of(gz * sz.rows, TILE), sz.rows)
    copies = [
        pltpu.make_async_copy(inverse, inverse_in, sems.at[0]),
        pltpu.make_async_copy(loads, loads_in, sems.at[1]),
        pltpu.make_async_copy(traces.at[:, :, here], traces_in, sems.at[2]),
        pltpu.make_async_copy(stiffness.at[0, :, here], stiffness_in, sems.at[3]),
        pltpu.make_async_copy(orders.at[0, 0], slots, sems.at[4]),
        pltpu.make_async_copy(rhs.at[0, 0, :, here], base.at[pl.ds(8, 8), :], sems.at[5]),
        pltpu.make_async_copy(lengths, lengths_in, sems.at[6]),
        pltpu.make_async_copy(count, count_in, sems.at[7]),
    ]
    for copy in copies:
        copy.start()
    pay[...] = jnp.zeros(pay.shape, jnp.float32)
    base[sz.modes : 8, :] = jnp.zeros((8 - sz.modes, sz.rows), jnp.float32)
    for copy in copies:
        copy.wait()
    for m in range(sz.modes):
        mask = (m < count_in[0, 0]).astype(jnp.float32)
        for t in range(sz.subs):
            pay[0, m : m + 1, t * SLOT : t * SLOT + sz.modes] = inverse_in[
                m, :, t * sz.modes : (t + 1) * sz.modes
            ]
        loads_row = loads_in[m] * mask
        row = pay[0, m : m + 1, 0:TILE]
        for load in range(sz.loads):
            row = jnp.where(lanes((1, TILE)) == SLOT * load + LOAD_LANE, loads_row[:, load : load + 1], row)
        pay[0, m : m + 1, 0:TILE] = row
        base[m : m + 1, :] = traces_in[m] * mask
    position = lax.broadcasted_iota(jnp.int32, (1, sz.cap), 1)
    base[6:7, :] = stiffness_in[...]
    for j in range(sz.own_faces):
        index = gz * sz.own_faces + j
        base[7:8, own_face(sz, j)] = (position < lengths_in[0, 0, index]).astype(jnp.float32)
        chosen = jnp.broadcast_to(slots[pl.ds(index, 1), :], (8, sz.cap))
        base[16:24, own_face(sz, j)] = chosen.astype(jnp.float32)
    put_slots(sz, faces, [base[0:8, own_face(sz, j)] for j in range(sz.own_faces)])
    chunk = pay[0]
    for k in range(1, pay.shape[0]):
        pay[k] = chunk


def modes_kernel(sz, base, *refs):
    arrived, (modes_ref, right, coupling) = refs[: sz.own_faces], refs[sz.own_faces :]
    right[...] = base[8:16, :]
    row = lax.broadcasted_iota(jnp.int32, (8, 1), 0)
    arrived = get_slots(sz, arrived)
    for j in range(sz.own_faces):
        here = own_face(sz, j)
        other = permuted(sz, arrived[j], base[16:24, here])
        mine = base[0:8, here]
        live = mine[7:8, :]
        total = live * (mine[6:7, :] + other[6:7, :])
        weight = live / (total + 1.0 - live)
        modes_ref[0:8, here] = jnp.where(row == 6, weight, jnp.where(row == 7, live, mine * live))
        slots_row = jnp.where(row == 6, base[16:24, here], 0.0)
        modes_ref[8:16, here] = jnp.where(row < sz.modes, other * live, slots_row)
    weights = weights_of(sz, modes_ref)
    coarse_rows = [
        jnp.where(row < sz.modes, modes_ref[0:8, own_face(sz, j)] * weights[j], 0.0)
        for j in range(sz.own_faces)
    ]
    tile = jnp.zeros((8, TILE), jnp.float32)
    coupling[...] = mode_products(sz, tile, coarse_rows, modes_ref, 2 * MODE_SPAN)


def assemble(sz, modes_ref, refs):
    own, arrived = get_slots(sz, refs[: sz.own_faces]), get_slots(sz, refs[sz.own_faces : -1])
    for j in range(sz.own_faces):
        here = own_face(sz, j)
        other = permuted(sz, arrived[j], modes_ref[14:15, here])
        refs[-1][:, here] = modes_ref[7:8, here] * (own[j] + other)
    return own


def first_tile_kernel(sz, modes_ref, coupling, *refs):
    vectors, pay = assemble(sz, modes_ref, refs[:-1]), refs[-1]
    tile = mode_products(sz, coupling[...], vectors, modes_ref, 0)
    scaled = [v * w for v, w in zip(vectors, weights_of(sz, modes_ref))]
    spread(pay, mode_products(sz, tile, scaled, modes_ref, MODE_SPAN))


def second_tile_kernel(sz, modes_ref, residual_ref, direction_ref, *refs):
    pieces, pay = assemble(sz, modes_ref, refs[:-1]), refs[-1]
    weights = weights_of(sz, modes_ref)
    gz = lax.axis_index("gz")
    lane = lanes()
    curvature = jnp.zeros((8, 1), jnp.float32)
    resid_dot = jnp.zeros((8, 1), jnp.float32)
    for j, piece in enumerate(pieces):
        own = residual_ref[:, face_slots(sz, gz, j)]
        resid_dot += jnp.sum(own * (weights[j] * own), axis=1, keepdims=True)
        direction = direction_ref[:, face_slots(sz, gz, j)]
        curvature += jnp.sum(direction * piece, axis=1, keepdims=True)
    tile = jnp.where(lane == SCALARS, curvature, jnp.zeros((8, TILE), jnp.float32))
    tile = jnp.where(lane == SCALARS + 1, resid_dot, tile)
    tile = mode_products(sz, tile, pieces, modes_ref, 0)
    scaled = [v * w for v, w in zip(pieces, weights)]
    spread(pay, mode_products(sz, tile, scaled, modes_ref, MODE_SPAN))


def first_kernel(sz, operator, shared, right, modes_ref, modes_rest, *refs):
    outs, refs = refs[: sz.own_faces], refs[sz.own_faces :]
    estimate_ref, inverse_ref, coarse_ref, held, product, vector, sems = refs
    stream = Stream(sz, operator, held, product, sems)
    fill_inverse(sz, shared, inverse_ref)
    turned = []
    for k in range(sz.coarse_pad // TILE):
        block = jnp.transpose(inverse_ref[k * TILE : (k + 1) * TILE, 0:TILE])
        rows = [SLOT * load + LOAD_LANE for load in range(sz.loads)]
        turned.append(jnp.concatenate([block[r : r + 1] for r in rows], axis=0))
    coarse_ref[...] = exact_dot(jnp.concatenate(turned, axis=1), inverse_ref[...])
    mine = own_coefficients(sz, coarse_ref)
    for part, modes in views(sz, modes_ref, modes_rest):
        for j in range(sz.own_faces):
            here = face_slots(sz, part, j)
            estimate = mode_sum(sz, coarse_ref, mine, modes, part, j)
            estimate_ref[:, here] = estimate
            vector[:, here] = estimate.astype(jnp.bfloat16)
    pieces = stream.apply(vector)
    put_slots(sz, outs, [right[:, own_face(sz, j)] - piece for j, piece in enumerate(pieces)])


def second_kernel(sz, operator, pieces, shared, modes_ref, modes_rest, gap, gap_rest, *refs):
    outs, refs = refs[: sz.own_faces], refs[sz.own_faces :]
    residual_ref, direction_ref, inverse_ref, coupling_ref, *refs = refs
    coarse_a, coarse_b, held, product, vector, sems = refs
    stream = Stream(sz, operator, held, product, sems)
    fill_inverse(sz, shared, inverse_ref)
    tiles = [sub_tile(sz, pieces, sub) for sub in range(sz.subs)]
    fill_coupling(sz, tiles, coupling_ref)
    solve_pair(sz, tiles, inverse_ref, coupling_ref, coarse_a, coarse_b)
    first, second = own_coefficients(sz, coarse_a), own_coefficients(sz, coarse_b)
    both = zip(views(sz, gap, gap_rest), views(sz, modes_ref, modes_rest))
    for (part, vector_part), (_, modes) in both:
        for j in range(sz.own_faces):
            here = face_slots(sz, part, j)
            residual = vector_part[:, own_face(sz, j)] - mode_sum(sz, coarse_a, first, modes, part, j)
            weight = modes[6:7, own_face(sz, j)]
            direction = weight * residual - mode_sum(sz, coarse_b, second, modes, part, j)
            residual_ref[:, here] = residual
            direction_ref[:, here] = direction
            vector[:, here] = direction.astype(jnp.bfloat16)
    put_slots(sz, outs, stream.apply(vector))


def third_kernel(
    sz, operator, pieces, shared, before, residual_ref, direction_ref,
    modes_ref, modes_rest, image, image_rest, *refs,
):
    earlier, refs = get_slots(sz, refs[: sz.own_faces]), refs[sz.own_faces :]
    pay, later_ref, scalars_ref = refs[:3]
    inverse_ref, coupling_ref, coarse_a, coarse_b, dots, held, product, vector, sems = refs[3:]
    stream = Stream(sz, operator, held, product, sems)
    lane = lanes()
    fill_inverse(sz, shared, inverse_ref)
    fill_coupling(sz, [sub_tile(sz, before, sub) for sub in range(sz.subs)], coupling_ref)
    tiles = [sub_tile(sz, pieces, sub) for sub in range(sz.subs)]
    totals = tiles[0]
    for tile in tiles[1:]:
        totals = totals + tile
    curvature = 2.0 * totals[:, SCALARS : SCALARS + 1]
    resid_dot = totals[:, SCALARS + 1 : SCALARS + 2]
    step = resid_dot / curvature
    scalars_ref[...] = jnp.where(lane == 0, curvature, resid_dot)
    solve_pair(sz, tiles, inverse_ref, coupling_ref, coarse_a, coarse_b)
    first, second = own_coefficients(sz, coarse_a), own_coefficients(sz, coarse_b)
    both = zip(views(sz, image, image_rest), views(sz, modes_ref, modes_rest))
    for (part, vector_part), (_, modes) in both:
        for j in range(sz.own_faces):
            here = face_slots(sz, part, j)
            corrected = vector_part[:, own_face(sz, j)] - mode_sum(sz, coarse_a, first, modes, part, j)
            weight = modes[6:7, own_face(sz, j)]
            scaled = weight * corrected - mode_sum(sz, coarse_b, second, modes, part, j)
            residual = residual_ref[:, here] - step * corrected
            dots[:, here] = residual * (weight * residual)
            later = direction_ref[:, here] - step * scaled
            later_ref[:, here] = later
            vector[:, here] = later.astype(jnp.bfloat16)
    gz = lax.axis_index("gz")
    dot_part = jnp.zeros((8, 1), jnp.float32)
    for j in range(sz.own_faces):
        dot_part += jnp.sum(dots[:, face_slots(sz, gz, j)], axis=1, keepdims=True)
    pieces = stream.apply(vector)
    later_part = jnp.zeros((8, 1), jnp.float32)
    cross_part = jnp.zeros((8, 1), jnp.float32)
    for j, piece in enumerate(pieces):
        mine = later_ref[:, face_slots(sz, gz, j)]
        direction = direction_ref[:, face_slots(sz, gz, j)]
        later_part += jnp.sum(mine * piece, axis=1, keepdims=True)
        cross_part += jnp.sum(mine * earlier[j] + direction * piece, axis=1, keepdims=True)
    load = lax.broadcasted_iota(jnp.int32, (8, TILE), 0)
    line = jnp.where(lane == load, later_part, 0.0)
    line = jnp.where(lane == load + 8, cross_part, line)
    line = jnp.where(lane == load + 16, dot_part, line)
    spread(pay, jnp.sum(line, axis=0, keepdims=True))


def last_kernel(sz, pieces, scalars, estimate, direction, later, out):
    totals = pieces[0]
    for k in range(1, pieces.shape[0]):
        totals = totals + pieces[k]
    curvature, previous = scalars[:, 0:1], scalars[:, 1:2]
    load = lax.broadcasted_iota(jnp.int32, (8, TILE), 0)
    later_part, cross_part, dot = [
        jnp.sum(jnp.where(lanes() == load + 8 * k, totals, 0.0), axis=1, keepdims=True)
        for k in range(3)
    ]
    ratio = dot / previous
    final = 2.0 * (later_part + ratio * cross_part) + ratio * ratio * curvature
    first, second = previous / curvature, dot / final
    moved = estimate[...] + first * direction[...]
    out[0, 0] = moved + second * (later[...] + ratio * direction[...])


def shards(mesh_shape, operator, rhs_parts, stiffness, traces, coarse_inverse, rigid_loads,
           face_lengths, face_order, mode_count):
    sz = Sizes(mesh_shape, operator, traces, rhs_parts.shape[2])
    vmem = pl.BlockSpec(memory_space=pltpu.VMEM)
    smem = pl.BlockSpec(memory_space=pltpu.SMEM)
    hbm = pl.BlockSpec(memory_space=pltpu.HBM)
    everywhere = ("gx", "gy", "gz")
    small = sz.coarse_pad <= 256

    def call(kernel, out_shape, in_specs, scratch, *operands, limit=None, cost=None):
        return pl.pallas_call(
            functools.partial(kernel, sz),
            out_shape=out_shape,
            in_specs=in_specs,
            out_specs=jax.tree.map(lambda _: vmem, out_shape),
            scratch_shapes=scratch,
            cost_estimate=cost,
            compiler_params=pltpu.CompilerParams(
                vmem_limit_bytes=(limit or (16 if small else 56)) * MIB
            ),
        )(*operands)

    faces = sz.own_faces
    pieces = sz.rows // PIECE
    coarse = pltpu.VMEM((8, sz.coarse_pad), jnp.float32)
    square = pltpu.VMEM((sz.coarse_pad, sz.coarse_pad), jnp.float32)
    half, full, face = f32(8, sz.rows), f32(8, sz.order), f32(8, sz.cap)
    blocks = operator.reshape(sz.rows // 8, 8, sz.order)
    one_step = sz.devices <= 64
    spread_tile = f32(sz.devices if one_step else 1, 8, TILE)
    apply_scratch = [
        pltpu.VMEM((sz.rows // 8, 8, sz.order), jnp.bfloat16),
        pltpu.VMEM((8, sz.rows), jnp.float32),
        pltpu.VMEM((8, sz.order), jnp.bfloat16),
        pltpu.SemaphoreType.DMA((pieces,)),
    ]
    large = 50 if small else 56

    def swap(own):
        return [lax.ppermute(own[j], everywhere, face_pairs(sz, j)) for j in range(faces)]

    def share(chunk, axes):
        if chunk.shape[0] == 1:
            return lax.all_gather(chunk, axes, axis=0, tiled=True)
        return lax.all_to_all(chunk, axes, split_axis=0, concat_axis=0, tiled=True)

    def rest(part):
        if sz.gz == 2:
            return lax.ppermute(part, "gz", [(0, 1), (1, 0)])
        return lax.all_gather(part, "gz", axis=0, tiled=False)

    def tile(kernel, own, *operands):
        operands = operands + tuple(own) + tuple(swap(own))
        part, pay = call(kernel, [half, spread_tile], [vmem] * len(operands), [], *operands)
        return share(pay, everywhere), part, rest(part)

    *own, pay, base = call(
        start_kernel,
        [face] * faces + [f32(sz.subs if one_step else 1, 8, sz.coarse_pad), f32(24, sz.rows)],
        [hbm] * 8,
        [
            pltpu.VMEM((sz.modes, 1, sz.rows), jnp.float32),
            pltpu.VMEM((sz.modes, 1, sz.loads), jnp.float32),
            pltpu.VMEM((sz.modes, 1, sz.subs * sz.modes), jnp.float32),
            pltpu.VMEM((1, sz.rows), jnp.float32),
            pltpu.VMEM((4, sz.cap), jnp.int32),
            pltpu.SMEM((1, 1, 4), jnp.int32),
            pltpu.SMEM((1, 1), jnp.int32),
            pltpu.SemaphoreType.DMA((8,)),
        ],
        traces.reshape(sz.modes, 1, sz.order), rigid_loads.reshape(sz.modes, 1, sz.loads),
        coarse_inverse.reshape(sz.modes, 1, -1), stiffness, face_order, rhs_parts,
        face_lengths, mode_count, limit=60,
    )
    shared = share(pay, ("gx", "gy"))
    modes, right, coupling = call(
        modes_kernel, [f32(16, sz.rows), half, f32(8, TILE)], [vmem] * (1 + faces), [], base, *swap(own)
    )
    modes_rest = rest(modes)
    *own, estimate = call(
        first_kernel, [face] * faces + [full], [hbm] + [vmem] * 4,
        [square, coarse] + apply_scratch,
        blocks, shared, right, modes, modes_rest, limit=large,
    )
    before, gap, gap_rest = tile(first_tile_kernel, own, modes, coupling)
    *own, residual, direction = call(
        second_kernel, [face] * faces + [full, full], [hbm] + [vmem] * 6,
        [square, square, coarse, coarse] + apply_scratch,
        blocks, before, shared, modes, modes_rest, gap, gap_rest, limit=large,
    )
    after, image, image_rest = tile(second_tile_kernel, own, modes, residual, direction)
    pay, later, scalars = call(
        third_kernel,
        [f32(sz.devices if one_step else 1, 1, TILE), full, f32(8, TILE)],
        [hbm] + [vmem] * (9 + faces),
        [square, square, coarse, coarse, pltpu.VMEM((8, sz.order), jnp.float32)] + apply_scratch,
        blocks, after, shared, before, residual, direction, modes, modes_rest,
        image, image_rest, *own, limit=large,
    )
    return call(
        last_kernel, f32(1, 1, 8, sz.order), [vmem] * 5, [],
        share(pay, everywhere), scalars, estimate, direction, later,
    )


def solution(mesh):
    in_specs = (
        P("gx", "gy", "gz", None),
        P("gx", "gy", None, None),
        P("gx", "gy", None),
        P("gx", "gy", None, None),
        P("gx", "gy", None, None),
        P("gx", "gy", None, None),
        P("gx", "gy", None),
        P("gx", "gy", None, None),
        P("gx", "gy"),
    )
    out_specs = P("gx", "gy", None, None)
    mesh_shape = tuple(mesh.shape[axis] for axis in ("gx", "gy", "gz"))
    return jax.shard_map(
        functools.partial(shards, mesh_shape),
        mesh=mesh, in_specs=in_specs, out_specs=out_specs, check_vma=False,
    )
```

```python
import functools

import jax
import jax.numpy as jnp
from jax import lax
from jax.experimental import pallas as pl
from jax.experimental.pallas import tpu as pltpu
from jax.sharding import PartitionSpec as P

ROW_CHUNK = 256
PIECE = 128
LOAD_LANE = 6
TILE = 128
SLOT = 8
MODE_SPAN = 5 * SLOT
SCALARS = 3 * MODE_SPAN
MIB = 1024 * 1024


class Sizes:
    def __init__(self, mesh_shape, operator, traces, loads):
        self.sx, self.sy, self.gz = mesh_shape
        self.rows = operator.shape[2]
        self.order = operator.shape[3]
        self.modes = traces.shape[2]
        self.cap = self.order // 4
        self.loads = loads
        self.subs = self.sx * self.sy
        self.devices = self.subs * self.gz
        self.coarse = self.subs * SLOT
        self.coarse_pad = -(-self.coarse // TILE) * TILE
        self.own_faces = self.rows // self.cap
        assert self.rows % self.cap == 0 and self.cap % TILE == 0
        assert self.modes <= SLOT - 2 and self.loads == 8


def f32(*shape):
    return jax.ShapeDtypeStruct(shape, jnp.float32)


def lanes(shape=(8, TILE)):
    return lax.broadcasted_iota(jnp.int32, shape, 1)


def exact_dot(a, b):
    return jnp.dot(a, b, precision=lax.Precision.HIGHEST, preferred_element_type=jnp.float32)


def clamp(index, count):
    return jnp.minimum(jnp.maximum(index, 0), count - 1)


def neighbour(sz, face):
    gx, gy = lax.axis_index("gx"), lax.axis_index("gy")
    x = gx + jnp.where(face == 0, -1, jnp.where(face == 1, 1, 0))
    y = gy + jnp.where(face == 2, -1, jnp.where(face == 3, 1, 0))
    return clamp(x, sz.sx) * sz.sy + clamp(y, sz.sy)


def grid_neighbour(sz, sub, face):
    x, y = divmod(sub, sz.sy)
    x, y = [(x - 1, y), (x + 1, y), (x, y - 1), (x, y + 1)][face]
    return x * sz.sy + y if 0 <= x < sz.sx and 0 <= y < sz.sy else None


def face_pairs(sz, slot):
    pairs = []
    for sub in range(sz.subs):
        for part in range(sz.gz):
            local = slot
            if sz.own_faces > 1:
                first = part * sz.own_faces + slot // 2 * 2
                index = divmod(sub, sz.sy)[first // 2]
                local = slot ^ 1 ^ index & 1
            face = part * sz.own_faces + local
            other = grid_neighbour(sz, sub, face)
            if other is not None:
                pairs.append((sub * sz.gz + part, other * sz.gz + (face ^ 1) // sz.own_faces))
    return pairs


def by_slot(sz, values):
    if sz.own_faces == 1:
        return values
    result = []
    for j in range(0, sz.own_faces, 2):
        first = lax.axis_index("gz") * sz.own_faces + j
        index = jnp.where(first < 2, lax.axis_index("gx"), lax.axis_index("gy"))
        odd = lax.rem(index, 2) == 1
        low, high = values[j], values[j + 1]
        result += [jnp.where(odd, low, high), jnp.where(odd, high, low)]
    return result


def own_face(sz, j):
    return slice(j * sz.cap, (j + 1) * sz.cap)


def put_slots(sz, outs, values):
    for out, value in zip(outs, by_slot(sz, values)):
        out[...] = value


def get_slots(sz, refs):
    return by_slot(sz, [ref[...] for ref in refs])


def permuted(sz, block, slots):
    count = sz.cap // TILE
    pieces = [block[:, k * TILE : (k + 1) * TILE] for k in range(count)]
    result = []
    for j in range(count):
        index = jnp.broadcast_to(slots[:, j * TILE : (j + 1) * TILE], (8, TILE)).astype(jnp.int32)
        low = index & (TILE - 1)
        high = index >> (TILE.bit_length() - 1)
        total = jnp.zeros((8, TILE), jnp.float32)
        for k in range(count):
            picked = jnp.take_along_axis(pieces[k], low, axis=1, mode="promise_in_bounds")
            total = jnp.where(high == k, picked, total)
        result.append(total)
    return jnp.concatenate(result, axis=1)


def coefficients(sz, coarse_ref, sub):
    start = sub * SLOT
    base = pl.multiple_of((start // TILE) * TILE, TILE)
    tile = coarse_ref[:, pl.ds(base, TILE)]
    return pltpu.roll(tile, lax.rem(TILE - lax.rem(start, TILE), TILE), 1)


def views(sz, own, rest):
    if sz.gz == 2:
        gz = lax.axis_index("gz")
        return [(gz, own), (1 - gz, rest)]
    return [(z, rest.at[z]) for z in range(sz.gz)]


def mode_sum(sz, coarse_ref, mine, modes_ref, part, j):
    other = coefficients(sz, coarse_ref, neighbour(sz, part * sz.own_faces + j))
    total = None
    for tile, base in ((mine, 0), (other, SLOT)):
        for m in range(sz.modes):
            term = tile[:, m : m + 1] * modes_ref[base + m : base + m + 1, own_face(sz, j)]
            total = term if total is None else total + term
    return total


def own_coefficients(sz, coarse_ref):
    return coefficients(sz, coarse_ref, lax.axis_index("gx") * sz.sy + lax.axis_index("gy"))


def face_slots(sz, part, j):
    return pl.ds(pl.multiple_of(part * sz.rows + j * sz.cap, TILE), sz.cap)


def mode_products(sz, tile, blocks, modes_ref, first_lane):
    lane = lanes()
    gz = lax.axis_index("gz")
    for m in range(sz.modes):
        total = None
        for j, block in enumerate(blocks):
            term = jnp.sum(block * modes_ref[m : m + 1, own_face(sz, j)], axis=1, keepdims=True)
            total = term if total is None else total + term
        tile = jnp.where(lane == first_lane + m, total, tile)
    for j, block in enumerate(blocks):
        face_lane = first_lane + SLOT * (1 + gz * sz.own_faces + j)
        for m in range(sz.modes):
            row = modes_ref[SLOT + m : SLOT + m + 1, own_face(sz, j)]
            total = jnp.sum(block * row, axis=1, keepdims=True)
            tile = jnp.where(lane == face_lane + m, total, tile)
    return tile


def weights_of(sz, modes_ref):
    return [modes_ref[6:7, own_face(sz, j)] for j in range(sz.own_faces)]


def sub_tile(sz, tiles, sub):
    total = tiles[sub * sz.gz]
    for part in range(1, sz.gz):
        total = total + tiles[sub * sz.gz + part]
    return total


def gathered_coarse(sz, tiles, held_ref, group):
    lane = lanes()
    held_ref[...] = jnp.zeros((8, sz.coarse_pad), jnp.float32)
    for sub in range(sz.subs):
        total = tiles[sub]
        for face in range(4):
            other = grid_neighbour(sz, sub, face)
            if other is not None:
                total = total + pltpu.roll(tiles[other], TILE - SLOT * (1 + (face ^ 1)), 1)
        start = sub * SLOT
        base, offset = start // TILE * TILE, start % TILE
        moved = pltpu.roll(total, (offset - group * MODE_SPAN) % TILE, 1)
        moved = jnp.where((lane >= offset) & (lane < offset + sz.modes), moved, 0.0)
        held_ref[:, base : base + TILE] += moved


def fill_coupling(sz, tiles, coupling_ref):
    lane = lanes()
    coupling_ref[...] = jnp.zeros((sz.coarse_pad, sz.coarse_pad), jnp.float32)
    for sub in range(sz.subs):
        for k in range(5):
            other = sub if k == 0 else grid_neighbour(sz, sub, k - 1)
            if other is None:
                continue
            base, offset = other * SLOT // TILE * TILE, other * SLOT % TILE
            moved = pltpu.roll(tiles[sub], (offset - 2 * MODE_SPAN - SLOT * k) % TILE, 1)
            moved = jnp.where((lane >= offset) & (lane < offset + sz.modes), moved, 0.0)
            coupling_ref[sub * SLOT : (sub + 1) * SLOT, base : base + TILE] += moved


def fill_inverse(sz, shared, inverse_ref):
    if sz.coarse_pad > sz.coarse:
        inverse_ref[sz.coarse :, :] = jnp.zeros((sz.coarse_pad - sz.coarse, sz.coarse_pad), jnp.float32)
    for sub in range(sz.subs):
        inverse_ref[sub * SLOT : (sub + 1) * SLOT, :] = shared[sub]


def solve_pair(sz, tiles, inverse_ref, coupling_ref, coarse_a, coarse_b):
    gathered_coarse(sz, tiles, coarse_a, 0)
    gathered_coarse(sz, tiles, coarse_b, 1)
    first = exact_dot(coarse_a[...], inverse_ref[...])
    coarse_a[...] = first
    coarse_b[...] = exact_dot(coarse_b[...] - exact_dot(first, coupling_ref[...]), inverse_ref[...])


def spread(out, tile):
    out[...] = jnp.broadcast_to(tile[None], out.shape)


def front_chunks(sz):
    return sz.rows // ROW_CHUNK * 2 // 3


class Stream:
    def __init__(self, sz, operator, held, product, sems, front=None):
        self.sz, self.operator, self.held, self.product, self.sems = sz, operator, held, product, sems
        self.front, self.first = front, front_chunks(sz) if front is not None else 0
        for p in range((sz.rows // ROW_CHUNK - self.first) * (ROW_CHUNK // PIECE)):
            self.copy(p).start()

    def copy(self, p):
        blocks = PIECE // 8
        source = pl.ds(self.first * (ROW_CHUNK // 8) + p * blocks, blocks)
        target = self.held.at[pl.ds(p * blocks, blocks)]
        return pltpu.make_async_copy(self.operator.at[source], target, self.sems.at[p])

    def multiply(self, vector, rows, k):
        part = lax.dot_general(
            vector[...], rows.reshape(ROW_CHUNK, self.sz.order), (((1,), (1,)), ((), ())),
            preferred_element_type=jnp.float32,
        )
        here = pl.ds(pl.multiple_of(k * ROW_CHUNK, TILE), ROW_CHUNK)
        self.product[:, here] = part.astype(jnp.bfloat16).astype(jnp.float32)

    def apply(self, vector):
        sz, step, blocks = self.sz, ROW_CHUNK // PIECE, ROW_CHUNK // 8
        for k in range(self.first):
            self.multiply(vector, self.front[k * blocks : (k + 1) * blocks], k)

        def chunk(k, carry):
            for p in range(step):
                self.copy(k * step + p).wait()
            self.multiply(vector, self.held[pl.ds(k * blocks, blocks)], self.first + k)
            return carry

        lax.fori_loop(0, sz.rows // ROW_CHUNK - self.first, chunk, 0)
        return [self.product[:, own_face(sz, j)] for j in range(sz.own_faces)]


def hold_kernel(sz, operator, after, front, sems):
    del after
    blocks = ROW_CHUNK // 8
    copies = []
    for k in range(front_chunks(sz)):
        here = pl.ds(k * blocks, blocks)
        copies.append(pltpu.make_async_copy(operator.at[here], front.at[here], sems.at[k]))
        copies[-1].start()
    for copy in copies:
        copy.wait()


def part_slots(sz, part):
    return pl.ds(pl.multiple_of(part * sz.rows, TILE), sz.rows)


def put_parts(sz, own, rest, vector):
    for part, ref in views(sz, own, rest):
        vector[:, part_slots(sz, part)] = ref[...].astype(vector.dtype)


def start_kernel(sz, traces, loads, inverse, stiffness, orders, rhs, lengths, count, *refs):
    outs, scratch = refs[: sz.own_faces + 2], refs[sz.own_faces + 2 :]
    faces, (pay, base) = outs[: sz.own_faces], outs[sz.own_faces :]
    traces_in, loads_in, inverse_in, stiffness_in, slots, lengths_in, count_in, sems = scratch
    gz = lax.axis_index("gz")
    here = pl.ds(pl.multiple_of(gz * sz.rows, TILE), sz.rows)
    copies = [
        pltpu.make_async_copy(inverse, inverse_in, sems.at[0]),
        pltpu.make_async_copy(loads, loads_in, sems.at[1]),
        pltpu.make_async_copy(traces.at[:, :, here], traces_in, sems.at[2]),
        pltpu.make_async_copy(stiffness.at[0, :, here], stiffness_in, sems.at[3]),
        pltpu.make_async_copy(orders.at[0, 0], slots, sems.at[4]),
        pltpu.make_async_copy(rhs.at[0, 0, :, here], base.at[pl.ds(8, 8), :], sems.at[5]),
        pltpu.make_async_copy(lengths, lengths_in, sems.at[6]),
        pltpu.make_async_copy(count, count_in, sems.at[7]),
    ]
    for copy in copies:
        copy.start()
    pay[...] = jnp.zeros(pay.shape, jnp.float32)
    base[sz.modes : 8, :] = jnp.zeros((8 - sz.modes, sz.rows), jnp.float32)
    for copy in copies:
        copy.wait()
    for m in range(sz.modes):
        mask = (m < count_in[0, 0]).astype(jnp.float32)
        for t in range(sz.subs):
            pay[0, m : m + 1, t * SLOT : t * SLOT + sz.modes] = inverse_in[
                m, :, t * sz.modes : (t + 1) * sz.modes
            ]
        loads_row = loads_in[m] * mask
        row = pay[0, m : m + 1, 0:TILE]
        for load in range(sz.loads):
            row = jnp.where(lanes((1, TILE)) == SLOT * load + LOAD_LANE, loads_row[:, load : load + 1], row)
        pay[0, m : m + 1, 0:TILE] = row
        base[m : m + 1, :] = traces_in[m] * mask
    position = lax.broadcasted_iota(jnp.int32, (1, sz.cap), 1)
    base[6:7, :] = stiffness_in[...]
    for j in range(sz.own_faces):
        index = gz * sz.own_faces + j
        base[7:8, own_face(sz, j)] = (position < lengths_in[0, 0, index]).astype(jnp.float32)
        chosen = jnp.broadcast_to(slots[pl.ds(index, 1), :], (8, sz.cap))
        base[16:24, own_face(sz, j)] = chosen.astype(jnp.float32)
    put_slots(sz, faces, [base[0:8, own_face(sz, j)] for j in range(sz.own_faces)])
    chunk = pay[0]
    for k in range(1, pay.shape[0]):
        pay[k] = chunk


def modes_kernel(sz, base, *refs):
    arrived, (modes_ref, right, coupling) = refs[: sz.own_faces], refs[sz.own_faces :]
    right[...] = base[8:16, :]
    row = lax.broadcasted_iota(jnp.int32, (8, 1), 0)
    arrived = get_slots(sz, arrived)
    for j in range(sz.own_faces):
        here = own_face(sz, j)
        other = permuted(sz, arrived[j], base[16:24, here])
        mine = base[0:8, here]
        live = mine[7:8, :]
        total = live * (mine[6:7, :] + other[6:7, :])
        weight = live / (total + 1.0 - live)
        modes_ref[0:8, here] = jnp.where(row == 6, weight, jnp.where(row == 7, live, mine * live))
        slots_row = jnp.where(row == 6, base[16:24, here], 0.0)
        modes_ref[8:16, here] = jnp.where(row < sz.modes, other * live, slots_row)
    weights = weights_of(sz, modes_ref)
    coarse_rows = [
        jnp.where(row < sz.modes, modes_ref[0:8, own_face(sz, j)] * weights[j], 0.0)
        for j in range(sz.own_faces)
    ]
    tile = jnp.zeros((8, TILE), jnp.float32)
    coupling[...] = mode_products(sz, tile, coarse_rows, modes_ref, 2 * MODE_SPAN)


def assembled(sz, own, arrived, modes_ref, j):
    here = own_face(sz, j)
    return modes_ref[7:8, here] * (own[j] + permuted(sz, arrived[j], modes_ref[14:15, here]))


def tile_products(sz, tile, vectors, modes_ref):
    tile = mode_products(sz, tile, vectors, modes_ref, 0)
    scaled = [v * w for v, w in zip(vectors, weights_of(sz, modes_ref))]
    return mode_products(sz, tile, scaled, modes_ref, MODE_SPAN)


def first_kernel(sz, operator, shared, right, coupling, modes_ref, modes_rest, *refs):
    outs, refs = refs[: sz.own_faces], refs[sz.own_faces :]
    pay, estimate_ref, inverse_ref, coarse_ref, held, product, vector, sems = refs
    stream = Stream(sz, operator, held, product, sems)
    fill_inverse(sz, shared, inverse_ref)
    turned = []
    for k in range(sz.coarse_pad // TILE):
        block = jnp.transpose(inverse_ref[k * TILE : (k + 1) * TILE, 0:TILE])
        rows = [SLOT * load + LOAD_LANE for load in range(sz.loads)]
        turned.append(jnp.concatenate([block[r : r + 1] for r in rows], axis=0))
    coarse_ref[...] = exact_dot(jnp.concatenate(turned, axis=1), inverse_ref[...])
    mine = own_coefficients(sz, coarse_ref)
    for part, modes in views(sz, modes_ref, modes_rest):
        for j in range(sz.own_faces):
            here = face_slots(sz, part, j)
            estimate = mode_sum(sz, coarse_ref, mine, modes, part, j)
            estimate_ref[:, here] = estimate
            vector[:, here] = estimate.astype(jnp.bfloat16)
    pieces = stream.apply(vector)
    vectors = [right[:, own_face(sz, j)] - piece for j, piece in enumerate(pieces)]
    put_slots(sz, outs, vectors)
    spread(pay, tile_products(sz, coupling[...], vectors, modes_ref))


def second_kernel(sz, pieces, shared, modes_ref, *refs):
    own, refs = get_slots(sz, refs[: sz.own_faces]), refs[sz.own_faces :]
    arrived, refs = get_slots(sz, refs[: sz.own_faces]), refs[sz.own_faces :]
    residual_ref, direction_ref, inverse_ref, coupling_ref, coarse_a, coarse_b = refs
    gz = lax.axis_index("gz")
    fill_inverse(sz, shared, inverse_ref)
    tiles = [sub_tile(sz, pieces, sub) for sub in range(sz.subs)]
    fill_coupling(sz, tiles, coupling_ref)
    solve_pair(sz, tiles, inverse_ref, coupling_ref, coarse_a, coarse_b)
    first, second = own_coefficients(sz, coarse_a), own_coefficients(sz, coarse_b)
    for j in range(sz.own_faces):
        here = own_face(sz, j)
        gap = assembled(sz, own, arrived, modes_ref, j)
        residual = gap - mode_sum(sz, coarse_a, first, modes_ref, gz, j)
        residual_ref[:, here] = residual
        correction = mode_sum(sz, coarse_b, second, modes_ref, gz, j)
        direction_ref[:, here] = modes_ref[6:7, here] * residual - correction


def second_apply_kernel(sz, operator, front, modes_ref, residual, direction, rest, *refs):
    outs, refs = refs[: sz.own_faces], refs[sz.own_faces :]
    pay, held, product, vector, sems = refs
    stream = Stream(sz, operator, held, product, sems, front)
    put_parts(sz, direction, rest, vector)
    weights = weights_of(sz, modes_ref)
    lane = lanes()
    curvature = jnp.zeros((8, 1), jnp.float32)
    resid_dot = jnp.zeros((8, 1), jnp.float32)
    pieces = stream.apply(vector)
    put_slots(sz, outs, pieces)
    for j, piece in enumerate(pieces):
        here = own_face(sz, j)
        own = residual[:, here]
        resid_dot += jnp.sum(own * (weights[j] * own), axis=1, keepdims=True)
        curvature += jnp.sum(direction[:, here] * piece, axis=1, keepdims=True)
    tile = jnp.where(lane == SCALARS, curvature, jnp.zeros((8, TILE), jnp.float32))
    tile = jnp.where(lane == SCALARS + 1, resid_dot, tile)
    spread(pay, tile_products(sz, tile, pieces, modes_ref))


def third_kernel(sz, pieces, shared, before, modes_ref, residual_ref, direction_ref, *refs):
    own, refs = get_slots(sz, refs[: sz.own_faces]), refs[sz.own_faces :]
    arrived, refs = get_slots(sz, refs[: sz.own_faces]), refs[sz.own_faces :]
    later_ref, scalars_ref, inverse_ref, coupling_ref, coarse_a, coarse_b = refs
    gz = lax.axis_index("gz")
    lane = lanes()
    fill_inverse(sz, shared, inverse_ref)
    fill_coupling(sz, [sub_tile(sz, before, sub) for sub in range(sz.subs)], coupling_ref)
    tiles = [sub_tile(sz, pieces, sub) for sub in range(sz.subs)]
    totals = tiles[0]
    for tile in tiles[1:]:
        totals = totals + tile
    curvature = 2.0 * totals[:, SCALARS : SCALARS + 1]
    resid_dot = totals[:, SCALARS + 1 : SCALARS + 2]
    step = resid_dot / curvature
    solve_pair(sz, tiles, inverse_ref, coupling_ref, coarse_a, coarse_b)
    first, second = own_coefficients(sz, coarse_a), own_coefficients(sz, coarse_b)
    dot_part = jnp.zeros((8, 1), jnp.float32)
    for j in range(sz.own_faces):
        here = own_face(sz, j)
        image = assembled(sz, own, arrived, modes_ref, j)
        corrected = image - mode_sum(sz, coarse_a, first, modes_ref, gz, j)
        weight = modes_ref[6:7, here]
        scaled = weight * corrected - mode_sum(sz, coarse_b, second, modes_ref, gz, j)
        residual = residual_ref[:, here] - step * corrected
        dot_part += jnp.sum(residual * (weight * residual), axis=1, keepdims=True)
        later_ref[:, here] = direction_ref[:, here] - step * scaled
    scalars_ref[...] = jnp.where(lane == 0, curvature, jnp.where(lane == 1, resid_dot, dot_part))


def third_apply_kernel(sz, operator, front, direction, scalars, later, rest, *refs):
    before, refs = get_slots(sz, refs[: sz.own_faces]), refs[sz.own_faces :]
    pay, held, product, vector, sems = refs
    stream = Stream(sz, operator, held, product, sems, front)
    put_parts(sz, later, rest, vector)
    pieces = stream.apply(vector)
    lane = lanes()
    later_part = jnp.zeros((8, 1), jnp.float32)
    cross_part = jnp.zeros((8, 1), jnp.float32)
    for j, piece in enumerate(pieces):
        mine = later[:, own_face(sz, j)]
        earlier = direction[:, own_face(sz, j)]
        later_part += jnp.sum(mine * piece, axis=1, keepdims=True)
        cross_part += jnp.sum(mine * before[j] + earlier * piece, axis=1, keepdims=True)
    load = lax.broadcasted_iota(jnp.int32, (8, TILE), 0)
    line = jnp.where(lane == load, later_part, 0.0)
    line = jnp.where(lane == load + 8, cross_part, line)
    line = jnp.where(lane == load + 16, scalars[:, 2:3], line)
    spread(pay, jnp.sum(line, axis=0, keepdims=True))


def last_kernel(sz, pieces, scalars, estimate, direction, direction_rest, later, later_rest, out):
    totals = pieces[0]
    for k in range(1, pieces.shape[0]):
        totals = totals + pieces[k]
    curvature, previous = scalars[:, 0:1], scalars[:, 1:2]
    load = lax.broadcasted_iota(jnp.int32, (8, TILE), 0)
    later_part, cross_part, dot = [
        jnp.sum(jnp.where(lanes() == load + 8 * k, totals, 0.0), axis=1, keepdims=True)
        for k in range(3)
    ]
    ratio = dot / previous
    final = 2.0 * (later_part + ratio * cross_part) + ratio * ratio * curvature
    first, second = previous / curvature, dot / final
    both = zip(views(sz, direction, direction_rest), views(sz, later, later_rest))
    for (part, earlier), (_, mine) in both:
        here = part_slots(sz, part)
        moved = estimate[:, here] + first * earlier[...]
        out[0, 0, :, here] = moved + second * (mine[...] + ratio * earlier[...])


def shards(mesh_shape, operator, rhs_parts, stiffness, traces, coarse_inverse, rigid_loads,
           face_lengths, face_order, mode_count):
    sz = Sizes(mesh_shape, operator, traces, rhs_parts.shape[2])
    vmem = pl.BlockSpec(memory_space=pltpu.VMEM)
    smem = pl.BlockSpec(memory_space=pltpu.SMEM)
    hbm = pl.BlockSpec(memory_space=pltpu.HBM)
    everywhere = ("gx", "gy", "gz")
    small = sz.coarse_pad <= 256

    def call(kernel, out_shape, in_specs, scratch, *operands, limit=None, cost=None):
        return pl.pallas_call(
            functools.partial(kernel, sz),
            out_shape=out_shape,
            in_specs=in_specs,
            out_specs=jax.tree.map(lambda _: vmem, out_shape),
            scratch_shapes=scratch,
            cost_estimate=cost,
            compiler_params=pltpu.CompilerParams(
                vmem_limit_bytes=(limit or (16 if small else 56)) * MIB
            ),
        )(*operands)

    faces = sz.own_faces
    coarse = pltpu.VMEM((8, sz.coarse_pad), jnp.float32)
    square = pltpu.VMEM((sz.coarse_pad, sz.coarse_pad), jnp.float32)
    half, full, face = f32(8, sz.rows), f32(8, sz.order), f32(8, sz.cap)
    blocks = operator.reshape(sz.rows // 8, 8, sz.order)
    one_step = sz.devices <= 64
    spread_tile = f32(sz.devices if one_step else 1, 8, TILE)
    front_rows = front_chunks(sz) * ROW_CHUNK

    def apply_scratch(rows):
        return [
            pltpu.VMEM((rows // 8, 8, sz.order), jnp.bfloat16),
            pltpu.VMEM((8, sz.rows), jnp.float32),
            pltpu.VMEM((8, sz.order), jnp.bfloat16),
            pltpu.SemaphoreType.DMA((rows // PIECE,)),
        ]

    def hold(after):
        return call(
            hold_kernel, jax.ShapeDtypeStruct((front_rows // 8, 8, sz.order), jnp.bfloat16),
            [hbm, vmem], [pltpu.SemaphoreType.DMA((front_chunks(sz),))], blocks, after, limit=42,
            cost=pl.CostEstimate(flops=0, bytes_accessed=4 * sz.rows * sz.order, transcendentals=0),
        )

    def swap(own):
        return [lax.ppermute(own[j], everywhere, face_pairs(sz, j)) for j in range(faces)]

    def share(chunk, axes):
        if chunk.shape[0] == 1:
            return lax.all_gather(chunk, axes, axis=0, tiled=True)
        return lax.all_to_all(chunk, axes, split_axis=0, concat_axis=0, tiled=True)

    def rest(part):
        if sz.gz == 2:
            return lax.ppermute(part, "gz", [(0, 1), (1, 0)])
        return lax.all_gather(part, "gz", axis=0, tiled=False)

    *own, pay, base = call(
        start_kernel,
        [face] * faces + [f32(sz.subs if one_step else 1, 8, sz.coarse_pad), f32(24, sz.rows)],
        [hbm] * 8,
        [
            pltpu.VMEM((sz.modes, 1, sz.rows), jnp.float32),
            pltpu.VMEM((sz.modes, 1, sz.loads), jnp.float32),
            pltpu.VMEM((sz.modes, 1, sz.subs * sz.modes), jnp.float32),
            pltpu.VMEM((1, sz.rows), jnp.float32),
            pltpu.VMEM((4, sz.cap), jnp.int32),
            pltpu.SMEM((1, 1, 4), jnp.int32),
            pltpu.SMEM((1, 1), jnp.int32),
            pltpu.SemaphoreType.DMA((8,)),
        ],
        traces.reshape(sz.modes, 1, sz.order), rigid_loads.reshape(sz.modes, 1, sz.loads),
        coarse_inverse.reshape(sz.modes, 1, -1), stiffness, face_order, rhs_parts,
        face_lengths, mode_count, limit=60,
    )
    shared = share(pay, ("gx", "gy"))
    modes, right, coupling = call(
        modes_kernel, [f32(16, sz.rows), half, f32(8, TILE)], [vmem] * (1 + faces), [], base, *swap(own)
    )
    modes_rest = rest(modes)
    *own, pay, estimate = call(
        first_kernel, [face] * faces + [spread_tile, full], [hbm] + [vmem] * 5,
        [square, coarse] + apply_scratch(sz.rows),
        blocks, shared, right, coupling, modes, modes_rest, limit=50 if small else 56,
    )
    before = share(pay, everywhere)
    residual, direction = call(
        second_kernel, [half, half], [vmem] * (3 + 2 * faces), [square, square, coarse, coarse],
        before, shared, modes, *own, *swap(own),
    )
    direction_rest = rest(direction)
    *own, pay = call(
        second_apply_kernel, [face] * faces + [spread_tile], [hbm] + [vmem] * 5,
        apply_scratch(sz.rows - front_rows),
        blocks, hold(direction), modes, residual, direction, direction_rest, limit=42,
    )
    after = share(pay, everywhere)
    later, scalars = call(
        third_kernel, [half, f32(8, TILE)], [vmem] * (6 + 2 * faces),
        [square, square, coarse, coarse],
        after, shared, before, modes, residual, direction, *own, *swap(own),
    )
    later_rest = rest(later)
    pay = call(
        third_apply_kernel, f32(sz.devices if one_step else 1, 1, TILE),
        [hbm] + [vmem] * (5 + faces), apply_scratch(sz.rows - front_rows),
        blocks, hold(later), direction, scalars, later, later_rest, *own, limit=42,
    )
    return call(
        last_kernel, f32(1, 1, 8, sz.order), [vmem] * 7, [],
        share(pay, everywhere), scalars, estimate, direction, direction_rest, later, later_rest,
    )


def solution(mesh):
    in_specs = (
        P("gx", "gy", "gz", None),
        P("gx", "gy", None, None),
        P("gx", "gy", None),
        P("gx", "gy", None, None),
        P("gx", "gy", None, None),
        P("gx", "gy", None, None),
        P("gx", "gy", None),
        P("gx", "gy", None, None),
        P("gx", "gy"),
    )
    out_specs = P("gx", "gy", None, None)
    mesh_shape = tuple(mesh.shape[axis] for axis in ("gx", "gy", "gz"))
    return jax.shard_map(
        functools.partial(shards, mesh_shape),
        mesh=mesh, in_specs=in_specs, out_specs=out_specs, check_vma=False,
    )
```

```python
import functools

import jax
import jax.numpy as jnp
from jax import lax
from jax.experimental import pallas as pl
from jax.experimental.pallas import tpu as pltpu
from jax.sharding import PartitionSpec as P

ROW_CHUNK = 256
PIECE = 128
LOAD_LANE = 6
TILE = 128
SLOT = 8
FOLD = TILE // 2
MIB = 1024 * 1024


class Sizes:
    def __init__(self, mesh_shape, operator, traces, loads):
        self.sx, self.sy, self.gz = mesh_shape
        self.rows = operator.shape[2]
        self.order = operator.shape[3]
        self.modes = traces.shape[2]
        self.cap = self.order // 4
        self.loads = loads
        self.subs = self.sx * self.sy
        self.devices = self.subs * self.gz
        self.coarse = self.subs * SLOT
        self.coarse_pad = -(-self.coarse // TILE) * TILE
        self.own_faces = self.rows // self.cap
        self.group = self.modes * (1 + self.own_faces)
        self.sums = 3 * self.group
        assert self.rows % self.cap == 0 and self.cap % TILE == 0
        assert self.modes <= SLOT - 2 and self.loads == 8 and self.sums + 2 <= FOLD


def f32(*shape):
    return jax.ShapeDtypeStruct(shape, jnp.float32)


def lanes(shape=(8, TILE)):
    return lax.broadcasted_iota(jnp.int32, shape, 1)


def exact_dot(a, b):
    return jnp.dot(a, b, precision=lax.Precision.HIGHEST, preferred_element_type=jnp.float32)


def clamp(index, count):
    return jnp.minimum(jnp.maximum(index, 0), count - 1)


def neighbour(sz, face):
    gx, gy = lax.axis_index("gx"), lax.axis_index("gy")
    x = gx + jnp.where(face == 0, -1, jnp.where(face == 1, 1, 0))
    y = gy + jnp.where(face == 2, -1, jnp.where(face == 3, 1, 0))
    return clamp(x, sz.sx) * sz.sy + clamp(y, sz.sy)


def grid_neighbour(sz, sub, face):
    x, y = divmod(sub, sz.sy)
    x, y = [(x - 1, y), (x + 1, y), (x, y - 1), (x, y + 1)][face]
    return x * sz.sy + y if 0 <= x < sz.sx and 0 <= y < sz.sy else None


def face_pairs(sz, slot):
    pairs = []
    for sub in range(sz.subs):
        for part in range(sz.gz):
            local = slot
            if sz.own_faces > 1:
                first = part * sz.own_faces + slot // 2 * 2
                index = divmod(sub, sz.sy)[first // 2]
                local = slot ^ index & 1
            face = part * sz.own_faces + local
            other = grid_neighbour(sz, sub, face)
            if other is not None:
                pairs.append((sub * sz.gz + part, other * sz.gz + (face ^ 1) // sz.own_faces))
    return pairs


def by_slot(sz, values):
    if sz.own_faces == 1:
        return values
    result = []
    for j in range(0, sz.own_faces, 2):
        first = lax.axis_index("gz") * sz.own_faces + j
        index = jnp.where(first < 2, lax.axis_index("gx"), lax.axis_index("gy"))
        even = lax.rem(index, 2) == 0
        low, high = values[j], values[j + 1]
        result += [jnp.where(even, low, high), jnp.where(even, high, low)]
    return result


def own_face(sz, j):
    return slice(j * sz.cap, (j + 1) * sz.cap)


def put_slots(sz, outs, values):
    for out, value in zip(outs, by_slot(sz, values)):
        out[...] = value


def get_slots(sz, refs):
    return by_slot(sz, [ref[...] for ref in refs])


def permuted(sz, block, slots):
    count = sz.cap // TILE
    pieces = [block[:, k * TILE : (k + 1) * TILE] for k in range(count)]
    result = []
    for j in range(count):
        index = jnp.broadcast_to(slots[:, j * TILE : (j + 1) * TILE], (8, TILE)).astype(jnp.int32)
        low = index & (TILE - 1)
        high = index >> (TILE.bit_length() - 1)
        total = jnp.zeros((8, TILE), jnp.float32)
        for k in range(count):
            picked = jnp.take_along_axis(pieces[k], low, axis=1, mode="promise_in_bounds")
            total = jnp.where(high == k, picked, total)
        result.append(total)
    return jnp.concatenate(result, axis=1)


def coefficients(sz, coarse_ref, sub):
    start = sub * SLOT
    base = pl.multiple_of((start // TILE) * TILE, TILE)
    tile = coarse_ref[:, pl.ds(base, TILE)]
    return pltpu.roll(tile, lax.rem(TILE - lax.rem(start, TILE), TILE), 1)


def views(sz, own, rest):
    if sz.gz == 2:
        gz = lax.axis_index("gz")
        return [(gz, own), (1 - gz, rest)]
    return [(z, rest.at[z]) for z in range(sz.gz)]


def mode_sum(sz, coarse_ref, mine, modes_ref, part, j):
    other = coefficients(sz, coarse_ref, neighbour(sz, part * sz.own_faces + j))
    total = None
    for tile, base in ((mine, 0), (other, SLOT)):
        for m in range(sz.modes):
            term = tile[:, m : m + 1] * modes_ref[base + m : base + m + 1, own_face(sz, j)]
            total = term if total is None else total + term
    return total


def own_coefficients(sz, coarse_ref):
    return coefficients(sz, coarse_ref, lax.axis_index("gx") * sz.sy + lax.axis_index("gy"))


def face_slots(sz, part, j):
    return pl.ds(pl.multiple_of(part * sz.rows + j * sz.cap, TILE), sz.cap)


def mode_products(sz, tile, blocks, modes_ref, first_lane):
    lane = lanes()
    for m in range(sz.modes):
        total = None
        for j, block in enumerate(blocks):
            term = jnp.sum(block * modes_ref[m : m + 1, own_face(sz, j)], axis=1, keepdims=True)
            total = term if total is None else total + term
        tile = jnp.where(lane == first_lane + m, total, tile)
    for j, block in enumerate(blocks):
        face_lane = first_lane + sz.modes * (1 + j)
        for m in range(sz.modes):
            row = modes_ref[SLOT + m : SLOT + m + 1, own_face(sz, j)]
            total = jnp.sum(block * row, axis=1, keepdims=True)
            tile = jnp.where(lane == face_lane + m, total, tile)
    return tile


def weights_of(sz, modes_ref):
    return [modes_ref[6:7, own_face(sz, j)] for j in range(sz.own_faces)]


def unfolded(tile):
    return jnp.concatenate([tile, pltpu.roll(tile, FOLD, 1)], axis=0)


def put_modes(sz, target, rows, tile, lane, sub):
    start = sub * SLOT
    base, offset = start // TILE * TILE, start % TILE
    moved = pltpu.roll(tile, (offset - lane) % TILE, 1)
    wanted = (lanes() >= offset) & (lanes() < offset + sz.modes)
    target[rows, base : base + TILE] += jnp.where(wanted, moved, 0.0)


def fill_coupling(sz, pieces, coupling_ref):
    coupling_ref[...] = jnp.zeros((sz.coarse_pad, sz.coarse_pad), jnp.float32)
    for sub in range(sz.subs):
        rows = slice(sub * SLOT, (sub + 1) * SLOT)
        parts = [unfolded(pieces[sub * sz.gz + z]) for z in range(sz.gz)]
        own = parts[0]
        for part in parts[1:]:
            own = own + part
        put_modes(sz, coupling_ref, rows, own, 2 * sz.group, sub)
        for face in range(4):
            other = grid_neighbour(sz, sub, face)
            if other is not None:
                part, j = divmod(face, sz.own_faces)
                lane = 2 * sz.group + sz.modes * (1 + j)
                put_modes(sz, coupling_ref, rows, parts[part], lane, other)


def fill_inverse(sz, shared, inverse_ref):
    if sz.coarse_pad > sz.coarse:
        inverse_ref[sz.coarse :, :] = jnp.zeros((sz.coarse_pad - sz.coarse, sz.coarse_pad), jnp.float32)
    for sub in range(sz.subs):
        inverse_ref[sub * SLOT : (sub + 1) * SLOT, :] = shared[sub]


def solve_pair(sz, pieces, inverse_ref, coupling_ref, coarse_a, coarse_b):
    coarse_a[...] = jnp.zeros((8, sz.coarse_pad), jnp.float32)
    coarse_b[...] = jnp.zeros((8, sz.coarse_pad), jnp.float32)
    for sub in range(sz.subs):
        total = pieces[sub * sz.gz]
        for part in range(1, sz.gz):
            total = total + pieces[sub * sz.gz + part]
        for face in range(4):
            other = grid_neighbour(sz, sub, face)
            if other is not None:
                part, j = divmod(face ^ 1, sz.own_faces)
                moved = pltpu.roll(pieces[other * sz.gz + part], TILE - sz.modes * (1 + j), 1)
                total = total + moved
        total = unfolded(total)
        put_modes(sz, coarse_a, slice(0, 8), total, 0, sub)
        put_modes(sz, coarse_b, slice(0, 8), total, sz.group, sub)
    first = exact_dot(coarse_a[...], inverse_ref[...])
    coarse_a[...] = first
    coarse_b[...] = exact_dot(coarse_b[...] - exact_dot(first, coupling_ref[...]), inverse_ref[...])


def spread(out, tile):
    out[...] = jnp.broadcast_to(tile[None], out.shape)


def spread_folded(out, tile):
    spread(out, tile[0:4] + pltpu.roll(tile[4:8], FOLD, 1))


def multiply(sz, vector, rows, product, k):
    part = lax.dot_general(
        vector[...], rows.reshape(ROW_CHUNK, sz.order), (((1,), (1,)), ((), ())),
        preferred_element_type=jnp.float32,
    )
    here = pl.ds(pl.multiple_of(k * ROW_CHUNK, TILE), ROW_CHUNK)
    product[:, here] = part.astype(jnp.bfloat16).astype(jnp.float32)


class Stream:
    def __init__(self, sz, operator, held, product, sems):
        self.sz, self.operator, self.held, self.product, self.sems = sz, operator, held, product, sems
        for p in range(sz.rows // PIECE):
            self.copy(p).start()

    def copy(self, p):
        here = pl.ds(p * (PIECE // 8), PIECE // 8)
        return pltpu.make_async_copy(self.operator.at[here], self.held.at[here], self.sems.at[p])

    def apply(self, vector):
        sz, step, blocks = self.sz, ROW_CHUNK // PIECE, ROW_CHUNK // 8

        def chunk(k, carry):
            for p in range(step):
                self.copy(k * step + p).wait()
            multiply(sz, vector, self.held[pl.ds(k * blocks, blocks)], self.product, k)
            return carry

        lax.fori_loop(0, sz.rows // ROW_CHUNK, chunk, 0)
        return [self.product[:, own_face(sz, j)] for j in range(sz.own_faces)]


def apply_held(sz, vector, held, product):
    blocks = ROW_CHUNK // 8
    for k in range(sz.rows // ROW_CHUNK):
        multiply(sz, vector, held[k * blocks : (k + 1) * blocks], product, k)
    return [product[:, own_face(sz, j)] for j in range(sz.own_faces)]


def hold_kernel(sz, operator, after, held, sems):
    del after
    blocks = ROW_CHUNK // 8
    copies = []
    for k in range(sz.rows // ROW_CHUNK):
        here = pl.ds(k * blocks, blocks)
        copies.append(pltpu.make_async_copy(operator.at[here], held.at[here], sems.at[k]))
        copies[-1].start()
    for copy in copies:
        copy.wait()


def part_slots(sz, part):
    return pl.ds(pl.multiple_of(part * sz.rows, TILE), sz.rows)


def put_parts(sz, own, rest, vector):
    for part, ref in views(sz, own, rest):
        vector[:, part_slots(sz, part)] = ref[...].astype(vector.dtype)


def start_kernel(sz, traces, loads, inverse, stiffness, orders, rhs, lengths, count, *refs):
    outs, scratch = refs[: sz.own_faces + 2], refs[sz.own_faces + 2 :]
    faces, (pay, base) = outs[: sz.own_faces], outs[sz.own_faces :]
    traces_in, loads_in, inverse_in, stiffness_in, slots, lengths_in, count_in, sems = scratch
    gz = lax.axis_index("gz")
    here = pl.ds(pl.multiple_of(gz * sz.rows, TILE), sz.rows)
    copies = [
        pltpu.make_async_copy(inverse, inverse_in, sems.at[0]),
        pltpu.make_async_copy(loads, loads_in, sems.at[1]),
        pltpu.make_async_copy(traces.at[:, :, here], traces_in, sems.at[2]),
        pltpu.make_async_copy(stiffness.at[0, :, here], stiffness_in, sems.at[3]),
        pltpu.make_async_copy(orders.at[0, 0], slots, sems.at[4]),
        pltpu.make_async_copy(rhs.at[0, 0, :, here], base.at[pl.ds(8, 8), :], sems.at[5]),
        pltpu.make_async_copy(lengths, lengths_in, sems.at[6]),
        pltpu.make_async_copy(count, count_in, sems.at[7]),
    ]
    for copy in copies:
        copy.start()
    pay[...] = jnp.zeros(pay.shape, jnp.float32)
    base[sz.modes : 8, :] = jnp.zeros((8 - sz.modes, sz.rows), jnp.float32)
    for copy in copies:
        copy.wait()
    for m in range(sz.modes):
        mask = (m < count_in[0, 0]).astype(jnp.float32)
        for t in range(sz.subs):
            pay[0, m : m + 1, t * SLOT : t * SLOT + sz.modes] = inverse_in[
                m, :, t * sz.modes : (t + 1) * sz.modes
            ]
        loads_row = loads_in[m] * mask
        row = pay[0, m : m + 1, 0:TILE]
        for load in range(sz.loads):
            row = jnp.where(lanes((1, TILE)) == SLOT * load + LOAD_LANE, loads_row[:, load : load + 1], row)
        pay[0, m : m + 1, 0:TILE] = row
        base[m : m + 1, :] = traces_in[m] * mask
    position = lax.broadcasted_iota(jnp.int32, (1, sz.cap), 1)
    base[6:7, :] = stiffness_in[...]
    for j in range(sz.own_faces):
        index = gz * sz.own_faces + j
        base[7:8, own_face(sz, j)] = (position < lengths_in[0, 0, index]).astype(jnp.float32)
        chosen = jnp.broadcast_to(slots[pl.ds(index, 1), :], (8, sz.cap))
        base[16:24, own_face(sz, j)] = chosen.astype(jnp.float32)
    put_slots(sz, faces, [base[0:8, own_face(sz, j)] for j in range(sz.own_faces)])
    chunk = pay[0]
    for k in range(1, pay.shape[0]):
        pay[k] = chunk


def modes_kernel(sz, base, *refs):
    arrived, (modes_ref, right, coupling) = refs[: sz.own_faces], refs[sz.own_faces :]
    right[...] = base[8:16, :]
    row = lax.broadcasted_iota(jnp.int32, (8, 1), 0)
    arrived = get_slots(sz, arrived)
    for j in range(sz.own_faces):
        here = own_face(sz, j)
        other = permuted(sz, arrived[j], base[16:24, here])
        mine = base[0:8, here]
        live = mine[7:8, :]
        total = live * (mine[6:7, :] + other[6:7, :])
        weight = live / (total + 1.0 - live)
        modes_ref[0:8, here] = jnp.where(row == 6, weight, jnp.where(row == 7, live, mine * live))
        slots_row = jnp.where(row == 6, base[16:24, here], 0.0)
        modes_ref[8:16, here] = jnp.where(row < sz.modes, other * live, slots_row)
    weights = weights_of(sz, modes_ref)
    coarse_rows = [
        jnp.where(row < sz.modes, modes_ref[0:8, own_face(sz, j)] * weights[j], 0.0)
        for j in range(sz.own_faces)
    ]
    tile = jnp.zeros((8, TILE), jnp.float32)
    coupling[...] = mode_products(sz, tile, coarse_rows, modes_ref, 2 * sz.group)


def assembled(sz, own, arrived, modes_ref, j):
    here = own_face(sz, j)
    return modes_ref[7:8, here] * (own[j] + permuted(sz, arrived[j], modes_ref[14:15, here]))


def tile_products(sz, tile, vectors, modes_ref):
    tile = mode_products(sz, tile, vectors, modes_ref, 0)
    scaled = [v * w for v, w in zip(vectors, weights_of(sz, modes_ref))]
    return mode_products(sz, tile, scaled, modes_ref, sz.group)


def first_kernel(sz, operator, shared, right, coupling, modes_ref, modes_rest, *refs):
    outs, refs = refs[: sz.own_faces], refs[sz.own_faces :]
    pay, estimate_ref, inverse_ref, coarse_ref, held, product, vector, sems = refs
    stream = Stream(sz, operator, held, product, sems)
    fill_inverse(sz, shared, inverse_ref)
    turned = []
    for k in range(sz.coarse_pad // TILE):
        block = jnp.transpose(inverse_ref[k * TILE : (k + 1) * TILE, 0:TILE])
        rows = [SLOT * load + LOAD_LANE for load in range(sz.loads)]
        turned.append(jnp.concatenate([block[r : r + 1] for r in rows], axis=0))
    coarse_ref[...] = exact_dot(jnp.concatenate(turned, axis=1), inverse_ref[...])
    mine = own_coefficients(sz, coarse_ref)
    for part, modes in views(sz, modes_ref, modes_rest):
        for j in range(sz.own_faces):
            here = face_slots(sz, part, j)
            estimate = mode_sum(sz, coarse_ref, mine, modes, part, j)
            estimate_ref[:, here] = estimate
            vector[:, here] = estimate.astype(jnp.bfloat16)
    pieces = stream.apply(vector)
    vectors = [right[:, own_face(sz, j)] - piece for j, piece in enumerate(pieces)]
    put_slots(sz, outs, vectors)
    spread_folded(pay, tile_products(sz, coupling[...], vectors, modes_ref))


def second_kernel(sz, pieces, shared, modes_ref, *refs):
    own, refs = get_slots(sz, refs[: sz.own_faces]), refs[sz.own_faces :]
    arrived, refs = get_slots(sz, refs[: sz.own_faces]), refs[sz.own_faces :]
    residual_ref, direction_ref, inverse_ref, coupling_ref, coarse_a, coarse_b = refs
    gz = lax.axis_index("gz")
    fill_inverse(sz, shared, inverse_ref)
    fill_coupling(sz, pieces, coupling_ref)
    solve_pair(sz, pieces, inverse_ref, coupling_ref, coarse_a, coarse_b)
    first, second = own_coefficients(sz, coarse_a), own_coefficients(sz, coarse_b)
    for j in range(sz.own_faces):
        here = own_face(sz, j)
        gap = assembled(sz, own, arrived, modes_ref, j)
        residual = gap - mode_sum(sz, coarse_a, first, modes_ref, gz, j)
        residual_ref[:, here] = residual
        correction = mode_sum(sz, coarse_b, second, modes_ref, gz, j)
        direction_ref[:, here] = modes_ref[6:7, here] * residual - correction


def second_apply_kernel(sz, held, modes_ref, residual, direction, rest, *refs):
    outs, refs = refs[: sz.own_faces], refs[sz.own_faces :]
    pay, product, vector = refs
    put_parts(sz, direction, rest, vector)
    weights = weights_of(sz, modes_ref)
    lane = lanes()
    curvature = jnp.zeros((8, 1), jnp.float32)
    resid_dot = jnp.zeros((8, 1), jnp.float32)
    pieces = apply_held(sz, vector, held, product)
    put_slots(sz, outs, pieces)
    for j, piece in enumerate(pieces):
        here = own_face(sz, j)
        own = residual[:, here]
        resid_dot += jnp.sum(own * (weights[j] * own), axis=1, keepdims=True)
        curvature += jnp.sum(direction[:, here] * piece, axis=1, keepdims=True)
    tile = jnp.where(lane == sz.sums, curvature, jnp.zeros((8, TILE), jnp.float32))
    tile = jnp.where(lane == sz.sums + 1, resid_dot, tile)
    spread_folded(pay, tile_products(sz, tile, pieces, modes_ref))


def third_kernel(sz, pieces, shared, before, modes_ref, residual_ref, direction_ref, *refs):
    own, refs = get_slots(sz, refs[: sz.own_faces]), refs[sz.own_faces :]
    arrived, refs = get_slots(sz, refs[: sz.own_faces]), refs[sz.own_faces :]
    later_ref, scalars_ref, inverse_ref, coupling_ref, coarse_a, coarse_b = refs
    gz = lax.axis_index("gz")
    lane = lanes()
    fill_inverse(sz, shared, inverse_ref)
    fill_coupling(sz, before, coupling_ref)
    totals = pieces[0]
    for k in range(1, sz.devices):
        totals = totals + pieces[k]
    totals = unfolded(totals)
    curvature = 2.0 * totals[:, sz.sums : sz.sums + 1]
    resid_dot = totals[:, sz.sums + 1 : sz.sums + 2]
    step = resid_dot / curvature
    solve_pair(sz, pieces, inverse_ref, coupling_ref, coarse_a, coarse_b)
    first, second = own_coefficients(sz, coarse_a), own_coefficients(sz, coarse_b)
    dot_part = jnp.zeros((8, 1), jnp.float32)
    for j in range(sz.own_faces):
        here = own_face(sz, j)
        image = assembled(sz, own, arrived, modes_ref, j)
        corrected = image - mode_sum(sz, coarse_a, first, modes_ref, gz, j)
        weight = modes_ref[6:7, here]
        scaled = weight * corrected - mode_sum(sz, coarse_b, second, modes_ref, gz, j)
        residual = residual_ref[:, here] - step * corrected
        dot_part += jnp.sum(residual * (weight * residual), axis=1, keepdims=True)
        later_ref[:, here] = direction_ref[:, here] - step * scaled
    scalars_ref[...] = jnp.where(lane == 0, curvature, jnp.where(lane == 1, resid_dot, dot_part))


def third_apply_kernel(sz, held, direction, scalars, later, rest, *refs):
    before, refs = get_slots(sz, refs[: sz.own_faces]), refs[sz.own_faces :]
    pay, product, vector = refs
    put_parts(sz, later, rest, vector)
    pieces = apply_held(sz, vector, held, product)
    lane = lanes()
    later_part = jnp.zeros((8, 1), jnp.float32)
    cross_part = jnp.zeros((8, 1), jnp.float32)
    for j, piece in enumerate(pieces):
        mine = later[:, own_face(sz, j)]
        earlier = direction[:, own_face(sz, j)]
        later_part += jnp.sum(mine * piece, axis=1, keepdims=True)
        cross_part += jnp.sum(mine * before[j] + earlier * piece, axis=1, keepdims=True)
    load = lax.broadcasted_iota(jnp.int32, (8, TILE), 0)
    line = jnp.where(lane == load, later_part, 0.0)
    line = jnp.where(lane == load + 8, cross_part, line)
    line = jnp.where(lane == load + 16, scalars[:, 2:3], line)
    spread(pay, jnp.sum(line, axis=0, keepdims=True))


def last_kernel(sz, pieces, scalars, estimate, direction, direction_rest, later, later_rest, out):
    totals = pieces[0]
    for k in range(1, pieces.shape[0]):
        totals = totals + pieces[k]
    curvature, previous = scalars[:, 0:1], scalars[:, 1:2]
    load = lax.broadcasted_iota(jnp.int32, (8, TILE), 0)
    later_part, cross_part, dot = [
        jnp.sum(jnp.where(lanes() == load + 8 * k, totals, 0.0), axis=1, keepdims=True)
        for k in range(3)
    ]
    ratio = dot / previous
    final = 2.0 * (later_part + ratio * cross_part) + ratio * ratio * curvature
    first, second = previous / curvature, dot / final
    both = zip(views(sz, direction, direction_rest), views(sz, later, later_rest))
    for (part, earlier), (_, mine) in both:
        here = part_slots(sz, part)
        moved = estimate[:, here] + first * earlier[...]
        out[0, 0, :, here] = moved + second * (mine[...] + ratio * earlier[...])


def shards(mesh_shape, operator, rhs_parts, stiffness, traces, coarse_inverse, rigid_loads,
           face_lengths, face_order, mode_count):
    sz = Sizes(mesh_shape, operator, traces, rhs_parts.shape[2])
    vmem = pl.BlockSpec(memory_space=pltpu.VMEM)
    smem = pl.BlockSpec(memory_space=pltpu.SMEM)
    hbm = pl.BlockSpec(memory_space=pltpu.HBM)
    everywhere = ("gx", "gy", "gz")
    small = sz.coarse_pad <= 256

    def call(kernel, out_shape, in_specs, scratch, *operands, limit=None, cost=None):
        return pl.pallas_call(
            functools.partial(kernel, sz),
            out_shape=out_shape,
            in_specs=in_specs,
            out_specs=jax.tree.map(lambda _: vmem, out_shape),
            scratch_shapes=scratch,
            cost_estimate=cost,
            compiler_params=pltpu.CompilerParams(
                vmem_limit_bytes=(limit or (16 if small else 56)) * MIB
            ),
        )(*operands)

    faces = sz.own_faces
    coarse = pltpu.VMEM((8, sz.coarse_pad), jnp.float32)
    square = pltpu.VMEM((sz.coarse_pad, sz.coarse_pad), jnp.float32)
    half, full, face = f32(8, sz.rows), f32(8, sz.order), f32(8, sz.cap)
    blocks = operator.reshape(sz.rows // 8, 8, sz.order)
    one_step = sz.devices <= 64
    spread_tile = f32(sz.devices if one_step else 1, 4, TILE)
    apply_scratch = [
        pltpu.VMEM((8, sz.rows), jnp.float32),
        pltpu.VMEM((8, sz.order), jnp.bfloat16),
    ]
    copies = sz.rows // PIECE
    stream_scratch = [pltpu.VMEM((sz.rows // 8, 8, sz.order), jnp.bfloat16)] + apply_scratch
    stream_scratch += [pltpu.SemaphoreType.DMA((copies,))]

    def hold(after):
        return call(
            hold_kernel, jax.ShapeDtypeStruct((sz.rows // 8, 8, sz.order), jnp.bfloat16),
            [hbm, vmem], [pltpu.SemaphoreType.DMA((copies,))], blocks, after, limit=42,
            cost=pl.CostEstimate(flops=0, bytes_accessed=4 * sz.rows * sz.order, transcendentals=0),
        )

    def swap(own):
        return [lax.ppermute(own[j], everywhere, face_pairs(sz, j)) for j in range(faces)]

    def share(chunk, axes):
        if chunk.shape[0] == 1:
            return lax.all_gather(chunk, axes, axis=0, tiled=True)
        return lax.all_to_all(chunk, axes, split_axis=0, concat_axis=0, tiled=True)

    def rest(part):
        if sz.gz == 2:
            return lax.ppermute(part, "gz", [(0, 1), (1, 0)])
        return lax.all_gather(part, "gz", axis=0, tiled=False)

    *own, pay, base = call(
        start_kernel,
        [face] * faces + [f32(sz.subs if one_step else 1, 8, sz.coarse_pad), f32(24, sz.rows)],
        [hbm] * 8,
        [
            pltpu.VMEM((sz.modes, 1, sz.rows), jnp.float32),
            pltpu.VMEM((sz.modes, 1, sz.loads), jnp.float32),
            pltpu.VMEM((sz.modes, 1, sz.subs * sz.modes), jnp.float32),
            pltpu.VMEM((1, sz.rows), jnp.float32),
            pltpu.VMEM((4, sz.cap), jnp.int32),
            pltpu.SMEM((1, 1, 4), jnp.int32),
            pltpu.SMEM((1, 1), jnp.int32),
            pltpu.SemaphoreType.DMA((8,)),
        ],
        traces.reshape(sz.modes, 1, sz.order), rigid_loads.reshape(sz.modes, 1, sz.loads),
        coarse_inverse.reshape(sz.modes, 1, -1), stiffness, face_order, rhs_parts,
        face_lengths, mode_count, limit=60,
    )
    shared = share(pay, ("gx", "gy"))
    modes, right, coupling = call(
        modes_kernel, [f32(16, sz.rows), half, f32(8, TILE)], [vmem] * (1 + faces), [], base, *swap(own)
    )
    modes_rest = rest(modes)
    *own, pay, estimate = call(
        first_kernel, [face] * faces + [spread_tile, full], [hbm] + [vmem] * 5,
        [square, coarse] + stream_scratch,
        blocks, shared, right, coupling, modes, modes_rest, limit=50 if small else 56,
    )
    before = share(pay, everywhere)
    residual, direction = call(
        second_kernel, [half, half], [vmem] * (3 + 2 * faces), [square, square, coarse, coarse],
        before, shared, modes, *own, *swap(own),
    )
    direction_rest = rest(direction)
    *own, pay = call(
        second_apply_kernel, [face] * faces + [spread_tile], [vmem] * 5,
        apply_scratch, hold(direction), modes, residual, direction, direction_rest,
    )
    after = share(pay, everywhere)
    later, scalars = call(
        third_kernel, [half, f32(8, TILE)], [vmem] * (6 + 2 * faces),
        [square, square, coarse, coarse],
        after, shared, before, modes, residual, direction, *own, *swap(own),
    )
    later_rest = rest(later)
    pay = call(
        third_apply_kernel, f32(sz.devices if one_step else 1, 1, TILE),
        [vmem] * (5 + faces), apply_scratch,
        hold(later), direction, scalars, later, later_rest, *own,
    )
    return call(
        last_kernel, f32(1, 1, 8, sz.order), [vmem] * 7, [],
        share(pay, everywhere), scalars, estimate, direction, direction_rest, later, later_rest,
    )


def solution(mesh):
    in_specs = (
        P("gx", "gy", "gz", None),
        P("gx", "gy", None, None),
        P("gx", "gy", None),
        P("gx", "gy", None, None),
        P("gx", "gy", None, None),
        P("gx", "gy", None, None),
        P("gx", "gy", None),
        P("gx", "gy", None, None),
        P("gx", "gy"),
    )
    out_specs = P("gx", "gy", None, None)
    mesh_shape = tuple(mesh.shape[axis] for axis in ("gx", "gy", "gz"))
    return jax.shard_map(
        functools.partial(shards, mesh_shape),
        mesh=mesh, in_specs=in_specs, out_specs=out_specs, check_vma=False,
    )
```

```python
import functools

import jax
import jax.numpy as jnp
from jax import lax
from jax.experimental import pallas as pl
from jax.experimental.pallas import tpu as pltpu
from jax.sharding import PartitionSpec as P

ROW_CHUNK = 256
PIECE = 128
LOAD_LANE = 6
TILE = 128
SLOT = 8
FOLD = TILE // 2
MIB = 1024 * 1024


class Sizes:
    def __init__(self, mesh_shape, operator, traces, loads):
        self.sx, self.sy, self.gz = mesh_shape
        self.rows = operator.shape[2]
        self.order = operator.shape[3]
        self.modes = traces.shape[2]
        self.cap = self.order // 4
        self.loads = loads
        self.subs = self.sx * self.sy
        self.devices = self.subs * self.gz
        self.coarse = self.subs * SLOT
        self.coarse_pad = -(-self.coarse // TILE) * TILE
        self.own_faces = self.rows // self.cap
        self.group = self.modes * (1 + self.own_faces)
        self.sums = 3 * self.group
        assert self.rows % self.cap == 0 and self.cap % TILE == 0
        assert self.modes <= SLOT - 2 and self.loads == 8 and self.sums + 2 <= FOLD


def f32(*shape):
    return jax.ShapeDtypeStruct(shape, jnp.float32)


def lanes(shape=(8, TILE)):
    return lax.broadcasted_iota(jnp.int32, shape, 1)


def exact_dot(a, b):
    return jnp.dot(a, b, precision=lax.Precision.HIGHEST, preferred_element_type=jnp.float32)


def clamp(index, count):
    return jnp.minimum(jnp.maximum(index, 0), count - 1)


def neighbour(sz, face):
    gx, gy = lax.axis_index("gx"), lax.axis_index("gy")
    x = gx + jnp.where(face == 0, -1, jnp.where(face == 1, 1, 0))
    y = gy + jnp.where(face == 2, -1, jnp.where(face == 3, 1, 0))
    return clamp(x, sz.sx) * sz.sy + clamp(y, sz.sy)


def grid_neighbour(sz, sub, face):
    x, y = divmod(sub, sz.sy)
    x, y = [(x - 1, y), (x + 1, y), (x, y - 1), (x, y + 1)][face]
    return x * sz.sy + y if 0 <= x < sz.sx and 0 <= y < sz.sy else None


def face_pairs(sz, slot):
    pairs = []
    for sub in range(sz.subs):
        for part in range(sz.gz):
            local = slot
            if sz.own_faces > 1:
                first = part * sz.own_faces + slot // 2 * 2
                index = divmod(sub, sz.sy)[first // 2]
                local = slot ^ index & 1
            face = part * sz.own_faces + local
            other = grid_neighbour(sz, sub, face)
            if other is not None:
                pairs.append((sub * sz.gz + part, other * sz.gz + (face ^ 1) // sz.own_faces))
    return pairs


def by_slot(sz, values):
    if sz.own_faces == 1:
        return values
    result = []
    for j in range(0, sz.own_faces, 2):
        first = lax.axis_index("gz") * sz.own_faces + j
        index = jnp.where(first < 2, lax.axis_index("gx"), lax.axis_index("gy"))
        even = lax.rem(index, 2) == 0
        low, high = values[j], values[j + 1]
        result += [jnp.where(even, low, high), jnp.where(even, high, low)]
    return result


def own_face(sz, j):
    return slice(j * sz.cap, (j + 1) * sz.cap)


def put_slots(sz, outs, values):
    for out, value in zip(outs, by_slot(sz, values)):
        out[...] = value.astype(out.dtype)


def get_slots(sz, refs):
    return by_slot(sz, [ref[...].astype(jnp.float32) for ref in refs])


def permuted(sz, block, slots):
    count = sz.cap // TILE
    pieces = [block[:, k * TILE : (k + 1) * TILE] for k in range(count)]
    result = []
    for j in range(count):
        index = jnp.broadcast_to(slots[:, j * TILE : (j + 1) * TILE], (8, TILE)).astype(jnp.int32)
        low = index & (TILE - 1)
        high = index >> (TILE.bit_length() - 1)
        total = jnp.zeros((8, TILE), jnp.float32)
        for k in range(count):
            picked = jnp.take_along_axis(pieces[k], low, axis=1, mode="promise_in_bounds")
            total = jnp.where(high == k, picked, total)
        result.append(total)
    return jnp.concatenate(result, axis=1)


def coefficients(sz, coarse_ref, sub):
    start = sub * SLOT
    base = pl.multiple_of((start // TILE) * TILE, TILE)
    tile = coarse_ref[:, pl.ds(base, TILE)]
    return pltpu.roll(tile, lax.rem(TILE - lax.rem(start, TILE), TILE), 1)


def views(sz, own, rest):
    if sz.gz == 2:
        gz = lax.axis_index("gz")
        return [(gz, own), (1 - gz, rest)]
    return [(z, rest.at[z]) for z in range(sz.gz)]


def mode_sum(sz, coarse_ref, mine, modes_ref, part, j):
    other = coefficients(sz, coarse_ref, neighbour(sz, part * sz.own_faces + j))
    total = None
    for tile, base in ((mine, 0), (other, SLOT)):
        for m in range(sz.modes):
            term = tile[:, m : m + 1] * modes_ref[base + m : base + m + 1, own_face(sz, j)]
            total = term if total is None else total + term
    return total


def own_coefficients(sz, coarse_ref):
    return coefficients(sz, coarse_ref, lax.axis_index("gx") * sz.sy + lax.axis_index("gy"))


def face_slots(sz, part, j):
    return pl.ds(pl.multiple_of(part * sz.rows + j * sz.cap, TILE), sz.cap)


def mode_products(sz, tile, blocks, modes_ref, first_lane):
    lane = lanes()
    for m in range(sz.modes):
        total = None
        for j, block in enumerate(blocks):
            term = jnp.sum(block * modes_ref[m : m + 1, own_face(sz, j)], axis=1, keepdims=True)
            total = term if total is None else total + term
        tile = jnp.where(lane == first_lane + m, total, tile)
    for j, block in enumerate(blocks):
        face_lane = first_lane + sz.modes * (1 + j)
        for m in range(sz.modes):
            row = modes_ref[SLOT + m : SLOT + m + 1, own_face(sz, j)]
            total = jnp.sum(block * row, axis=1, keepdims=True)
            tile = jnp.where(lane == face_lane + m, total, tile)
    return tile


def weights_of(sz, modes_ref):
    return [modes_ref[6:7, own_face(sz, j)] for j in range(sz.own_faces)]


def unfolded(tile):
    return jnp.concatenate([tile, pltpu.roll(tile, FOLD, 1)], axis=0)


def put_modes(sz, target, rows, tile, lane, sub):
    start = sub * SLOT
    base, offset = start // TILE * TILE, start % TILE
    moved = pltpu.roll(tile, (offset - lane) % TILE, 1)
    wanted = (lanes() >= offset) & (lanes() < offset + sz.modes)
    target[rows, base : base + TILE] += jnp.where(wanted, moved, 0.0)


def fill_coupling(sz, pieces, coupling_ref):
    coupling_ref[...] = jnp.zeros((sz.coarse_pad, sz.coarse_pad), jnp.float32)
    for sub in range(sz.subs):
        rows = slice(sub * SLOT, (sub + 1) * SLOT)
        parts = [unfolded(pieces[sub * sz.gz + z]) for z in range(sz.gz)]
        own = parts[0]
        for part in parts[1:]:
            own = own + part
        put_modes(sz, coupling_ref, rows, own, 2 * sz.group, sub)
        for face in range(4):
            other = grid_neighbour(sz, sub, face)
            if other is not None:
                part, j = divmod(face, sz.own_faces)
                lane = 2 * sz.group + sz.modes * (1 + j)
                put_modes(sz, coupling_ref, rows, parts[part], lane, other)


def fill_inverse(sz, shared, inverse_ref):
    if sz.coarse_pad > sz.coarse:
        inverse_ref[sz.coarse :, :] = jnp.zeros((sz.coarse_pad - sz.coarse, sz.coarse_pad), jnp.float32)
    for sub in range(sz.subs):
        inverse_ref[sub * SLOT : (sub + 1) * SLOT, :] = shared[sub]


def solve_pair(sz, pieces, inverse_ref, coupling_ref, coarse_a, coarse_b):
    coarse_a[...] = jnp.zeros((8, sz.coarse_pad), jnp.float32)
    coarse_b[...] = jnp.zeros((8, sz.coarse_pad), jnp.float32)
    for sub in range(sz.subs):
        total = pieces[sub * sz.gz]
        for part in range(1, sz.gz):
            total = total + pieces[sub * sz.gz + part]
        for face in range(4):
            other = grid_neighbour(sz, sub, face)
            if other is not None:
                part, j = divmod(face ^ 1, sz.own_faces)
                moved = pltpu.roll(pieces[other * sz.gz + part], TILE - sz.modes * (1 + j), 1)
                total = total + moved
        total = unfolded(total)
        put_modes(sz, coarse_a, slice(0, 8), total, 0, sub)
        put_modes(sz, coarse_b, slice(0, 8), total, sz.group, sub)
    first = exact_dot(coarse_a[...], inverse_ref[...])
    coarse_a[...] = first
    coarse_b[...] = exact_dot(coarse_b[...] - exact_dot(first, coupling_ref[...]), inverse_ref[...])


def spread(out, tile):
    out[...] = jnp.broadcast_to(tile[None], out.shape)


def spread_folded(out, tile):
    spread(out, tile[0:4] + pltpu.roll(tile[4:8], FOLD, 1))


def multiply(sz, vector, rows, product, k):
    part = lax.dot_general(
        vector[...], rows.reshape(ROW_CHUNK, sz.order), (((1,), (1,)), ((), ())),
        preferred_element_type=jnp.float32,
    )
    here = pl.ds(pl.multiple_of(k * ROW_CHUNK, TILE), ROW_CHUNK)
    product[:, here] = part.astype(jnp.bfloat16).astype(jnp.float32)


class Stream:
    def __init__(self, sz, operator, held, product, sems):
        self.sz, self.operator, self.held, self.product, self.sems = sz, operator, held, product, sems
        for p in range(sz.rows // PIECE):
            self.copy(p).start()

    def copy(self, p):
        here = pl.ds(p * (PIECE // 8), PIECE // 8)
        return pltpu.make_async_copy(self.operator.at[here], self.held.at[here], self.sems.at[p])

    def apply(self, vector):
        sz, step, blocks = self.sz, ROW_CHUNK // PIECE, ROW_CHUNK // 8

        def chunk(k, carry):
            for p in range(step):
                self.copy(k * step + p).wait()
            multiply(sz, vector, self.held[pl.ds(k * blocks, blocks)], self.product, k)
            return carry

        lax.fori_loop(0, sz.rows // ROW_CHUNK, chunk, 0)
        return [self.product[:, own_face(sz, j)] for j in range(sz.own_faces)]


def apply_held(sz, vector, held, product):
    blocks = ROW_CHUNK // 8
    for k in range(sz.rows // ROW_CHUNK):
        multiply(sz, vector, held[k * blocks : (k + 1) * blocks], product, k)
    return [product[:, own_face(sz, j)] for j in range(sz.own_faces)]


def hold_kernel(sz, operator, after, held, sems):
    del after
    blocks = ROW_CHUNK // 8
    copies = []
    for k in range(sz.rows // ROW_CHUNK):
        here = pl.ds(k * blocks, blocks)
        copies.append(pltpu.make_async_copy(operator.at[here], held.at[here], sems.at[k]))
        copies[-1].start()
    for copy in copies:
        copy.wait()


def part_slots(sz, part):
    return pl.ds(pl.multiple_of(part * sz.rows, TILE), sz.rows)


def put_parts(sz, own, rest, vector):
    for part, ref in views(sz, own, rest):
        vector[:, part_slots(sz, part)] = ref[...].astype(vector.dtype)


def start_kernel(sz, traces, loads, inverse, stiffness, orders, rhs, lengths, count, *refs):
    outs, scratch = refs[: sz.own_faces + 2], refs[sz.own_faces + 2 :]
    faces, (pay, base) = outs[: sz.own_faces], outs[sz.own_faces :]
    traces_in, loads_in, inverse_in, stiffness_in, slots, lengths_in, count_in, sems = scratch
    gz = lax.axis_index("gz")
    here = pl.ds(pl.multiple_of(gz * sz.rows, TILE), sz.rows)
    copies = [
        pltpu.make_async_copy(inverse, inverse_in, sems.at[0]),
        pltpu.make_async_copy(loads, loads_in, sems.at[1]),
        pltpu.make_async_copy(traces.at[:, :, here], traces_in, sems.at[2]),
        pltpu.make_async_copy(stiffness.at[0, :, here], stiffness_in, sems.at[3]),
        pltpu.make_async_copy(orders.at[0, 0], slots, sems.at[4]),
        pltpu.make_async_copy(rhs.at[0, 0, :, here], base.at[pl.ds(8, 8), :], sems.at[5]),
        pltpu.make_async_copy(lengths, lengths_in, sems.at[6]),
        pltpu.make_async_copy(count, count_in, sems.at[7]),
    ]
    for copy in copies:
        copy.start()
    pay[...] = jnp.zeros(pay.shape, jnp.float32)
    base[sz.modes : 8, :] = jnp.zeros((8 - sz.modes, sz.rows), jnp.float32)
    for copy in copies:
        copy.wait()
    for m in range(sz.modes):
        mask = (m < count_in[0, 0]).astype(jnp.float32)
        for t in range(sz.subs):
            pay[0, m : m + 1, t * SLOT : t * SLOT + sz.modes] = inverse_in[
                m, :, t * sz.modes : (t + 1) * sz.modes
            ]
        loads_row = loads_in[m] * mask
        row = pay[0, m : m + 1, 0:TILE]
        for load in range(sz.loads):
            row = jnp.where(lanes((1, TILE)) == SLOT * load + LOAD_LANE, loads_row[:, load : load + 1], row)
        pay[0, m : m + 1, 0:TILE] = row
        base[m : m + 1, :] = traces_in[m] * mask
    position = lax.broadcasted_iota(jnp.int32, (1, sz.cap), 1)
    base[6:7, :] = stiffness_in[...]
    for j in range(sz.own_faces):
        index = gz * sz.own_faces + j
        base[7:8, own_face(sz, j)] = (position < lengths_in[0, 0, index]).astype(jnp.float32)
        chosen = jnp.broadcast_to(slots[pl.ds(index, 1), :], (8, sz.cap))
        base[16:24, own_face(sz, j)] = chosen.astype(jnp.float32)
    put_slots(sz, faces, [base[0:8, own_face(sz, j)] for j in range(sz.own_faces)])
    chunk = pay[0]
    for k in range(1, pay.shape[0]):
        pay[k] = chunk


def modes_kernel(sz, base, *refs):
    arrived, (modes_ref, right, coupling) = refs[: sz.own_faces], refs[sz.own_faces :]
    right[...] = base[8:16, :]
    row = lax.broadcasted_iota(jnp.int32, (8, 1), 0)
    arrived = get_slots(sz, arrived)
    for j in range(sz.own_faces):
        here = own_face(sz, j)
        other = permuted(sz, arrived[j], base[16:24, here])
        mine = base[0:8, here]
        live = mine[7:8, :]
        total = live * (mine[6:7, :] + other[6:7, :])
        weight = live / (total + 1.0 - live)
        modes_ref[0:8, here] = jnp.where(row == 6, weight, jnp.where(row == 7, live, mine * live))
        slots_row = jnp.where(row == 6, base[16:24, here], 0.0)
        modes_ref[8:16, here] = jnp.where(row < sz.modes, other * live, slots_row)
    weights = weights_of(sz, modes_ref)
    coarse_rows = [
        jnp.where(row < sz.modes, modes_ref[0:8, own_face(sz, j)] * weights[j], 0.0)
        for j in range(sz.own_faces)
    ]
    tile = jnp.zeros((8, TILE), jnp.float32)
    coupling[...] = mode_products(sz, tile, coarse_rows, modes_ref, 2 * sz.group)


def assembled(sz, own, arrived, modes_ref, j):
    here = own_face(sz, j)
    return modes_ref[7:8, here] * (own[j] + permuted(sz, arrived[j], modes_ref[14:15, here]))


def tile_products(sz, tile, vectors, modes_ref):
    tile = mode_products(sz, tile, vectors, modes_ref, 0)
    scaled = [v * w for v, w in zip(vectors, weights_of(sz, modes_ref))]
    return mode_products(sz, tile, scaled, modes_ref, sz.group)


def first_kernel(sz, operator, shared, right, coupling, modes_ref, modes_rest, *refs):
    outs, refs = refs[: sz.own_faces], refs[sz.own_faces :]
    pay, estimate_ref, inverse_ref, coarse_ref, held, product, vector, sems = refs
    stream = Stream(sz, operator, held, product, sems)
    fill_inverse(sz, shared, inverse_ref)
    turned = []
    for k in range(sz.coarse_pad // TILE):
        block = jnp.transpose(inverse_ref[k * TILE : (k + 1) * TILE, 0:TILE])
        rows = [SLOT * load + LOAD_LANE for load in range(sz.loads)]
        turned.append(jnp.concatenate([block[r : r + 1] for r in rows], axis=0))
    coarse_ref[...] = exact_dot(jnp.concatenate(turned, axis=1), inverse_ref[...])
    mine = own_coefficients(sz, coarse_ref)
    for part, modes in views(sz, modes_ref, modes_rest):
        for j in range(sz.own_faces):
            here = face_slots(sz, part, j)
            estimate = mode_sum(sz, coarse_ref, mine, modes, part, j)
            estimate_ref[:, here] = estimate
            vector[:, here] = estimate.astype(jnp.bfloat16)
    pieces = stream.apply(vector)
    vectors = [right[:, own_face(sz, j)] - piece for j, piece in enumerate(pieces)]
    put_slots(sz, outs, vectors)
    spread_folded(pay, tile_products(sz, coupling[...], vectors, modes_ref))


def second_kernel(sz, pieces, shared, modes_ref, *refs):
    own, refs = get_slots(sz, refs[: sz.own_faces]), refs[sz.own_faces :]
    arrived, refs = get_slots(sz, refs[: sz.own_faces]), refs[sz.own_faces :]
    residual_ref, direction_ref, inverse_ref, coupling_ref, coarse_a, coarse_b = refs
    gz = lax.axis_index("gz")
    fill_inverse(sz, shared, inverse_ref)
    fill_coupling(sz, pieces, coupling_ref)
    solve_pair(sz, pieces, inverse_ref, coupling_ref, coarse_a, coarse_b)
    first, second = own_coefficients(sz, coarse_a), own_coefficients(sz, coarse_b)
    for j in range(sz.own_faces):
        here = own_face(sz, j)
        gap = assembled(sz, own, arrived, modes_ref, j)
        residual = gap - mode_sum(sz, coarse_a, first, modes_ref, gz, j)
        residual_ref[:, here] = residual
        correction = mode_sum(sz, coarse_b, second, modes_ref, gz, j)
        direction_ref[:, here] = modes_ref[6:7, here] * residual - correction


def second_apply_kernel(sz, held, modes_ref, residual, direction, rest, *refs):
    outs, refs = refs[: sz.own_faces], refs[sz.own_faces :]
    pay, product, vector = refs
    put_parts(sz, direction, rest, vector)
    weights = weights_of(sz, modes_ref)
    lane = lanes()
    curvature = jnp.zeros((8, 1), jnp.float32)
    resid_dot = jnp.zeros((8, 1), jnp.float32)
    pieces = apply_held(sz, vector, held, product)
    put_slots(sz, outs, pieces)
    for j, piece in enumerate(pieces):
        here = own_face(sz, j)
        own = residual[:, here]
        resid_dot += jnp.sum(own * (weights[j] * own), axis=1, keepdims=True)
        curvature += jnp.sum(direction[:, here] * piece, axis=1, keepdims=True)
    tile = jnp.where(lane == sz.sums, curvature, jnp.zeros((8, TILE), jnp.float32))
    tile = jnp.where(lane == sz.sums + 1, resid_dot, tile)
    spread_folded(pay, tile_products(sz, tile, pieces, modes_ref))


def third_kernel(sz, pieces, shared, before, modes_ref, residual_ref, direction_ref, *refs):
    own, refs = get_slots(sz, refs[: sz.own_faces]), refs[sz.own_faces :]
    arrived, refs = get_slots(sz, refs[: sz.own_faces]), refs[sz.own_faces :]
    later_ref, scalars_ref, inverse_ref, coupling_ref, coarse_a, coarse_b = refs
    gz = lax.axis_index("gz")
    lane = lanes()
    fill_inverse(sz, shared, inverse_ref)
    fill_coupling(sz, before, coupling_ref)
    totals = pieces[0]
    for k in range(1, sz.devices):
        totals = totals + pieces[k]
    totals = unfolded(totals)
    curvature = 2.0 * totals[:, sz.sums : sz.sums + 1]
    resid_dot = totals[:, sz.sums + 1 : sz.sums + 2]
    step = resid_dot / curvature
    solve_pair(sz, pieces, inverse_ref, coupling_ref, coarse_a, coarse_b)
    first, second = own_coefficients(sz, coarse_a), own_coefficients(sz, coarse_b)
    dot_part = jnp.zeros((8, 1), jnp.float32)
    for j in range(sz.own_faces):
        here = own_face(sz, j)
        image = assembled(sz, own, arrived, modes_ref, j)
        corrected = image - mode_sum(sz, coarse_a, first, modes_ref, gz, j)
        weight = modes_ref[6:7, here]
        scaled = weight * corrected - mode_sum(sz, coarse_b, second, modes_ref, gz, j)
        residual = residual_ref[:, here] - step * corrected
        dot_part += jnp.sum(residual * (weight * residual), axis=1, keepdims=True)
        later_ref[:, here] = direction_ref[:, here] - step * scaled
    scalars_ref[...] = jnp.where(lane == 0, curvature, jnp.where(lane == 1, resid_dot, dot_part))


def third_apply_kernel(sz, held, direction, scalars, later, rest, *refs):
    before, refs = get_slots(sz, refs[: sz.own_faces]), refs[sz.own_faces :]
    pay, product, vector = refs
    put_parts(sz, later, rest, vector)
    pieces = apply_held(sz, vector, held, product)
    lane = lanes()
    later_part = jnp.zeros((8, 1), jnp.float32)
    cross_part = jnp.zeros((8, 1), jnp.float32)
    for j, piece in enumerate(pieces):
        mine = later[:, own_face(sz, j)]
        earlier = direction[:, own_face(sz, j)]
        later_part += jnp.sum(mine * piece, axis=1, keepdims=True)
        cross_part += jnp.sum(mine * before[j] + earlier * piece, axis=1, keepdims=True)
    load = lax.broadcasted_iota(jnp.int32, (8, TILE), 0)
    line = jnp.where(lane == load, later_part, 0.0)
    line = jnp.where(lane == load + 8, cross_part, line)
    line = jnp.where(lane == load + 16, scalars[:, 2:3], line)
    spread(pay, jnp.sum(line, axis=0, keepdims=True))


def last_kernel(sz, pieces, scalars, estimate, direction, direction_rest, later, later_rest, out):
    totals = pieces[0]
    for k in range(1, pieces.shape[0]):
        totals = totals + pieces[k]
    curvature, previous = scalars[:, 0:1], scalars[:, 1:2]
    load = lax.broadcasted_iota(jnp.int32, (8, TILE), 0)
    later_part, cross_part, dot = [
        jnp.sum(jnp.where(lanes() == load + 8 * k, totals, 0.0), axis=1, keepdims=True)
        for k in range(3)
    ]
    ratio = dot / previous
    final = 2.0 * (later_part + ratio * cross_part) + ratio * ratio * curvature
    first, second = previous / curvature, dot / final
    both = zip(views(sz, direction, direction_rest), views(sz, later, later_rest))
    for (part, earlier), (_, mine) in both:
        here = part_slots(sz, part)
        moved = estimate[:, here] + first * earlier[...]
        out[0, 0, :, here] = moved + second * (mine[...] + ratio * earlier[...])


def shards(mesh_shape, operator, rhs_parts, stiffness, traces, coarse_inverse, rigid_loads,
           face_lengths, face_order, mode_count):
    sz = Sizes(mesh_shape, operator, traces, rhs_parts.shape[2])
    vmem = pl.BlockSpec(memory_space=pltpu.VMEM)
    smem = pl.BlockSpec(memory_space=pltpu.SMEM)
    hbm = pl.BlockSpec(memory_space=pltpu.HBM)
    everywhere = ("gx", "gy", "gz")
    small = sz.coarse_pad <= 256

    def call(kernel, out_shape, in_specs, scratch, *operands, limit=None, cost=None):
        return pl.pallas_call(
            functools.partial(kernel, sz),
            out_shape=out_shape,
            in_specs=in_specs,
            out_specs=jax.tree.map(lambda _: vmem, out_shape),
            scratch_shapes=scratch,
            cost_estimate=cost,
            compiler_params=pltpu.CompilerParams(
                vmem_limit_bytes=(limit or (16 if small else 56)) * MIB
            ),
        )(*operands)

    faces = sz.own_faces
    coarse = pltpu.VMEM((8, sz.coarse_pad), jnp.float32)
    square = pltpu.VMEM((sz.coarse_pad, sz.coarse_pad), jnp.float32)
    half, full, face = f32(8, sz.rows), f32(8, sz.order), f32(8, sz.cap)
    rounded_face = jax.ShapeDtypeStruct((8, sz.cap), jnp.bfloat16)
    blocks = operator.reshape(sz.rows // 8, 8, sz.order)
    one_step = sz.devices <= 64
    spread_tile = f32(sz.devices if one_step else 1, 4, TILE)
    apply_scratch = [
        pltpu.VMEM((8, sz.rows), jnp.float32),
        pltpu.VMEM((8, sz.order), jnp.bfloat16),
    ]
    copies = sz.rows // PIECE
    stream_scratch = [pltpu.VMEM((sz.rows // 8, 8, sz.order), jnp.bfloat16)] + apply_scratch
    stream_scratch += [pltpu.SemaphoreType.DMA((copies,))]

    def hold(after):
        return call(
            hold_kernel, jax.ShapeDtypeStruct((sz.rows // 8, 8, sz.order), jnp.bfloat16),
            [hbm, vmem], [pltpu.SemaphoreType.DMA((copies,))], blocks, after, limit=42,
            cost=pl.CostEstimate(flops=0, bytes_accessed=4 * sz.rows * sz.order, transcendentals=0),
        )

    def swap(own):
        return [lax.ppermute(own[j], everywhere, face_pairs(sz, j)) for j in range(faces)]

    def share(chunk, axes):
        if chunk.shape[0] == 1:
            return lax.all_gather(chunk, axes, axis=0, tiled=True)
        return lax.all_to_all(chunk, axes, split_axis=0, concat_axis=0, tiled=True)

    def rest(part):
        if sz.gz == 2:
            return lax.ppermute(part, "gz", [(0, 1), (1, 0)])
        return lax.all_gather(part, "gz", axis=0, tiled=False)

    *own, pay, base = call(
        start_kernel,
        [face] * faces + [f32(sz.subs if one_step else 1, 8, sz.coarse_pad), f32(24, sz.rows)],
        [hbm] * 8,
        [
            pltpu.VMEM((sz.modes, 1, sz.rows), jnp.float32),
            pltpu.VMEM((sz.modes, 1, sz.loads), jnp.float32),
            pltpu.VMEM((sz.modes, 1, sz.subs * sz.modes), jnp.float32),
            pltpu.VMEM((1, sz.rows), jnp.float32),
            pltpu.VMEM((4, sz.cap), jnp.int32),
            pltpu.SMEM((1, 1, 4), jnp.int32),
            pltpu.SMEM((1, 1), jnp.int32),
            pltpu.SemaphoreType.DMA((8,)),
        ],
        traces.reshape(sz.modes, 1, sz.order), rigid_loads.reshape(sz.modes, 1, sz.loads),
        coarse_inverse.reshape(sz.modes, 1, -1), stiffness, face_order, rhs_parts,
        face_lengths, mode_count, limit=60,
    )
    shared = share(pay, ("gx", "gy"))
    modes, right, coupling = call(
        modes_kernel, [f32(16, sz.rows), half, f32(8, TILE)], [vmem] * (1 + faces), [], base, *swap(own)
    )
    modes_rest = rest(modes)
    *own, pay, estimate = call(
        first_kernel, [face] * faces + [spread_tile, full], [hbm] + [vmem] * 5,
        [square, coarse] + stream_scratch,
        blocks, shared, right, coupling, modes, modes_rest, limit=50 if small else 56,
    )
    before = share(pay, everywhere)
    residual, direction = call(
        second_kernel, [half, half], [vmem] * (3 + 2 * faces), [square, square, coarse, coarse],
        before, shared, modes, *own, *swap(own),
    )
    direction_rest = rest(direction)
    *own, pay = call(
        second_apply_kernel, [rounded_face] * faces + [spread_tile], [vmem] * 5,
        apply_scratch, hold(direction), modes, residual, direction, direction_rest,
    )
    after = share(pay, everywhere)
    later, scalars = call(
        third_kernel, [half, f32(8, TILE)], [vmem] * (6 + 2 * faces),
        [square, square, coarse, coarse],
        after, shared, before, modes, residual, direction, *own, *swap(own),
    )
    later_rest = rest(later)
    pay = call(
        third_apply_kernel, f32(sz.devices if one_step else 1, 1, TILE),
        [vmem] * (5 + faces), apply_scratch,
        hold(later), direction, scalars, later, later_rest, *own,
    )
    return call(
        last_kernel, f32(1, 1, 8, sz.order), [vmem] * 7, [],
        share(pay, everywhere), scalars, estimate, direction, direction_rest, later, later_rest,
    )


def solution(mesh):
    in_specs = (
        P("gx", "gy", "gz", None),
        P("gx", "gy", None, None),
        P("gx", "gy", None),
        P("gx", "gy", None, None),
        P("gx", "gy", None, None),
        P("gx", "gy", None, None),
        P("gx", "gy", None),
        P("gx", "gy", None, None),
        P("gx", "gy"),
    )
    out_specs = P("gx", "gy", None, None)
    mesh_shape = tuple(mesh.shape[axis] for axis in ("gx", "gy", "gz"))
    return jax.shard_map(
        functools.partial(shards, mesh_shape),
        mesh=mesh, in_specs=in_specs, out_specs=out_specs, check_vma=False,
    )
```

```python
import functools

import jax
import jax.numpy as jnp
from jax import lax
from jax.experimental import pallas as pl
from jax.experimental.pallas import tpu as pltpu
from jax.sharding import PartitionSpec as P

ROW_CHUNK = 256
PIECE = 128
HOLD_PIECE = 64
LOAD_LANE = 6
TILE = 128
SLOT = 8
FOLD = TILE // 2
MIB = 1024 * 1024


class Sizes:
    def __init__(self, mesh_shape, operator, traces, loads):
        self.sx, self.sy, self.gz = mesh_shape
        self.rows = operator.shape[2]
        self.order = operator.shape[3]
        self.modes = traces.shape[2]
        self.cap = self.order // 4
        self.loads = loads
        self.subs = self.sx * self.sy
        self.devices = self.subs * self.gz
        self.coarse = self.subs * SLOT
        self.coarse_pad = -(-self.coarse // TILE) * TILE
        self.own_faces = self.rows // self.cap
        self.group = self.modes * (1 + self.own_faces)
        self.sums = 3 * self.group
        assert self.rows % self.cap == 0 and self.cap % TILE == 0
        assert self.modes <= SLOT - 2 and self.loads == 8 and self.sums + 2 <= FOLD


def f32(*shape):
    return jax.ShapeDtypeStruct(shape, jnp.float32)


def lanes(shape=(8, TILE)):
    return lax.broadcasted_iota(jnp.int32, shape, 1)


def exact_dot(a, b):
    return jnp.dot(a, b, precision=lax.Precision.HIGHEST, preferred_element_type=jnp.float32)


def clamp(index, count):
    return jnp.minimum(jnp.maximum(index, 0), count - 1)


def neighbour(sz, face):
    gx, gy = lax.axis_index("gx"), lax.axis_index("gy")
    x = gx + jnp.where(face == 0, -1, jnp.where(face == 1, 1, 0))
    y = gy + jnp.where(face == 2, -1, jnp.where(face == 3, 1, 0))
    return clamp(x, sz.sx) * sz.sy + clamp(y, sz.sy)


def grid_neighbour(sz, sub, face):
    x, y = divmod(sub, sz.sy)
    x, y = [(x - 1, y), (x + 1, y), (x, y - 1), (x, y + 1)][face]
    return x * sz.sy + y if 0 <= x < sz.sx and 0 <= y < sz.sy else None


def face_pairs(sz, slot):
    pairs = []
    for sub in range(sz.subs):
        for part in range(sz.gz):
            local = slot
            if sz.own_faces > 1:
                first = part * sz.own_faces + slot // 2 * 2
                index = divmod(sub, sz.sy)[first // 2]
                local = slot ^ index & 1
            face = part * sz.own_faces + local
            other = grid_neighbour(sz, sub, face)
            if other is not None:
                pairs.append((sub * sz.gz + part, other * sz.gz + (face ^ 1) // sz.own_faces))
    return pairs


def by_slot(sz, values):
    if sz.own_faces == 1:
        return values
    result = []
    for j in range(0, sz.own_faces, 2):
        first = lax.axis_index("gz") * sz.own_faces + j
        index = jnp.where(first < 2, lax.axis_index("gx"), lax.axis_index("gy"))
        even = lax.rem(index, 2) == 0
        low, high = values[j], values[j + 1]
        result += [jnp.where(even, low, high), jnp.where(even, high, low)]
    return result


def own_face(sz, j):
    return slice(j * sz.cap, (j + 1) * sz.cap)


def put_slots(sz, outs, values):
    for out, value in zip(outs, by_slot(sz, values)):
        out[...] = value


def get_slots(sz, refs):
    return by_slot(sz, [ref[...] for ref in refs])


def permuted(sz, block, slots):
    count = sz.cap // TILE
    pieces = [block[:, k * TILE : (k + 1) * TILE] for k in range(count)]
    result = []
    for j in range(count):
        index = jnp.broadcast_to(slots[:, j * TILE : (j + 1) * TILE], (8, TILE)).astype(jnp.int32)
        low = index & (TILE - 1)
        high = index >> (TILE.bit_length() - 1)
        total = jnp.zeros((8, TILE), jnp.float32)
        for k in range(count):
            picked = jnp.take_along_axis(pieces[k], low, axis=1, mode="promise_in_bounds")
            total = jnp.where(high == k, picked, total)
        result.append(total)
    return jnp.concatenate(result, axis=1)


def coefficients(sz, coarse_ref, sub):
    start = sub * SLOT
    base = pl.multiple_of((start // TILE) * TILE, TILE)
    tile = coarse_ref[:, pl.ds(base, TILE)]
    return pltpu.roll(tile, lax.rem(TILE - lax.rem(start, TILE), TILE), 1)


def views(sz, own, rest):
    if sz.gz == 2:
        gz = lax.axis_index("gz")
        return [(gz, own), (1 - gz, rest)]
    return [(z, rest.at[z]) for z in range(sz.gz)]


def mode_sum(sz, coarse_ref, mine, modes_ref, part, j):
    other = coefficients(sz, coarse_ref, neighbour(sz, part * sz.own_faces + j))
    total = None
    for tile, base in ((mine, 0), (other, SLOT)):
        for m in range(sz.modes):
            term = tile[:, m : m + 1] * modes_ref[base + m : base + m + 1, own_face(sz, j)]
            total = term if total is None else total + term
    return total


def own_coefficients(sz, coarse_ref):
    return coefficients(sz, coarse_ref, lax.axis_index("gx") * sz.sy + lax.axis_index("gy"))


def face_slots(sz, part, j):
    return pl.ds(pl.multiple_of(part * sz.rows + j * sz.cap, TILE), sz.cap)


def mode_products(sz, tile, blocks, modes_ref, first_lane):
    lane = lanes()
    for m in range(sz.modes):
        total = None
        for j, block in enumerate(blocks):
            term = jnp.sum(block * modes_ref[m : m + 1, own_face(sz, j)], axis=1, keepdims=True)
            total = term if total is None else total + term
        tile = jnp.where(lane == first_lane + m, total, tile)
    for j, block in enumerate(blocks):
        face_lane = first_lane + sz.modes * (1 + j)
        for m in range(sz.modes):
            row = modes_ref[SLOT + m : SLOT + m + 1, own_face(sz, j)]
            total = jnp.sum(block * row, axis=1, keepdims=True)
            tile = jnp.where(lane == face_lane + m, total, tile)
    return tile


def weights_of(sz, modes_ref):
    return [modes_ref[6:7, own_face(sz, j)] for j in range(sz.own_faces)]


def unfolded(tile):
    return jnp.concatenate([tile, pltpu.roll(tile, FOLD, 1)], axis=0)


def put_modes(sz, target, rows, tile, lane, sub):
    start = sub * SLOT
    base, offset = start // TILE * TILE, start % TILE
    moved = pltpu.roll(tile, (offset - lane) % TILE, 1)
    wanted = (lanes() >= offset) & (lanes() < offset + sz.modes)
    target[rows, base : base + TILE] += jnp.where(wanted, moved, 0.0)


def fill_coupling(sz, pieces, coupling_ref):
    coupling_ref[...] = jnp.zeros((sz.coarse_pad, sz.coarse_pad), jnp.float32)
    for sub in range(sz.subs):
        rows = slice(sub * SLOT, (sub + 1) * SLOT)
        parts = [unfolded(pieces[sub * sz.gz + z]) for z in range(sz.gz)]
        own = parts[0]
        for part in parts[1:]:
            own = own + part
        put_modes(sz, coupling_ref, rows, own, 2 * sz.group, sub)
        for face in range(4):
            other = grid_neighbour(sz, sub, face)
            if other is not None:
                part, j = divmod(face, sz.own_faces)
                lane = 2 * sz.group + sz.modes * (1 + j)
                put_modes(sz, coupling_ref, rows, parts[part], lane, other)


def fill_inverse(sz, shared, inverse_ref):
    if sz.coarse_pad > sz.coarse:
        inverse_ref[sz.coarse :, :] = jnp.zeros((sz.coarse_pad - sz.coarse, sz.coarse_pad), jnp.float32)
    for sub in range(sz.subs):
        inverse_ref[sub * SLOT : (sub + 1) * SLOT, :] = shared[sub]


def solve_pair(sz, pieces, inverse_ref, coupling_ref, coarse_a, coarse_b):
    coarse_a[...] = jnp.zeros((8, sz.coarse_pad), jnp.float32)
    coarse_b[...] = jnp.zeros((8, sz.coarse_pad), jnp.float32)
    for sub in range(sz.subs):
        total = pieces[sub * sz.gz]
        for part in range(1, sz.gz):
            total = total + pieces[sub * sz.gz + part]
        for face in range(4):
            other = grid_neighbour(sz, sub, face)
            if other is not None:
                part, j = divmod(face ^ 1, sz.own_faces)
                moved = pltpu.roll(pieces[other * sz.gz + part], TILE - sz.modes * (1 + j), 1)
                total = total + moved
        total = unfolded(total)
        put_modes(sz, coarse_a, slice(0, 8), total, 0, sub)
        put_modes(sz, coarse_b, slice(0, 8), total, sz.group, sub)
    first = exact_dot(coarse_a[...], inverse_ref[...])
    coarse_a[...] = first
    coarse_b[...] = exact_dot(coarse_b[...] - exact_dot(first, coupling_ref[...]), inverse_ref[...])


def spread(out, tile):
    out[...] = jnp.broadcast_to(tile[None], out.shape)


def spread_folded(out, tile):
    spread(out, tile[0:4] + pltpu.roll(tile[4:8], FOLD, 1))


def multiply(sz, vector, rows, product, k):
    part = lax.dot_general(
        vector[...], rows.reshape(ROW_CHUNK, sz.order), (((1,), (1,)), ((), ())),
        preferred_element_type=jnp.float32,
    )
    here = pl.ds(pl.multiple_of(k * ROW_CHUNK, TILE), ROW_CHUNK)
    product[:, here] = part.astype(jnp.bfloat16).astype(jnp.float32)


class Stream:
    def __init__(self, sz, operator, held, product, sems):
        self.sz, self.operator, self.held, self.product, self.sems = sz, operator, held, product, sems
        for p in range(sz.rows // PIECE):
            self.copy(p).start()

    def copy(self, p):
        here = pl.ds(p * (PIECE // 8), PIECE // 8)
        return pltpu.make_async_copy(self.operator.at[here], self.held.at[here], self.sems.at[p])

    def apply(self, vector):
        sz, step, blocks = self.sz, ROW_CHUNK // PIECE, ROW_CHUNK // 8

        def chunk(k, carry):
            for p in range(step):
                self.copy(k * step + p).wait()
            multiply(sz, vector, self.held[pl.ds(k * blocks, blocks)], self.product, k)
            return carry

        lax.fori_loop(0, sz.rows // ROW_CHUNK, chunk, 0)
        return [self.product[:, own_face(sz, j)] for j in range(sz.own_faces)]


def apply_held(sz, vector, held, product):
    blocks = ROW_CHUNK // 8
    for k in range(sz.rows // ROW_CHUNK):
        multiply(sz, vector, held[k * blocks : (k + 1) * blocks], product, k)
    return [product[:, own_face(sz, j)] for j in range(sz.own_faces)]


def hold_kernel(sz, operator, after, held, sems):
    del after
    blocks = HOLD_PIECE // 8
    copies = []
    for k in range(sz.rows // HOLD_PIECE):
        here = pl.ds(k * blocks, blocks)
        copies.append(pltpu.make_async_copy(operator.at[here], held.at[here], sems.at[k]))
        copies[-1].start()
    for copy in copies:
        copy.wait()


def part_slots(sz, part):
    return pl.ds(pl.multiple_of(part * sz.rows, TILE), sz.rows)


def put_parts(sz, own, rest, vector):
    for part, ref in views(sz, own, rest):
        vector[:, part_slots(sz, part)] = ref[...].astype(vector.dtype)


def start_kernel(sz, traces, loads, inverse, stiffness, orders, rhs, lengths, count, *refs):
    outs, scratch = refs[: sz.own_faces + 2], refs[sz.own_faces + 2 :]
    faces, (pay, base) = outs[: sz.own_faces], outs[sz.own_faces :]
    traces_in, loads_in, inverse_in, stiffness_in, slots, lengths_in, count_in, sems = scratch
    gz = lax.axis_index("gz")
    here = pl.ds(pl.multiple_of(gz * sz.rows, TILE), sz.rows)
    copies = [
        pltpu.make_async_copy(inverse, inverse_in, sems.at[0]),
        pltpu.make_async_copy(loads, loads_in, sems.at[1]),
        pltpu.make_async_copy(traces.at[:, :, here], traces_in, sems.at[2]),
        pltpu.make_async_copy(stiffness.at[0, :, here], stiffness_in, sems.at[3]),
        pltpu.make_async_copy(orders.at[0, 0], slots, sems.at[4]),
        pltpu.make_async_copy(rhs.at[0, 0, :, here], base.at[pl.ds(8, 8), :], sems.at[5]),
        pltpu.make_async_copy(lengths, lengths_in, sems.at[6]),
        pltpu.make_async_copy(count, count_in, sems.at[7]),
    ]
    for copy in copies:
        copy.start()
    pay[...] = jnp.zeros(pay.shape, jnp.float32)
    base[sz.modes : 8, :] = jnp.zeros((8 - sz.modes, sz.rows), jnp.float32)
    for copy in copies:
        copy.wait()
    for m in range(sz.modes):
        mask = (m < count_in[0, 0]).astype(jnp.float32)
        for t in range(sz.subs):
            pay[0, m : m + 1, t * SLOT : t * SLOT + sz.modes] = inverse_in[
                m, :, t * sz.modes : (t + 1) * sz.modes
            ]
        loads_row = loads_in[m] * mask
        row = pay[0, m : m + 1, 0:TILE]
        for load in range(sz.loads):
            row = jnp.where(lanes((1, TILE)) == SLOT * load + LOAD_LANE, loads_row[:, load : load + 1], row)
        pay[0, m : m + 1, 0:TILE] = row
        base[m : m + 1, :] = traces_in[m] * mask
    position = lax.broadcasted_iota(jnp.int32, (1, sz.cap), 1)
    base[6:7, :] = stiffness_in[...]
    for j in range(sz.own_faces):
        index = gz * sz.own_faces + j
        base[7:8, own_face(sz, j)] = (position < lengths_in[0, 0, index]).astype(jnp.float32)
        chosen = jnp.broadcast_to(slots[pl.ds(index, 1), :], (8, sz.cap))
        base[16:24, own_face(sz, j)] = chosen.astype(jnp.float32)
    put_slots(sz, faces, [base[0:8, own_face(sz, j)] for j in range(sz.own_faces)])
    chunk = pay[0]
    for k in range(1, pay.shape[0]):
        pay[k] = chunk


def modes_kernel(sz, base, *refs):
    arrived, (modes_ref, right, coupling) = refs[: sz.own_faces], refs[sz.own_faces :]
    right[...] = base[8:16, :]
    row = lax.broadcasted_iota(jnp.int32, (8, 1), 0)
    arrived = get_slots(sz, arrived)
    for j in range(sz.own_faces):
        here = own_face(sz, j)
        other = permuted(sz, arrived[j], base[16:24, here])
        mine = base[0:8, here]
        live = mine[7:8, :]
        total = live * (mine[6:7, :] + other[6:7, :])
        weight = live / (total + 1.0 - live)
        modes_ref[0:8, here] = jnp.where(row == 6, weight, jnp.where(row == 7, live, mine * live))
        slots_row = jnp.where(row == 6, base[16:24, here], 0.0)
        modes_ref[8:16, here] = jnp.where(row < sz.modes, other * live, slots_row)
    weights = weights_of(sz, modes_ref)
    coarse_rows = [
        jnp.where(row < sz.modes, modes_ref[0:8, own_face(sz, j)] * weights[j], 0.0)
        for j in range(sz.own_faces)
    ]
    tile = jnp.zeros((8, TILE), jnp.float32)
    coupling[...] = mode_products(sz, tile, coarse_rows, modes_ref, 2 * sz.group)


def assembled(sz, own, arrived, modes_ref, j):
    here = own_face(sz, j)
    return modes_ref[7:8, here] * (own[j] + permuted(sz, arrived[j], modes_ref[14:15, here]))


def tile_products(sz, tile, vectors, modes_ref):
    tile = mode_products(sz, tile, vectors, modes_ref, 0)
    scaled = [v * w for v, w in zip(vectors, weights_of(sz, modes_ref))]
    return mode_products(sz, tile, scaled, modes_ref, sz.group)


def first_kernel(sz, operator, shared, right, coupling, modes_ref, modes_rest, *refs):
    outs, refs = refs[: sz.own_faces], refs[sz.own_faces :]
    pay, estimate_ref, inverse_ref, coarse_ref, held, product, vector, sems = refs
    stream = Stream(sz, operator, held, product, sems)
    fill_inverse(sz, shared, inverse_ref)
    turned = []
    for k in range(sz.coarse_pad // TILE):
        block = jnp.transpose(inverse_ref[k * TILE : (k + 1) * TILE, 0:TILE])
        rows = [SLOT * load + LOAD_LANE for load in range(sz.loads)]
        turned.append(jnp.concatenate([block[r : r + 1] for r in rows], axis=0))
    coarse_ref[...] = exact_dot(jnp.concatenate(turned, axis=1), inverse_ref[...])
    mine = own_coefficients(sz, coarse_ref)
    for part, modes in views(sz, modes_ref, modes_rest):
        for j in range(sz.own_faces):
            here = face_slots(sz, part, j)
            estimate = mode_sum(sz, coarse_ref, mine, modes, part, j)
            estimate_ref[:, here] = estimate
            vector[:, here] = estimate.astype(jnp.bfloat16)
    pieces = stream.apply(vector)
    vectors = [right[:, own_face(sz, j)] - piece for j, piece in enumerate(pieces)]
    put_slots(sz, outs, vectors)
    spread_folded(pay, tile_products(sz, coupling[...], vectors, modes_ref))


def second_kernel(sz, pieces, shared, modes_ref, *refs):
    own, refs = get_slots(sz, refs[: sz.own_faces]), refs[sz.own_faces :]
    arrived, refs = get_slots(sz, refs[: sz.own_faces]), refs[sz.own_faces :]
    residual_ref, direction_ref, inverse_ref, coupling_ref, coarse_a, coarse_b = refs
    gz = lax.axis_index("gz")
    fill_inverse(sz, shared, inverse_ref)
    fill_coupling(sz, pieces, coupling_ref)
    solve_pair(sz, pieces, inverse_ref, coupling_ref, coarse_a, coarse_b)
    first, second = own_coefficients(sz, coarse_a), own_coefficients(sz, coarse_b)
    for j in range(sz.own_faces):
        here = own_face(sz, j)
        gap = assembled(sz, own, arrived, modes_ref, j)
        residual = gap - mode_sum(sz, coarse_a, first, modes_ref, gz, j)
        residual_ref[:, here] = residual
        correction = mode_sum(sz, coarse_b, second, modes_ref, gz, j)
        direction_ref[:, here] = modes_ref[6:7, here] * residual - correction


def second_apply_kernel(sz, held, modes_ref, residual, direction, rest, *refs):
    outs, refs = refs[: sz.own_faces], refs[sz.own_faces :]
    pay, product, vector = refs
    put_parts(sz, direction, rest, vector)
    weights = weights_of(sz, modes_ref)
    lane = lanes()
    curvature = jnp.zeros((8, 1), jnp.float32)
    resid_dot = jnp.zeros((8, 1), jnp.float32)
    pieces = apply_held(sz, vector, held, product)
    put_slots(sz, outs, pieces)
    for j, piece in enumerate(pieces):
        here = own_face(sz, j)
        own = residual[:, here]
        resid_dot += jnp.sum(own * (weights[j] * own), axis=1, keepdims=True)
        curvature += jnp.sum(direction[:, here] * piece, axis=1, keepdims=True)
    tile = jnp.where(lane == sz.sums, curvature, jnp.zeros((8, TILE), jnp.float32))
    tile = jnp.where(lane == sz.sums + 1, resid_dot, tile)
    spread_folded(pay, tile_products(sz, tile, pieces, modes_ref))


def third_kernel(sz, pieces, shared, before, modes_ref, residual_ref, direction_ref, *refs):
    own, refs = get_slots(sz, refs[: sz.own_faces]), refs[sz.own_faces :]
    arrived, refs = get_slots(sz, refs[: sz.own_faces]), refs[sz.own_faces :]
    later_ref, scalars_ref, inverse_ref, coupling_ref, coarse_a, coarse_b = refs
    gz = lax.axis_index("gz")
    lane = lanes()
    fill_inverse(sz, shared, inverse_ref)
    fill_coupling(sz, before, coupling_ref)
    totals = pieces[0]
    for k in range(1, sz.devices):
        totals = totals + pieces[k]
    totals = unfolded(totals)
    curvature = 2.0 * totals[:, sz.sums : sz.sums + 1]
    resid_dot = totals[:, sz.sums + 1 : sz.sums + 2]
    step = resid_dot / curvature
    solve_pair(sz, pieces, inverse_ref, coupling_ref, coarse_a, coarse_b)
    first, second = own_coefficients(sz, coarse_a), own_coefficients(sz, coarse_b)
    dot_part = jnp.zeros((8, 1), jnp.float32)
    for j in range(sz.own_faces):
        here = own_face(sz, j)
        image = assembled(sz, own, arrived, modes_ref, j)
        corrected = image - mode_sum(sz, coarse_a, first, modes_ref, gz, j)
        weight = modes_ref[6:7, here]
        scaled = weight * corrected - mode_sum(sz, coarse_b, second, modes_ref, gz, j)
        residual = residual_ref[:, here] - step * corrected
        dot_part += jnp.sum(residual * (weight * residual), axis=1, keepdims=True)
        later_ref[:, here] = direction_ref[:, here] - step * scaled
    scalars_ref[...] = jnp.where(lane == 0, curvature, jnp.where(lane == 1, resid_dot, dot_part))


def third_apply_kernel(sz, held, direction, scalars, later, rest, *refs):
    before, refs = get_slots(sz, refs[: sz.own_faces]), refs[sz.own_faces :]
    pay, product, vector = refs
    put_parts(sz, later, rest, vector)
    pieces = apply_held(sz, vector, held, product)
    lane = lanes()
    later_part = jnp.zeros((8, 1), jnp.float32)
    cross_part = jnp.zeros((8, 1), jnp.float32)
    for j, piece in enumerate(pieces):
        mine = later[:, own_face(sz, j)]
        earlier = direction[:, own_face(sz, j)]
        later_part += jnp.sum(mine * piece, axis=1, keepdims=True)
        cross_part += jnp.sum(mine * before[j] + earlier * piece, axis=1, keepdims=True)
    load = lax.broadcasted_iota(jnp.int32, (8, TILE), 0)
    line = jnp.where(lane == load, later_part, 0.0)
    line = jnp.where(lane == load + 8, cross_part, line)
    line = jnp.where(lane == load + 16, scalars[:, 2:3], line)
    spread(pay, jnp.sum(line, axis=0, keepdims=True))


def last_kernel(sz, pieces, scalars, estimate, direction, direction_rest, later, later_rest, out):
    totals = pieces[0]
    for k in range(1, pieces.shape[0]):
        totals = totals + pieces[k]
    curvature, previous = scalars[:, 0:1], scalars[:, 1:2]
    load = lax.broadcasted_iota(jnp.int32, (8, TILE), 0)
    later_part, cross_part, dot = [
        jnp.sum(jnp.where(lanes() == load + 8 * k, totals, 0.0), axis=1, keepdims=True)
        for k in range(3)
    ]
    ratio = dot / previous
    final = 2.0 * (later_part + ratio * cross_part) + ratio * ratio * curvature
    first, second = previous / curvature, dot / final
    both = zip(views(sz, direction, direction_rest), views(sz, later, later_rest))
    for (part, earlier), (_, mine) in both:
        here = part_slots(sz, part)
        moved = estimate[:, here] + first * earlier[...]
        out[0, 0, :, here] = moved + second * (mine[...] + ratio * earlier[...])


def shards(mesh_shape, operator, rhs_parts, stiffness, traces, coarse_inverse, rigid_loads,
           face_lengths, face_order, mode_count):
    sz = Sizes(mesh_shape, operator, traces, rhs_parts.shape[2])
    vmem = pl.BlockSpec(memory_space=pltpu.VMEM)
    smem = pl.BlockSpec(memory_space=pltpu.SMEM)
    hbm = pl.BlockSpec(memory_space=pltpu.HBM)
    everywhere = ("gx", "gy", "gz")
    small = sz.coarse_pad <= 256

    def call(kernel, out_shape, in_specs, scratch, *operands, limit=None, cost=None):
        return pl.pallas_call(
            functools.partial(kernel, sz),
            out_shape=out_shape,
            in_specs=in_specs,
            out_specs=jax.tree.map(lambda _: vmem, out_shape),
            scratch_shapes=scratch,
            cost_estimate=cost,
            compiler_params=pltpu.CompilerParams(
                vmem_limit_bytes=(limit or (16 if small else 56)) * MIB
            ),
        )(*operands)

    faces = sz.own_faces
    coarse = pltpu.VMEM((8, sz.coarse_pad), jnp.float32)
    square = pltpu.VMEM((sz.coarse_pad, sz.coarse_pad), jnp.float32)
    half, full, face = f32(8, sz.rows), f32(8, sz.order), f32(8, sz.cap)
    blocks = operator.reshape(sz.rows // 8, 8, sz.order)
    one_step = sz.devices <= 64
    spread_tile = f32(sz.devices if one_step else 1, 4, TILE)
    apply_scratch = [
        pltpu.VMEM((8, sz.rows), jnp.float32),
        pltpu.VMEM((8, sz.order), jnp.bfloat16),
    ]
    copies = sz.rows // PIECE
    stream_scratch = [pltpu.VMEM((sz.rows // 8, 8, sz.order), jnp.bfloat16)] + apply_scratch
    stream_scratch += [pltpu.SemaphoreType.DMA((copies,))]

    def hold(after):
        return call(
            hold_kernel, jax.ShapeDtypeStruct((sz.rows // 8, 8, sz.order), jnp.bfloat16),
            [hbm, vmem], [pltpu.SemaphoreType.DMA((sz.rows // HOLD_PIECE,))], blocks, after, limit=42,
            cost=pl.CostEstimate(flops=0, bytes_accessed=4 * sz.rows * sz.order, transcendentals=0),
        )

    def swap(own):
        return [lax.ppermute(own[j], everywhere, face_pairs(sz, j)) for j in range(faces)]

    def share(chunk, axes):
        if chunk.shape[0] == 1:
            return lax.all_gather(chunk, axes, axis=0, tiled=True)
        return lax.all_to_all(chunk, axes, split_axis=0, concat_axis=0, tiled=True)

    def rest(part):
        if sz.gz == 2:
            return lax.ppermute(part, "gz", [(0, 1), (1, 0)])
        return lax.all_gather(part, "gz", axis=0, tiled=False)

    *own, pay, base = call(
        start_kernel,
        [face] * faces + [f32(sz.subs if one_step else 1, 8, sz.coarse_pad), f32(24, sz.rows)],
        [hbm] * 8,
        [
            pltpu.VMEM((sz.modes, 1, sz.rows), jnp.float32),
            pltpu.VMEM((sz.modes, 1, sz.loads), jnp.float32),
            pltpu.VMEM((sz.modes, 1, sz.subs * sz.modes), jnp.float32),
            pltpu.VMEM((1, sz.rows), jnp.float32),
            pltpu.VMEM((4, sz.cap), jnp.int32),
            pltpu.SMEM((1, 1, 4), jnp.int32),
            pltpu.SMEM((1, 1), jnp.int32),
            pltpu.SemaphoreType.DMA((8,)),
        ],
        traces.reshape(sz.modes, 1, sz.order), rigid_loads.reshape(sz.modes, 1, sz.loads),
        coarse_inverse.reshape(sz.modes, 1, -1), stiffness, face_order, rhs_parts,
        face_lengths, mode_count, limit=60,
    )
    shared = share(pay, ("gx", "gy"))
    modes, right, coupling = call(
        modes_kernel, [f32(16, sz.rows), half, f32(8, TILE)], [vmem] * (1 + faces), [], base, *swap(own)
    )
    modes_rest = rest(modes)
    *own, pay, estimate = call(
        first_kernel, [face] * faces + [spread_tile, full], [hbm] + [vmem] * 5,
        [square, coarse] + stream_scratch,
        blocks, shared, right, coupling, modes, modes_rest, limit=50 if small else 56,
    )
    before = share(pay, everywhere)
    residual, direction = call(
        second_kernel, [half, half], [vmem] * (3 + 2 * faces), [square, square, coarse, coarse],
        before, shared, modes, *own, *swap(own),
    )
    direction_rest = rest(direction)
    *own, pay = call(
        second_apply_kernel, [face] * faces + [spread_tile], [vmem] * 5,
        apply_scratch, hold(direction), modes, residual, direction, direction_rest,
    )
    after = share(pay, everywhere)
    later, scalars = call(
        third_kernel, [half, f32(8, TILE)], [vmem] * (6 + 2 * faces),
        [square, square, coarse, coarse],
        after, shared, before, modes, residual, direction, *own, *swap(own),
    )
    later_rest = rest(later)
    pay = call(
        third_apply_kernel, f32(sz.devices if one_step else 1, 1, TILE),
        [vmem] * (5 + faces), apply_scratch,
        hold(later), direction, scalars, later, later_rest, *own,
    )
    return call(
        last_kernel, f32(1, 1, 8, sz.order), [vmem] * 7, [],
        share(pay, everywhere), scalars, estimate, direction, direction_rest, later, later_rest,
    )


def solution(mesh):
    in_specs = (
        P("gx", "gy", "gz", None),
        P("gx", "gy", None, None),
        P("gx", "gy", None),
        P("gx", "gy", None, None),
        P("gx", "gy", None, None),
        P("gx", "gy", None, None),
        P("gx", "gy", None),
        P("gx", "gy", None, None),
        P("gx", "gy"),
    )
    out_specs = P("gx", "gy", None, None)
    mesh_shape = tuple(mesh.shape[axis] for axis in ("gx", "gy", "gz"))
    return jax.shard_map(
        functools.partial(shards, mesh_shape),
        mesh=mesh, in_specs=in_specs, out_specs=out_specs, check_vma=False,
    )
```

```python
import functools

import jax
import jax.numpy as jnp
from jax import lax
from jax.experimental import pallas as pl
from jax.experimental.pallas import tpu as pltpu
from jax.sharding import PartitionSpec as P

ROW_CHUNK = 256
PIECE = 128
LOAD_LANE = 6
TILE = 128
SLOT = 8
FOLD = TILE // 2
MIB = 1024 * 1024


class Sizes:
    def __init__(self, mesh_shape, operator, traces, loads):
        self.sx, self.sy, self.gz = mesh_shape
        self.rows = operator.shape[2]
        self.order = operator.shape[3]
        self.modes = traces.shape[2]
        self.cap = self.order // 4
        self.loads = loads
        self.subs = self.sx * self.sy
        self.devices = self.subs * self.gz
        self.coarse = self.subs * SLOT
        self.coarse_pad = -(-self.coarse // TILE) * TILE
        self.own_faces = self.rows // self.cap
        self.group = self.modes * (1 + self.own_faces)
        self.sums = 3 * self.group
        assert self.rows % self.cap == 0 and self.cap % TILE == 0
        assert self.modes <= SLOT - 2 and self.loads == 8 and self.sums + 2 <= FOLD


def f32(*shape):
    return jax.ShapeDtypeStruct(shape, jnp.float32)


def lanes(shape=(8, TILE)):
    return lax.broadcasted_iota(jnp.int32, shape, 1)


def exact_dot(a, b):
    return jnp.dot(a, b, precision=lax.Precision.HIGHEST, preferred_element_type=jnp.float32)


def clamp(index, count):
    return jnp.minimum(jnp.maximum(index, 0), count - 1)


def neighbour(sz, face):
    gx, gy = lax.axis_index("gx"), lax.axis_index("gy")
    x = gx + jnp.where(face == 0, -1, jnp.where(face == 1, 1, 0))
    y = gy + jnp.where(face == 2, -1, jnp.where(face == 3, 1, 0))
    return clamp(x, sz.sx) * sz.sy + clamp(y, sz.sy)


def grid_neighbour(sz, sub, face):
    x, y = divmod(sub, sz.sy)
    x, y = [(x - 1, y), (x + 1, y), (x, y - 1), (x, y + 1)][face]
    return x * sz.sy + y if 0 <= x < sz.sx and 0 <= y < sz.sy else None


def face_pairs(sz, slot):
    pairs = []
    for sub in range(sz.subs):
        for part in range(sz.gz):
            local = slot
            if sz.own_faces > 1:
                first = part * sz.own_faces + slot // 2 * 2
                index = divmod(sub, sz.sy)[first // 2]
                local = slot ^ index & 1
            face = part * sz.own_faces + local
            other = grid_neighbour(sz, sub, face)
            if other is not None:
                pairs.append((sub * sz.gz + part, other * sz.gz + (face ^ 1) // sz.own_faces))
    return pairs


def by_slot(sz, values):
    if sz.own_faces == 1:
        return values
    result = []
    for j in range(0, sz.own_faces, 2):
        first = lax.axis_index("gz") * sz.own_faces + j
        index = jnp.where(first < 2, lax.axis_index("gx"), lax.axis_index("gy"))
        even = lax.rem(index, 2) == 0
        low, high = values[j], values[j + 1]
        result += [jnp.where(even, low, high), jnp.where(even, high, low)]
    return result


def own_face(sz, j):
    return slice(j * sz.cap, (j + 1) * sz.cap)


def put_slots(sz, outs, values):
    for out, value in zip(outs, by_slot(sz, values)):
        out[...] = value


def get_slots(sz, refs):
    return by_slot(sz, [ref[...] for ref in refs])


def permuted(sz, block, slots):
    count = sz.cap // TILE
    pieces = [block[:, k * TILE : (k + 1) * TILE] for k in range(count)]
    result = []
    for j in range(count):
        index = jnp.broadcast_to(slots[:, j * TILE : (j + 1) * TILE], (8, TILE)).astype(jnp.int32)
        low = index & (TILE - 1)
        high = index >> (TILE.bit_length() - 1)
        total = jnp.zeros((8, TILE), jnp.float32)
        for k in range(count):
            picked = jnp.take_along_axis(pieces[k], low, axis=1, mode="promise_in_bounds")
            total = jnp.where(high == k, picked, total)
        result.append(total)
    return jnp.concatenate(result, axis=1)


def coefficients(sz, coarse_ref, sub):
    start = sub * SLOT
    base = pl.multiple_of((start // TILE) * TILE, TILE)
    tile = coarse_ref[:, pl.ds(base, TILE)]
    return pltpu.roll(tile, lax.rem(TILE - lax.rem(start, TILE), TILE), 1)


def views(sz, own, rest):
    if sz.gz == 2:
        gz = lax.axis_index("gz")
        return [(gz, own), (1 - gz, rest)]
    return [(z, rest.at[z]) for z in range(sz.gz)]


def mode_sum(sz, coarse_ref, mine, modes_ref, part, j):
    other = coefficients(sz, coarse_ref, neighbour(sz, part * sz.own_faces + j))
    total = None
    for tile, base in ((mine, 0), (other, SLOT)):
        for m in range(sz.modes):
            term = tile[:, m : m + 1] * modes_ref[base + m : base + m + 1, own_face(sz, j)]
            total = term if total is None else total + term
    return total


def own_coefficients(sz, coarse_ref):
    return coefficients(sz, coarse_ref, lax.axis_index("gx") * sz.sy + lax.axis_index("gy"))


def face_slots(sz, part, j):
    return pl.ds(pl.multiple_of(part * sz.rows + j * sz.cap, TILE), sz.cap)


def mode_products(sz, tile, blocks, modes_ref, first_lane):
    lane = lanes()
    for m in range(sz.modes):
        total = None
        for j, block in enumerate(blocks):
            term = jnp.sum(block * modes_ref[m : m + 1, own_face(sz, j)], axis=1, keepdims=True)
            total = term if total is None else total + term
        tile = jnp.where(lane == first_lane + m, total, tile)
    for j, block in enumerate(blocks):
        face_lane = first_lane + sz.modes * (1 + j)
        for m in range(sz.modes):
            row = modes_ref[SLOT + m : SLOT + m + 1, own_face(sz, j)]
            total = jnp.sum(block * row, axis=1, keepdims=True)
            tile = jnp.where(lane == face_lane + m, total, tile)
    return tile


def weights_of(sz, modes_ref):
    return [modes_ref[6:7, own_face(sz, j)] for j in range(sz.own_faces)]


def unfolded(tile):
    return jnp.concatenate([tile, pltpu.roll(tile, FOLD, 1)], axis=0)


def put_modes(sz, target, rows, tile, lane, sub):
    start = sub * SLOT
    base, offset = start // TILE * TILE, start % TILE
    moved = pltpu.roll(tile, (offset - lane) % TILE, 1)
    wanted = (lanes() >= offset) & (lanes() < offset + sz.modes)
    target[rows, base : base + TILE] += jnp.where(wanted, moved, 0.0)


def fill_coupling(sz, pieces, coupling_ref):
    coupling_ref[...] = jnp.zeros((sz.coarse_pad, sz.coarse_pad), jnp.float32)
    for sub in range(sz.subs):
        rows = slice(sub * SLOT, (sub + 1) * SLOT)
        parts = [unfolded(pieces[sub * sz.gz + z]) for z in range(sz.gz)]
        own = parts[0]
        for part in parts[1:]:
            own = own + part
        put_modes(sz, coupling_ref, rows, own, 2 * sz.group, sub)
        for face in range(4):
            other = grid_neighbour(sz, sub, face)
            if other is not None:
                part, j = divmod(face, sz.own_faces)
                lane = 2 * sz.group + sz.modes * (1 + j)
                put_modes(sz, coupling_ref, rows, parts[part], lane, other)


def fill_inverse(sz, shared, inverse_ref):
    if sz.coarse_pad > sz.coarse:
        inverse_ref[sz.coarse :, :] = jnp.zeros((sz.coarse_pad - sz.coarse, sz.coarse_pad), jnp.float32)
    for sub in range(sz.subs):
        inverse_ref[sub * SLOT : (sub + 1) * SLOT, :] = shared[sub]


def solve_pair(sz, pieces, inverse_ref, coupling_ref, coarse_a, coarse_b):
    coarse_a[...] = jnp.zeros((8, sz.coarse_pad), jnp.float32)
    coarse_b[...] = jnp.zeros((8, sz.coarse_pad), jnp.float32)
    for sub in range(sz.subs):
        total = pieces[sub * sz.gz]
        for part in range(1, sz.gz):
            total = total + pieces[sub * sz.gz + part]
        for face in range(4):
            other = grid_neighbour(sz, sub, face)
            if other is not None:
                part, j = divmod(face ^ 1, sz.own_faces)
                moved = pltpu.roll(pieces[other * sz.gz + part], TILE - sz.modes * (1 + j), 1)
                total = total + moved
        total = unfolded(total)
        put_modes(sz, coarse_a, slice(0, 8), total, 0, sub)
        put_modes(sz, coarse_b, slice(0, 8), total, sz.group, sub)
    first = exact_dot(coarse_a[...], inverse_ref[...])
    coarse_a[...] = first
    coarse_b[...] = exact_dot(coarse_b[...] - exact_dot(first, coupling_ref[...]), inverse_ref[...])


def spread(out, tile):
    out[...] = jnp.broadcast_to(tile[None], out.shape)


def spread_folded(out, tile):
    spread(out, tile[0:4] + pltpu.roll(tile[4:8], FOLD, 1))


def multiply(sz, vector, rows, product, k):
    part = lax.dot_general(
        vector[...], rows.reshape(ROW_CHUNK, sz.order), (((1,), (1,)), ((), ())),
        preferred_element_type=jnp.float32,
    )
    here = pl.ds(pl.multiple_of(k * ROW_CHUNK, TILE), ROW_CHUNK)
    product[:, here] = part.astype(jnp.bfloat16).astype(jnp.float32)


class Stream:
    def __init__(self, sz, operator, held, product, sems):
        self.sz, self.operator, self.held, self.product, self.sems = sz, operator, held, product, sems
        for p in range(sz.rows // PIECE):
            self.copy(p).start()

    def copy(self, p):
        here = pl.ds(p * (PIECE // 8), PIECE // 8)
        return pltpu.make_async_copy(self.operator.at[here], self.held.at[here], self.sems.at[p])

    def apply(self, vector):
        sz, step, blocks = self.sz, ROW_CHUNK // PIECE, ROW_CHUNK // 8

        def chunk(k, carry):
            for p in range(step):
                self.copy(k * step + p).wait()
            multiply(sz, vector, self.held[pl.ds(k * blocks, blocks)], self.product, k)
            return carry

        lax.fori_loop(0, sz.rows // ROW_CHUNK, chunk, 0)
        return [self.product[:, own_face(sz, j)] for j in range(sz.own_faces)]


def apply_held(sz, vector, held, product):
    blocks = ROW_CHUNK // 8
    for k in range(sz.rows // ROW_CHUNK):
        multiply(sz, vector, held[k * blocks : (k + 1) * blocks], product, k)
    return [product[:, own_face(sz, j)] for j in range(sz.own_faces)]


def hold_kernel(sz, operator, after, held, sems):
    del after
    blocks = ROW_CHUNK // 8
    copies = []
    for k in range(sz.rows // ROW_CHUNK):
        here = pl.ds(k * blocks, blocks)
        copies.append(pltpu.make_async_copy(operator.at[here], held.at[here], sems.at[k]))
        copies[-1].start()
    for copy in copies:
        copy.wait()


def part_slots(sz, part):
    return pl.ds(pl.multiple_of(part * sz.rows, TILE), sz.rows)


def put_parts(sz, own, rest, vector):
    for part, ref in views(sz, own, rest):
        vector[:, part_slots(sz, part)] = ref[...].astype(vector.dtype)


def start_kernel(sz, traces, loads, inverse, stiffness, orders, rhs, lengths, count, *refs):
    outs, scratch = refs[: sz.own_faces + 2], refs[sz.own_faces + 2 :]
    faces, (pay, base) = outs[: sz.own_faces], outs[sz.own_faces :]
    traces_in, loads_in, inverse_in, stiffness_in, slots, lengths_in, count_in, sems = scratch
    gz = lax.axis_index("gz")
    here = pl.ds(pl.multiple_of(gz * sz.rows, TILE), sz.rows)
    copies = [
        pltpu.make_async_copy(inverse, inverse_in, sems.at[0]),
        pltpu.make_async_copy(loads, loads_in, sems.at[1]),
        pltpu.make_async_copy(traces.at[:, :, here], traces_in, sems.at[2]),
        pltpu.make_async_copy(stiffness.at[0, :, here], stiffness_in, sems.at[3]),
        pltpu.make_async_copy(orders.at[0, 0], slots, sems.at[4]),
        pltpu.make_async_copy(rhs.at[0, 0, :, here], base.at[pl.ds(8, 8), :], sems.at[5]),
        pltpu.make_async_copy(lengths, lengths_in, sems.at[6]),
        pltpu.make_async_copy(count, count_in, sems.at[7]),
    ]
    for copy in copies:
        copy.start()
    pay[...] = jnp.zeros(pay.shape, jnp.float32)
    base[sz.modes : 8, :] = jnp.zeros((8 - sz.modes, sz.rows), jnp.float32)
    for copy in copies:
        copy.wait()
    for m in range(sz.modes):
        mask = (m < count_in[0, 0]).astype(jnp.float32)
        for t in range(sz.subs):
            pay[0, m : m + 1, t * SLOT : t * SLOT + sz.modes] = inverse_in[
                m, :, t * sz.modes : (t + 1) * sz.modes
            ]
        loads_row = loads_in[m] * mask
        row = pay[0, m : m + 1, 0:TILE]
        for load in range(sz.loads):
            row = jnp.where(lanes((1, TILE)) == SLOT * load + LOAD_LANE, loads_row[:, load : load + 1], row)
        pay[0, m : m + 1, 0:TILE] = row
        base[m : m + 1, :] = traces_in[m] * mask
    position = lax.broadcasted_iota(jnp.int32, (1, sz.cap), 1)
    base[6:7, :] = stiffness_in[...]
    for j in range(sz.own_faces):
        index = gz * sz.own_faces + j
        base[7:8, own_face(sz, j)] = (position < lengths_in[0, 0, index]).astype(jnp.float32)
        chosen = jnp.broadcast_to(slots[pl.ds(index, 1), :], (8, sz.cap))
        base[16:24, own_face(sz, j)] = chosen.astype(jnp.float32)
    put_slots(sz, faces, [base[0:8, own_face(sz, j)] for j in range(sz.own_faces)])
    chunk = pay[0]
    for k in range(1, pay.shape[0]):
        pay[k] = chunk


def modes_kernel(sz, base, *refs):
    arrived, (modes_ref, right, coupling) = refs[: sz.own_faces], refs[sz.own_faces :]
    right[...] = base[8:16, :]
    row = lax.broadcasted_iota(jnp.int32, (8, 1), 0)
    arrived = get_slots(sz, arrived)
    for j in range(sz.own_faces):
        here = own_face(sz, j)
        other = permuted(sz, arrived[j], base[16:24, here])
        mine = base[0:8, here]
        live = mine[7:8, :]
        total = live * (mine[6:7, :] + other[6:7, :])
        weight = live / (total + 1.0 - live)
        modes_ref[0:8, here] = jnp.where(row == 6, weight, jnp.where(row == 7, live, mine * live))
        slots_row = jnp.where(row == 6, base[16:24, here], 0.0)
        modes_ref[8:16, here] = jnp.where(row < sz.modes, other * live, slots_row)
    weights = weights_of(sz, modes_ref)
    coarse_rows = [
        jnp.where(row < sz.modes, modes_ref[0:8, own_face(sz, j)] * weights[j], 0.0)
        for j in range(sz.own_faces)
    ]
    tile = jnp.zeros((8, TILE), jnp.float32)
    coupling[...] = mode_products(sz, tile, coarse_rows, modes_ref, 2 * sz.group)


def assembled(sz, own, arrived, modes_ref, j):
    here = own_face(sz, j)
    return modes_ref[7:8, here] * (own[j] + permuted(sz, arrived[j], modes_ref[14:15, here]))


def tile_products(sz, tile, vectors, modes_ref):
    lane = lanes()

    def put(tile, rows, source, target):
        moved = pltpu.roll(rows, (target - source) % TILE, 1)
        return jnp.where((lane >= target) & (lane < target + sz.modes), moved, tile)

    own = None
    for j, (vector, weight) in enumerate(zip(vectors, weights_of(sz, modes_ref))):
        both = jnp.concatenate([vector, vector * weight], axis=0)
        product = lax.dot_general(
            both, modes_ref[0:16, own_face(sz, j)], (((1,), (1,)), ((), ())),
            precision=lax.Precision.HIGHEST, preferred_element_type=jnp.float32,
        )
        product = jnp.concatenate([product, jnp.zeros((16, TILE - 16), jnp.float32)], axis=1)
        own = product if own is None else own + product
        for group in range(2):
            rows = product[8 * group : 8 * group + 8]
            tile = put(tile, rows, SLOT, group * sz.group + sz.modes * (1 + j))
    for group in range(2):
        tile = put(tile, own[8 * group : 8 * group + 8], 0, group * sz.group)
    return tile


def first_kernel(sz, operator, shared, right, coupling, modes_ref, modes_rest, *refs):
    outs, refs = refs[: sz.own_faces], refs[sz.own_faces :]
    pay, estimate_ref, inverse_ref, coarse_ref, held, product, vector, sems = refs
    stream = Stream(sz, operator, held, product, sems)
    fill_inverse(sz, shared, inverse_ref)
    turned = []
    for k in range(sz.coarse_pad // TILE):
        block = jnp.transpose(inverse_ref[k * TILE : (k + 1) * TILE, 0:TILE])
        rows = [SLOT * load + LOAD_LANE for load in range(sz.loads)]
        turned.append(jnp.concatenate([block[r : r + 1] for r in rows], axis=0))
    coarse_ref[...] = exact_dot(jnp.concatenate(turned, axis=1), inverse_ref[...])
    mine = own_coefficients(sz, coarse_ref)
    for part, modes in views(sz, modes_ref, modes_rest):
        for j in range(sz.own_faces):
            here = face_slots(sz, part, j)
            estimate = mode_sum(sz, coarse_ref, mine, modes, part, j)
            estimate_ref[:, here] = estimate
            vector[:, here] = estimate.astype(jnp.bfloat16)
    pieces = stream.apply(vector)
    vectors = [right[:, own_face(sz, j)] - piece for j, piece in enumerate(pieces)]
    put_slots(sz, outs, vectors)
    spread_folded(pay, tile_products(sz, coupling[...], vectors, modes_ref))


def second_kernel(sz, pieces, shared, modes_ref, *refs):
    own, refs = get_slots(sz, refs[: sz.own_faces]), refs[sz.own_faces :]
    arrived, refs = get_slots(sz, refs[: sz.own_faces]), refs[sz.own_faces :]
    residual_ref, direction_ref, inverse_ref, coupling_ref, coarse_a, coarse_b = refs
    gz = lax.axis_index("gz")
    fill_inverse(sz, shared, inverse_ref)
    fill_coupling(sz, pieces, coupling_ref)
    solve_pair(sz, pieces, inverse_ref, coupling_ref, coarse_a, coarse_b)
    first, second = own_coefficients(sz, coarse_a), own_coefficients(sz, coarse_b)
    for j in range(sz.own_faces):
        here = own_face(sz, j)
        gap = assembled(sz, own, arrived, modes_ref, j)
        residual = gap - mode_sum(sz, coarse_a, first, modes_ref, gz, j)
        residual_ref[:, here] = residual
        correction = mode_sum(sz, coarse_b, second, modes_ref, gz, j)
        direction_ref[:, here] = modes_ref[6:7, here] * residual - correction


def second_apply_kernel(sz, held, modes_ref, residual, direction, rest, *refs):
    outs, refs = refs[: sz.own_faces], refs[sz.own_faces :]
    pay, product, vector = refs
    put_parts(sz, direction, rest, vector)
    weights = weights_of(sz, modes_ref)
    lane = lanes()
    curvature = jnp.zeros((8, 1), jnp.float32)
    resid_dot = jnp.zeros((8, 1), jnp.float32)
    pieces = apply_held(sz, vector, held, product)
    put_slots(sz, outs, pieces)
    for j, piece in enumerate(pieces):
        here = own_face(sz, j)
        own = residual[:, here]
        resid_dot += jnp.sum(own * (weights[j] * own), axis=1, keepdims=True)
        curvature += jnp.sum(direction[:, here] * piece, axis=1, keepdims=True)
    tile = jnp.where(lane == sz.sums, curvature, jnp.zeros((8, TILE), jnp.float32))
    tile = jnp.where(lane == sz.sums + 1, resid_dot, tile)
    spread_folded(pay, tile_products(sz, tile, pieces, modes_ref))


def third_kernel(sz, pieces, shared, before, modes_ref, residual_ref, direction_ref, *refs):
    own, refs = get_slots(sz, refs[: sz.own_faces]), refs[sz.own_faces :]
    arrived, refs = get_slots(sz, refs[: sz.own_faces]), refs[sz.own_faces :]
    later_ref, scalars_ref, inverse_ref, coupling_ref, coarse_a, coarse_b = refs
    gz = lax.axis_index("gz")
    lane = lanes()
    fill_inverse(sz, shared, inverse_ref)
    fill_coupling(sz, before, coupling_ref)
    totals = pieces[0]
    for k in range(1, sz.devices):
        totals = totals + pieces[k]
    totals = unfolded(totals)
    curvature = 2.0 * totals[:, sz.sums : sz.sums + 1]
    resid_dot = totals[:, sz.sums + 1 : sz.sums + 2]
    step = resid_dot / curvature
    solve_pair(sz, pieces, inverse_ref, coupling_ref, coarse_a, coarse_b)
    first, second = own_coefficients(sz, coarse_a), own_coefficients(sz, coarse_b)
    dot_part = jnp.zeros((8, 1), jnp.float32)
    for j in range(sz.own_faces):
        here = own_face(sz, j)
        image = assembled(sz, own, arrived, modes_ref, j)
        corrected = image - mode_sum(sz, coarse_a, first, modes_ref, gz, j)
        weight = modes_ref[6:7, here]
        scaled = weight * corrected - mode_sum(sz, coarse_b, second, modes_ref, gz, j)
        residual = residual_ref[:, here] - step * corrected
        dot_part += jnp.sum(residual * (weight * residual), axis=1, keepdims=True)
        later_ref[:, here] = direction_ref[:, here] - step * scaled
    scalars_ref[...] = jnp.where(lane == 0, curvature, jnp.where(lane == 1, resid_dot, dot_part))


def third_apply_kernel(sz, held, direction, scalars, later, rest, *refs):
    before, refs = get_slots(sz, refs[: sz.own_faces]), refs[sz.own_faces :]
    pay, product, vector = refs
    put_parts(sz, later, rest, vector)
    pieces = apply_held(sz, vector, held, product)
    lane = lanes()
    later_part = jnp.zeros((8, 1), jnp.float32)
    cross_part = jnp.zeros((8, 1), jnp.float32)
    for j, piece in enumerate(pieces):
        mine = later[:, own_face(sz, j)]
        earlier = direction[:, own_face(sz, j)]
        later_part += jnp.sum(mine * piece, axis=1, keepdims=True)
        cross_part += jnp.sum(mine * before[j] + earlier * piece, axis=1, keepdims=True)
    load = lax.broadcasted_iota(jnp.int32, (8, TILE), 0)
    line = jnp.where(lane == load, later_part, 0.0)
    line = jnp.where(lane == load + 8, cross_part, line)
    line = jnp.where(lane == load + 16, scalars[:, 2:3], line)
    spread(pay, jnp.sum(line, axis=0, keepdims=True))


def last_kernel(sz, pieces, scalars, estimate, direction, direction_rest, later, later_rest, out):
    totals = pieces[0]
    for k in range(1, pieces.shape[0]):
        totals = totals + pieces[k]
    curvature, previous = scalars[:, 0:1], scalars[:, 1:2]
    load = lax.broadcasted_iota(jnp.int32, (8, TILE), 0)
    later_part, cross_part, dot = [
        jnp.sum(jnp.where(lanes() == load + 8 * k, totals, 0.0), axis=1, keepdims=True)
        for k in range(3)
    ]
    ratio = dot / previous
    final = 2.0 * (later_part + ratio * cross_part) + ratio * ratio * curvature
    first, second = previous / curvature, dot / final
    both = zip(views(sz, direction, direction_rest), views(sz, later, later_rest))
    for (part, earlier), (_, mine) in both:
        here = part_slots(sz, part)
        moved = estimate[:, here] + first * earlier[...]
        out[0, 0, :, here] = moved + second * (mine[...] + ratio * earlier[...])


def shards(mesh_shape, operator, rhs_parts, stiffness, traces, coarse_inverse, rigid_loads,
           face_lengths, face_order, mode_count):
    sz = Sizes(mesh_shape, operator, traces, rhs_parts.shape[2])
    vmem = pl.BlockSpec(memory_space=pltpu.VMEM)
    smem = pl.BlockSpec(memory_space=pltpu.SMEM)
    hbm = pl.BlockSpec(memory_space=pltpu.HBM)
    everywhere = ("gx", "gy", "gz")
    small = sz.coarse_pad <= 256

    def call(kernel, out_shape, in_specs, scratch, *operands, limit=None, cost=None):
        return pl.pallas_call(
            functools.partial(kernel, sz),
            out_shape=out_shape,
            in_specs=in_specs,
            out_specs=jax.tree.map(lambda _: vmem, out_shape),
            scratch_shapes=scratch,
            cost_estimate=cost,
            compiler_params=pltpu.CompilerParams(
                vmem_limit_bytes=(limit or (16 if small else 56)) * MIB
            ),
        )(*operands)

    faces = sz.own_faces
    coarse = pltpu.VMEM((8, sz.coarse_pad), jnp.float32)
    square = pltpu.VMEM((sz.coarse_pad, sz.coarse_pad), jnp.float32)
    half, full, face = f32(8, sz.rows), f32(8, sz.order), f32(8, sz.cap)
    blocks = operator.reshape(sz.rows // 8, 8, sz.order)
    one_step = sz.devices <= 64
    spread_tile = f32(sz.devices if one_step else 1, 4, TILE)
    apply_scratch = [
        pltpu.VMEM((8, sz.rows), jnp.float32),
        pltpu.VMEM((8, sz.order), jnp.bfloat16),
    ]
    copies = sz.rows // PIECE
    stream_scratch = [pltpu.VMEM((sz.rows // 8, 8, sz.order), jnp.bfloat16)] + apply_scratch
    stream_scratch += [pltpu.SemaphoreType.DMA((copies,))]

    def hold(after):
        return call(
            hold_kernel, jax.ShapeDtypeStruct((sz.rows // 8, 8, sz.order), jnp.bfloat16),
            [hbm, vmem], [pltpu.SemaphoreType.DMA((copies,))], blocks, after, limit=42,
            cost=pl.CostEstimate(flops=0, bytes_accessed=4 * sz.rows * sz.order, transcendentals=0),
        )

    def swap(own):
        return [lax.ppermute(own[j], everywhere, face_pairs(sz, j)) for j in range(faces)]

    def share(chunk, axes):
        if chunk.shape[0] == 1:
            return lax.all_gather(chunk, axes, axis=0, tiled=True)
        return lax.all_to_all(chunk, axes, split_axis=0, concat_axis=0, tiled=True)

    def rest(part):
        if sz.gz == 2:
            return lax.ppermute(part, "gz", [(0, 1), (1, 0)])
        return lax.all_gather(part, "gz", axis=0, tiled=False)

    *own, pay, base = call(
        start_kernel,
        [face] * faces + [f32(sz.subs if one_step else 1, 8, sz.coarse_pad), f32(24, sz.rows)],
        [hbm] * 8,
        [
            pltpu.VMEM((sz.modes, 1, sz.rows), jnp.float32),
            pltpu.VMEM((sz.modes, 1, sz.loads), jnp.float32),
            pltpu.VMEM((sz.modes, 1, sz.subs * sz.modes), jnp.float32),
            pltpu.VMEM((1, sz.rows), jnp.float32),
            pltpu.VMEM((4, sz.cap), jnp.int32),
            pltpu.SMEM((1, 1, 4), jnp.int32),
            pltpu.SMEM((1, 1), jnp.int32),
            pltpu.SemaphoreType.DMA((8,)),
        ],
        traces.reshape(sz.modes, 1, sz.order), rigid_loads.reshape(sz.modes, 1, sz.loads),
        coarse_inverse.reshape(sz.modes, 1, -1), stiffness, face_order, rhs_parts,
        face_lengths, mode_count, limit=60,
    )
    shared = share(pay, ("gx", "gy"))
    modes, right, coupling = call(
        modes_kernel, [f32(16, sz.rows), half, f32(8, TILE)], [vmem] * (1 + faces), [], base, *swap(own)
    )
    modes_rest = rest(modes)
    *own, pay, estimate = call(
        first_kernel, [face] * faces + [spread_tile, full], [hbm] + [vmem] * 5,
        [square, coarse] + stream_scratch,
        blocks, shared, right, coupling, modes, modes_rest, limit=50 if small else 56,
    )
    before = share(pay, everywhere)
    residual, direction = call(
        second_kernel, [half, half], [vmem] * (3 + 2 * faces), [square, square, coarse, coarse],
        before, shared, modes, *own, *swap(own),
    )
    direction_rest = rest(direction)
    *own, pay = call(
        second_apply_kernel, [face] * faces + [spread_tile], [vmem] * 5,
        apply_scratch, hold(direction), modes, residual, direction, direction_rest,
    )
    after = share(pay, everywhere)
    later, scalars = call(
        third_kernel, [half, f32(8, TILE)], [vmem] * (6 + 2 * faces),
        [square, square, coarse, coarse],
        after, shared, before, modes, residual, direction, *own, *swap(own),
    )
    later_rest = rest(later)
    pay = call(
        third_apply_kernel, f32(sz.devices if one_step else 1, 1, TILE),
        [vmem] * (5 + faces), apply_scratch,
        hold(later), direction, scalars, later, later_rest, *own,
    )
    return call(
        last_kernel, f32(1, 1, 8, sz.order), [vmem] * 7, [],
        share(pay, everywhere), scalars, estimate, direction, direction_rest, later, later_rest,
    )


def solution(mesh):
    in_specs = (
        P("gx", "gy", "gz", None),
        P("gx", "gy", None, None),
        P("gx", "gy", None),
        P("gx", "gy", None, None),
        P("gx", "gy", None, None),
        P("gx", "gy", None, None),
        P("gx", "gy", None),
        P("gx", "gy", None, None),
        P("gx", "gy"),
    )
    out_specs = P("gx", "gy", None, None)
    mesh_shape = tuple(mesh.shape[axis] for axis in ("gx", "gy", "gz"))
    return jax.shard_map(
        functools.partial(shards, mesh_shape),
        mesh=mesh, in_specs=in_specs, out_specs=out_specs, check_vma=False,
    )
```
